32 devices in a mesh: dp: 32 (over z, y, x, core).
Axes of the slice: x: 2, y: 2, z: 4, core: 2. Of those that a mesh axis runs over, the one named last changes fastest.
Arguments:
- tokens: bfloat16 [24576, 768], P('dp'), may hold values from -6 to 6
- cotangent: bfloat16 [24576, 768], P('dp'), may hold values from -6 to 6
- lengths: int32 [24], replicated, may hold values from 1 to 2048, 24576 in all
- gain_norm1: bfloat16 [768], P('dp'), may hold values from 0.25 to 1.75
- gain_norm2: bfloat16 [768], P('dp'), may hold values from 0.25 to 1.75
- proj_in: bfloat16 [768, 2048], P('dp'), may hold values from -0.21875 to 0.21875
- out_proj: bfloat16 [768, 1024], P('dp'), may hold values from -0.5 to 0.5
- gate_blocks: bfloat16 [1024, 512], P('dp'), may hold values from -0.375 to 0.375
- conv_weight: bfloat16 [4, 1024], P(None, 'dp'), may hold values from -3 to 3
- conv_bias: bfloat16 [1024], P('dp'), may hold values from -3 to 3
- gate_bias: bfloat16 [2, 1024], P(None, 'dp'), may hold values from -4 to 4
- decay_param: bfloat16 [1024], P('dp'), may hold values from -11.6 to -3.8
- mlp_in: bfloat16 [2304, 1536], P('dp'), may hold values from -0.21875 to 0.21875
- mlp_down: bfloat16 [2304, 768], P('dp'), may hold values from -0.25 to 0.25
Outputs:
- output: bfloat16 [24576, 768], P('dp')
- grad_tokens: bfloat16 [24576, 768], P('dp')
- grad_gain_norm1: float32 [768], P('dp')
- grad_gain_norm2: float32 [768], P('dp')
- grad_proj_in: float32 [768, 2048], P('dp')
- grad_out_proj: float32 [768, 1024], P('dp')
- grad_gate_blocks: float32 [1024, 512], P('dp')
- grad_conv_weight: float32 [4, 1024], P(None, 'dp')
- grad_conv_bias: float32 [1024], P('dp')
- grad_gate_bias: float32 [2, 1024], P(None, 'dp')
- grad_decay_param: float32 [1024], P('dp')
- grad_mlp_in: float32 [2304, 1536], P('dp')
- grad_mlp_down: float32 [2304, 768], P('dp')
The draws below stay inside these ranges and needn't reach their ends.
Inputs may be any that keep to these rules, and one draw needn't show every extreme that they name: Together the lengths fill all 24576 rows; the longest is exactly 2048.
All inputs are finite; a program needn't handle non-finite values.
Results may differ from the reference program's by a relative error of at most 0.009.
Values may be sent and summed in bfloat16 or wider, within the bound.
A program may use at most 192 MiB of HBM per device.

```python
import math
import jax
import jax.numpy as jnp
import numpy as np
from jax import lax

D = 768
R = 1024
FF = 2304
BLOCK = 256
CONV = 4
TOKENS = 24576
MAXLEN = 2048
NSEQ = 24


def draw_decay_param(key, part):
    key = jax.random.fold_in(key, 11)
    coin_key, slow_key, fast_key = jax.random.split(key, 3)
    coin = jax.random.uniform(coin_key, (R,), dtype=jnp.float32)
    slow_rate = jnp.exp(jax.random.uniform(slow_key, (R,), dtype=jnp.float32, minval=jnp.log(1e-05), maxval=jnp.log(5e-05)))
    fast_rate = jnp.exp(jax.random.uniform(fast_key, (R,), dtype=jnp.float32, minval=jnp.log(5e-05), maxval=jnp.log(0.02)))
    share = 0.5
    rate = jnp.where(coin < share, slow_rate, fast_rate)
    return jnp.log(jnp.expm1(rate)).astype(jnp.bfloat16)


def block_scale(key, extent, cuts, smallest, largest):
    factor_of, own = 1.0, jax.random.fold_in(key, 6)
    for position, shards_of in cuts:
        steps = jnp.exp(jax.random.uniform(jax.random.fold_in(own, position), (shards_of,), jnp.float32, smallest / len(cuts), largest / len(cuts)))
        factor_of = factor_of * jnp.repeat(steps, extent[position] // shards_of).reshape([-1 if axis == position else 1 for axis in range(len(extent))])
    return factor_of


def length_profile(amount, total, limit, lean):
    weights = [(1 << 20) // math.isqrt(rank ** lean) + 1 for rank in range(2, amount + 1)]
    rest, holding = total - limit - (amount - 1), [1] * (amount - 1)
    while rest > 0:
        candidates = [i for i in range(amount - 1) if holding[i] < limit]
        mass, left = sum([weights[i] for i in candidates]), rest
        for i in candidates:
            addition = min(limit - holding[i], max(1, left * weights[i] // mass), rest)
            holding[i] = holding[i] + addition
            rest = rest - addition
    return np.array([limit] + holding)


def ragged_sizes(own_key, count, total, bound, skew):
    if count == 2:
        one = jax.random.randint(own_key, (), max(1, total - bound), min(bound, total - 1) + 1)
        return jnp.stack([one, total - one])
    sizes = jnp.asarray(length_profile(count, total, bound, skew), jnp.int32)
    couples = (count - 1) // 2
    giver, sink = sizes[1:1 + 2 * couples:2], sizes[2:2 + 2 * couples:2]
    margin = jnp.minimum(giver - 1, bound - sink)
    moved = jax.random.randint(jax.random.fold_in(own_key, 1), (couples,), 0, 1 << 20) % (margin + 1)
    sizes = sizes.at[1:1 + 2 * couples:2].set(giver - moved).at[2:2 + 2 * couples:2].set(sink + moved)
    return sizes[jax.random.permutation(jax.random.fold_in(own_key, 2), count)]


def gaussian(key, dims, width, bound, pieces=(), kind=jnp.bfloat16):
    entries = jax.random.normal(key, dims, jnp.float32) * width
    if len(pieces) > 0:
        entries = block_scale(key, dims, pieces, -0.22, 0.18) * entries
    return jnp.clip(entries, min=-bound, max=bound).astype(kind)


def setup_inputs(seed: int = 0) -> dict:
    seeds = jax.random.split(jax.random.key(seed), 15)
    return {
        "tokens": gaussian(seeds[0], (TOKENS, D), 1.0, 6.0, ((0, 32),)),
        "cotangent": gaussian(seeds[1], (TOKENS, D), 1.0, 6.0, ((0, 32),)),
        "lengths": ragged_sizes(seeds[2], NSEQ, TOKENS, MAXLEN, 2).astype(jnp.int32),
        "gain_norm1": jnp.clip(1.0 + 0.15 * jax.random.normal(seeds[3], (D,), jnp.float32), 0.25, 1.75).astype(jnp.bfloat16),
        "gain_norm2": jnp.clip(1.0 + 0.15 * jax.random.normal(seeds[4], (D,), jnp.float32), 0.25, 1.75).astype(jnp.bfloat16),
        "proj_in": gaussian(seeds[5], (D, 2 * R), D ** -0.5, 0.21875, ((0, 32),)),
        "out_proj": gaussian(seeds[6], (D, R), (R // 8) ** -0.5, 0.5, ((0, 32),)),
        "gate_blocks": gaussian(seeds[7], (R, 2 * BLOCK), BLOCK ** -0.5, 0.375, ((0, 32),)),
        "conv_weight": gaussian(seeds[8], (CONV, R), 0.5, 3.0, ((1, 32),)),
        "conv_bias": gaussian(seeds[9], (R,), 0.5, 3.0, ((0, 32),)),
        "gate_bias": gaussian(seeds[10], (2, R), 1.0, 4.0, ((1, 32),)),
        "decay_param": draw_decay_param(jax.random.fold_in(seeds[14], 71), 0),
        "mlp_in": gaussian(seeds[12], (FF, 2 * D), D ** -0.5, 0.21875, ((0, 32),)),
        "mlp_down": gaussian(seeds[13], (FF, D), (FF // 4) ** -0.5, 0.25, ((0, 32),)),
    }


@jax.custom_vjp
def low(v):
    return lax.optimization_barrier(v.astype(jnp.bfloat16)).astype(jnp.float32)

@jax.custom_vjp
def low_back(v):
    return v

def low_keep(v):
    return (low(v), None)

def low_pass(kept, grad):
    return (grad,)

def back_keep(v):
    return (v, None)

def back_low(kept, grad):
    return (low(grad),)
low.defvjp(low_keep, low_pass)
low_back.defvjp(back_keep, back_low)
EPSILON = 1e-06

def rms_scale(values, gain_row):
    inverse = lax.rsqrt(lax.optimization_barrier(jnp.mean(values * values, axis=-1, keepdims=True)) + EPSILON)
    return values * inverse * gain_row

def combine_steps(earlier, later):
    return (earlier[0] * later[0], later[0] * earlier[1] + later[1])

def smooth_gelu(inputs):
    return jax.nn.gelu(inputs, approximate=True)

def gate_math(gate_pre, bias_rows, decay_vec, coded_rows, fresh_row):
    tok_rows, rnn_width = coded_rows.shape
    block_size = gate_pre.shape[2] // 2
    gate_x = jax.nn.sigmoid(gate_pre[:, :, :block_size].reshape(tok_rows, rnn_width) + bias_rows[0])
    gate_a = jax.nn.sigmoid(gate_pre[:, :, block_size:].reshape(tok_rows, rnn_width) + bias_rows[1])
    log_a = -8.0 * gate_a * jax.nn.softplus(decay_vec)
    factor = jnp.where(fresh_row, 0.0, jnp.exp(log_a))
    scale_term = jnp.where(fresh_row, 1.0, jnp.sqrt(-jnp.expm1(2.0 * log_a)))
    return (factor, scale_term * gate_x * coded_rows)

def reference(tokens, cotangent, lengths, gain_norm1, gain_norm2, proj_in, out_proj, gate_blocks, conv_weight, conv_bias, gate_bias, decay_param, mlp_in, mlp_down):
    total_rows, model_width = tokens.shape
    conv_taps, rnn_width = conv_weight.shape
    reach_back = conv_taps - 1
    places = jnp.arange(total_rows, dtype=jnp.int32)
    bounds = jnp.cumsum(lengths).astype(jnp.int32)
    labels = lax.optimization_barrier(jnp.sum((places[:, None] >= bounds[None, :]).astype(jnp.int32), axis=1)).astype(jnp.int32)
    labels_padded = jnp.concatenate([jnp.full((reach_back,), -1, dtype=jnp.int32), labels])
    fresh_row = (labels != labels_padded[reach_back - 1:reach_back - 1 + total_rows])[:, None]
    tap_masks = [(labels_padded[reach_back - offset:reach_back - offset + total_rows] == labels)[:, None].astype(jnp.float32) for offset in range(conv_taps)]
    highest = lax.Precision.HIGHEST

    def forward(residual, gain_one, gain_two, w_proj, w_out, w_gates, w_conv, b_conv, b_gates, w_decay, w_mlp, w_down):
        u_one = low(rms_scale(residual, gain_one))
        projected = low_back(jnp.dot(u_one, w_proj, precision=highest))
        branch_x = low(projected[:, :rnn_width])
        branch_y = projected[:, rnn_width:]
        padded = jnp.concatenate([jnp.zeros((reach_back, rnn_width), jnp.float32), branch_x], axis=0)
        conv_sum = jnp.zeros((total_rows, rnn_width), jnp.float32) + b_conv
        for offset in range(conv_taps):
            conv_sum = conv_sum + w_conv[offset] * padded[reach_back - offset:reach_back - offset + total_rows] * tap_masks[offset]
        coded_rows = low(conv_sum)
        block_size = w_gates.shape[1] // 2
        head_count = rnn_width // block_size
        blocks_w = w_gates.reshape(head_count, block_size, 2 * block_size)
        gate_pre = low_back(jnp.einsum('thi,hij->thj', coded_rows.reshape(total_rows, head_count, block_size), blocks_w, precision=highest))
        factor, drive_term = gate_math(gate_pre, b_gates, w_decay, coded_rows, fresh_row)
        prod_unused, state_rows = lax.associative_scan(combine_steps, (factor, drive_term), axis=0)
        mixed_rows = low(state_rows * smooth_gelu(branch_y))
        middle = residual + low_back(jnp.einsum('tr,dr->td', mixed_rows, w_out, precision=highest))
        u_two = low(rms_scale(middle, gain_two))
        gate_val = low_back(jnp.einsum('td,fd->tf', u_two, w_mlp[:, :model_width], precision=highest))
        up_val = low_back(jnp.einsum('td,fd->tf', u_two, w_mlp[:, model_width:], precision=highest))
        hidden = low(smooth_gelu(gate_val) * up_val)
        return middle + jnp.dot(hidden, w_down, precision=highest)
    primals = (tokens.astype(jnp.float32), gain_norm1.astype(jnp.float32), gain_norm2.astype(jnp.float32), proj_in.astype(jnp.float32), out_proj.astype(jnp.float32), gate_blocks.astype(jnp.float32), conv_weight.astype(jnp.float32), conv_bias.astype(jnp.float32), gate_bias.astype(jnp.float32), decay_param.astype(jnp.float32), mlp_in.astype(jnp.float32), mlp_down.astype(jnp.float32))
    output, pullback = jax.vjp(forward, *primals)
    grads = pullback(cotangent.astype(jnp.float32))
    return (output.astype(jnp.bfloat16), grads[0].astype(jnp.bfloat16), grads[1], grads[2], grads[3], grads[4], grads[5], grads[6], grads[7], grads[8], grads[9], grads[10], grads[11])
```

```python
import functools

import jax
import jax.numpy as jnp
from jax import lax
from jax.experimental import pallas as pl
from jax.experimental.pallas import tpu as pltpu
from jax.sharding import PartitionSpec as P

EPSILON = 1e-06
MESH = pl.DeviceIdType.MESH
F32, BF16 = jnp.float32, jnp.bfloat16
VM = pl.BlockSpec(memory_space=pltpu.VMEM)
ANY = pl.BlockSpec(memory_space=pl.ANY)
SM = pl.BlockSpec(memory_space=pltpu.SMEM)
MIB = 2**20
SEG = 8


def nn(a, b):
    return jnp.dot(a, b, preferred_element_type=F32)


def nt(a, b):
    return lax.dot_general(a, b, (((1,), (1,)), ((), ())), preferred_element_type=F32)


def tn(a, b):
    return lax.dot_general(a, b, (((0,), (0,)), ((), ())), preferred_element_type=F32)


class Place:
    def __init__(self):
        me = lax.axis_index("dp")
        self.me = me
        self.core = core = lax.rem(me, 2)
        x = lax.rem(lax.div(me, 2), 2)
        y = lax.rem(lax.div(me, 4), 2)
        self.z = z = lax.div(me, 8)
        self.yx = yx = 2 * y + x
        px, py = me + 2 - 4 * x, me + 4 - 8 * y
        gx, gy = yx + 1 - 2 * x, yx + 2 - 4 * y
        self.pa, self.pb = px + core * (py - px), py + core * (px - py)
        self.ga, self.gb = gx + core * (gy - gx), gy + core * (gx - gy)
        self.gd = 3 - yx
        self.pc = me + 1 - 2 * core
        self.other = 1 - core
        self.zs = [lax.rem(z + d, 4) for d in (1, 2, 3)]
        self.pz = [zz * 8 + lax.rem(me, 8) for zz in self.zs]


def remote(src, dst, ssem, rsem, device):
    return pltpu.make_async_remote_copy(
        src_ref=src, dst_ref=dst, send_sem=ssem, recv_sem=rsem, device_id=(device,), device_id_type=MESH
    )


def entry_barrier(pl_, count, reach):
    me = pl_.me
    bar = pltpu.get_barrier_semaphore()
    for p in [pl_.pc, pl_.pa, pl_.pb] + pl_.pz:
        pl.semaphore_signal(bar, inc=1, device_id=(p,), device_id_type=MESH)
    for d in range(1, reach + 1):

        @pl.when(me >= d)
        def _():
            pl.semaphore_signal(bar, inc=1, device_id=(me - d,), device_id_type=MESH)

        @pl.when(me + d < count)
        def _():
            pl.semaphore_signal(bar, inc=1, device_id=(me + d,), device_id_type=MESH)

    pl.semaphore_wait(bar, 6 + jnp.minimum(me, reach) + jnp.minimum(count - 1 - me, reach))


class Gather:
    def __init__(self, p, buf, ssem, rsem):
        self.p, self.buf, self.ssem, self.rsem = p, buf, ssem, rsem

    def copy(self, slot):
        p = self.p
        if slot < 3:
            src, dev = self.buf.at[p.core, p.yx, p.z], p.pz[slot]
        else:
            group = (p.yx, p.yx, p.ga, p.yx, p.ga, p.gb, p.gd)[slot - 3]
            src, dev = self.buf.at[p.core, group], (p.pa, p.pb, p.pb, p.pc, p.pc, p.pc, p.pc)[slot - 3]
        return remote(src, src, self.ssem.at[slot], self.rsem.at[slot], dev)

    def start(self, *slots):
        for s in slots:
            self.copy(s).start()

    def recv(self, *slots):
        for s in slots:
            self.copy(s).wait_recv()

    def stage(self, n):
        if n == 0:
            self.start(0, 1, 2)
        elif n == 1:
            self.recv(0, 1, 2)
            self.start(3, 4, 6)
        elif n == 2:
            self.recv(3)
            self.start(5, 7)
        elif n == 3:
            self.recv(4)
            self.start(8)
            self.recv(5)
            self.start(9)
        else:
            self.recv(6, 7, 8, 9)
            for s in range(10):
                self.copy(s).wait_send()


def sequence_offset(lengths, first, rows):
    t = first + lax.broadcasted_iota(jnp.int32, (rows, 128), 0)

    def one(i, c):
        bound, start = c
        bound = bound + lengths[i]
        return bound, jnp.where(t >= bound, bound, start)

    _, start = lax.fori_loop(0, lengths.shape[0], one, (jnp.int32(0), jnp.zeros((rows, 128), jnp.int32)))
    return t - start


def one_minus_exp(v):
    s = 1.0 + v * (1.0 / 8.0)
    for k in (7.0, 6.0, 5.0, 4.0, 3.0, 2.0):
        s = 1.0 + v * (1.0 / k) * s
    return jnp.where(v > -0.5, -v * s, 1.0 - jnp.exp(v))


def softplus(v):
    return jnp.maximum(v, 0.0) + jnp.log1p(jnp.exp(-jnp.abs(v)))


GELU_K = 0.7978845608028654


def gelu_parts(v):
    v2 = v * v
    th = jnp.tanh(GELU_K * v * (1.0 + 0.044715 * v2))
    half = 0.5 * (1.0 + th)
    slope = half + 0.5 * v * (1.0 - th * th) * (GELU_K * (1.0 + 3.0 * 0.044715 * v2))
    return v * half, slope


def gelu(v):
    return v * (0.5 * (1.0 + jnp.tanh(GELU_K * v * (1.0 + 0.044715 * (v * v)))))


def flat(v):
    return v.reshape(v.shape[0] * v.shape[1] * v.shape[2], v.shape[3])


def chips(v):
    return jnp.concatenate([v[yx, z] for z in range(4) for yx in range(4)], axis=0)


def put_chips(part, half, v):
    rows = v.shape[0] // 16
    for z in range(4):
        for yx in range(4):
            part[half, yx, z] = v[(4 * z + yx) * rows : (4 * z + yx + 1) * rows]


def put(page, v, row, group):
    for i in range(v.shape[1] // 128):
        page[group + i, row : row + v.shape[0], :] = v[:, i * 128 : (i + 1) * 128]


def rows_loop(total, block, body):
    def one(i, c):
        body(pl.multiple_of(i * block, block))
        return c

    lax.fori_loop(0, total // block, one, 0)


def blocks_loop(groups, total, block, body):
    n = total // block

    def one(i, c):
        body(lax.div(i, n), pl.multiple_of(lax.rem(i, n) * block, block))
        return c

    lax.fori_loop(0, groups * n, one, 0)


def pairs_loop(body):
    def one(i, c):
        body(2 * i, 0, False)
        body(2 * i + 1, 1, i == 3)
        return c

    lax.fori_loop(0, 4, one, 0)


def scan_segments(rows, factor, value, product, factor_row, value_row, product_row, reverse):
    step = rows // SEG

    def one(i, c):
        j = step - 1 - i if reverse else i
        out = []
        for g in range(8):
            h, q = c[g]
            a = factor[g, pl.ds(factor_row + j, SEG, stride=step), :]
            b = value[g, pl.ds(value_row + j, SEG, stride=step), :]
            if reverse:
                h = b + h
                value[g, pl.ds(value_row + j, SEG, stride=step), :] = h
                product[g, pl.ds(product_row + j, SEG, stride=step), :] = q
                h, q = a * h, a * q
            else:
                h, q = a * h + b, a * q
                value[g, pl.ds(value_row + j, SEG, stride=step), :] = h
                product[g, pl.ds(product_row + j, SEG, stride=step), :] = q
            out.append((h, q))
        return tuple(out)

    first = tuple((jnp.zeros((SEG, 128), F32), jnp.ones((SEG, 128), F32)) for _ in range(8))
    return lax.fori_loop(0, step, one, first)


def chain(ends, enter, reverse):
    order = range(SEG - 1, -1, -1) if reverse else range(SEG)
    inside, leave = [], []
    for g in range(8):
        h, q = ends[g]
        v = enter[g]
        rows = [None] * SEG
        for s in order:
            rows[s] = v
            v = q[s : s + 1, :] * v + h[s : s + 1, :]
        inside.append(jnp.concatenate(rows, axis=0))
        leave.append(v)
    return inside, leave


def products(ends):
    out = []
    for g in range(8):
        q = ends[g][1]
        v = q[0:1, :]
        for s in range(1, SEG):
            v = v * q[s : s + 1, :]
        out.append(v)
    return out


def carry_send(p, count, reach, sign, mine, inbox, ssem, rsem):
    for d in range(1, reach + 1):

        @pl.when((p.me + d < count) if sign > 0 else (p.me >= d))
        def _(d=d):
            remote(mine, inbox.at[d - 1], ssem.at[d - 1], rsem.at[d - 1], p.me + sign * d).start()


def carry_wait(p, count, reach, sign, mine, inbox, ssem, rsem):
    for d in range(1, reach + 1):
        there = remote(mine, inbox.at[d - 1], ssem.at[d - 1], rsem.at[d - 1], p.me + sign * d)

        @pl.when((p.me + d < count) if sign > 0 else (p.me >= d))
        def _(there=there):
            there.wait_send()

        @pl.when((p.me >= d) if sign > 0 else (p.me + d < count))
        def _(there=there):
            there.wait_recv()


def carry_fold(p, count, reach, sign, inbox):
    v = [jnp.zeros((1, 128), F32) for _ in range(8)]
    for d in range(reach, 0, -1):
        for g in range(8):
            v[g] = inbox[d - 1, 0, g : g + 1, :] * v[g] + inbox[d - 1, 1, g : g + 1, :]
    return v


def lanes(page, group, row, rows):
    return jnp.concatenate([page[group, pl.ds(row, rows), :], page[group + 1, pl.ds(row, rows), :]], axis=1)


def wide(page, groups, row, rows):
    return jnp.concatenate([page[g, pl.ds(row, rows), :] for g in range(groups)], axis=1)


def fold8(v):
    return jnp.sum(v.reshape(v.shape[0] // 8, 8, v.shape[1]), axis=0)


def forward_kernel(count, reach, *refs):
    (tokens, cot, lengths, cw, cb, gb, dec, g1, g2, w_proj, w_out, w_gate, w_in, w_down,
     out, o_par, o_gain, o_gg2, o_wproj, o_wgate, o_wout, o_gm, o_by, o_fac, o_gx, o_ga, o_sc, o_st, o_bx, o_coded,
     o_mixed, o_u1, o_dmid, o_db,
     wsmall, wproj, wgate, wout, wm, bx, by, fac, dr, pq, gx, ga, sc, ubuf, coded, mixed, middle, u2, hid, dgate, dup,
     since, xh, ssmall, rsmall, sproj, rproj, sout, rout, sgate, rgate, smlp, rmlp, hin, mine, inbox,
     gs, gr, ps, pr, hs, hr, cs, cr, osem) = refs
    p = Place()
    me = p.me
    rows, width = tokens.shape
    core0 = p.core == 0

    xh[...] = jnp.zeros_like(xh)
    inbox[...] = jnp.zeros_like(inbox)
    entry_barrier(p, count, reach)

    halo = remote(tokens.at[rows - 16 : rows], xh, hs.at[0], hr.at[0], me + 1)

    @pl.when(me + 1 < count)
    def _():
        halo.start()

    lane = lax.broadcasted_iota(jnp.int32, (32, 128), 1)
    row = lax.broadcasted_iota(jnp.int32, (32, 128), 0)
    spot = jnp.where(lane == lax.rem(me, 4) * 32 + row, 1.0, 0.0).astype(BF16)
    gcol = lax.broadcasted_iota(jnp.int32, (24, width), 1)
    grow = lax.broadcasted_iota(jnp.int32, (24, width), 0)
    gspot = jnp.where(gcol == me * 24 + grow, 1.0, 0.0).astype(BF16)
    ssmall[...] = jnp.zeros_like(ssmall)
    ssmall[0:4, :] = nn(cw[...], spot)
    ssmall[4:5, :] = nn(cb[...], spot)
    ssmall[5:7, :] = nn(gb[...], spot)
    ssmall[7:8, :] = nn(dec[...], spot)
    r1, r2 = nn(g1[...], gspot), nn(g2[...], gspot)
    for j in range(width // 128):
        ssmall[8 + j : 9 + j, :] = r1[:, j * 128 : (j + 1) * 128]
        ssmall[16 + j : 17 + j, :] = r2[:, j * 128 : (j + 1) * 128]
    trades = [
        remote(ssmall, rsmall, ps.at[0], pr.at[0], p.pc),
        remote(sproj.at[p.other], rproj, ps.at[1], pr.at[1], p.pc),
        remote(sgate.at[p.other], rgate, ps.at[2], pr.at[2], p.pc),
        remote(sout.at[p.other], rout, ps.at[3], pr.at[3], p.pc),
        remote(smlp.at[p.other], rmlp, ps.at[4], pr.at[4], p.pc),
    ]
    trades[0].start()
    for h in range(2):
        sproj[h] = w_proj[:, h * 1024 : (h + 1) * 1024].astype(F32)
    trades[1].start()
    for h in range(2):
        sgate[h] = w_gate[:, h * 256 : (h + 1) * 256].astype(F32)
        sout[h] = w_out[:, h * 512 : (h + 1) * 512].astype(F32)
    trades[2].start()
    trades[3].start()
    smlp[0] = w_in[:, :1152].astype(F32)
    smlp[1] = jnp.concatenate([w_in[:, 1152:], w_down[...]], axis=1).astype(F32)
    trades[4].start()

    chunks = [Gather(p, wsmall, gs.at[0], gr.at[0]), Gather(p, wproj, gs.at[1], gr.at[1]),
              Gather(p, wgate, gs.at[2], gr.at[2]), Gather(p, wout, gs.at[3], gr.at[3])] + [
        Gather(p, wm.at[k], gs.at[4 + k], gr.at[4 + k]) for k in range(3)
    ]
    batches = [chunks[0:2], chunks[2:4], chunks[4:5], chunks[5:6], chunks[6:7]]

    def slab(mine_, theirs):
        first = jnp.where(core0, mine_, theirs)
        second = jnp.where(core0, theirs, mine_)
        return jnp.concatenate([first, second], axis=0).astype(BF16)

    trades[0].wait_recv()
    both = ssmall[...] + rsmall[...]
    wsmall[p.core, p.yx, p.z] = jnp.where(core0, both[0:16], both[16:32]).astype(BF16)
    chunks[0].stage(0)
    trades[1].wait_recv()
    wproj[p.core, p.yx, p.z] = slab(sproj[p.core], rproj[...])
    chunks[1].stage(0)
    since[...] = sequence_offset(lengths, me * rows, rows)
    trades[2].wait_recv()
    wgate[p.core, p.yx, p.z] = slab(sgate[p.core], rgate[...])
    trades[3].wait_recv()
    wout[p.core, p.yx, p.z] = slab(sout[p.core], rout[...])
    trades[4].wait_recv()
    for k in range(3):
        wm[k, p.core, p.yx, p.z] = slab(smlp[p.core, 24 * k : 24 * k + 24, :], rmlp[24 * k : 24 * k + 24, :])
    for t in trades:
        t.wait_send()

    def slot(n):
        for i, batch in enumerate(batches):
            if 0 <= n - i <= 4 and not (i == 0 and n == 0):
                for c in batch:
                    c.stage(n - i)

    outs = []

    def save(src, dst):
        c = pltpu.make_async_copy(src, dst, osem.at[len(outs)])
        c.start()
        outs.append(c)
        return c

    slot(1)
    slot(2)
    slot(3)
    slot(4)

    for g in range(8):
        z_, yx_ = g // 2, 2 * (g % 2)
        o_par[g] = wsmall[0, yx_, z_].astype(F32)[0:8] + wsmall[0, yx_ + 1, z_].astype(F32)[0:8]
    gsum = [jnp.zeros((8, 128), F32), jnp.zeros((8, 128), F32)]
    for z_ in range(4):
        for yx_ in range(4):
            gsum[0] = gsum[0] + wsmall[0, yx_, z_].astype(F32)[8:16]
            gsum[1] = gsum[1] + wsmall[1, yx_, z_].astype(F32)[0:8]
    o_gain[...] = jnp.zeros_like(o_gain)
    for n in range(2):
        for j in range(width // 128):
            o_gain[n : n + 1, j * 128 : (j + 1) * 128] = gsum[n][j : j + 1]

    @pl.when(me + 1 < count)
    def _():
        halo.wait_send()

    @pl.when(me > 0)
    def _():
        halo.wait_recv()

    def norm_rows(x, n):
        inv = lax.rsqrt(jnp.mean(x * x, axis=1, keepdims=True) + EPSILON)
        return (x * inv * o_gain[n : n + 1, :]).astype(BF16)

    ubuf[0:16, :] = norm_rows(xh[...].astype(F32), 0)

    def norm_one(r0):
        ubuf[pl.ds(r0 + 16, 32), :] = norm_rows(tokens[pl.ds(r0, 32), :].astype(F32), 0)

    rows_loop(rows, 32, norm_one)
    save(ubuf.at[16 : rows + 16], o_u1)

    def project(h, c):
        cols = pl.ds(pl.multiple_of(h * 256, 256), 256)
        v = nn(ubuf[...], chips(wproj[0, :, :, :, cols])).astype(BF16).astype(F32)
        bx[2 * h], bx[2 * h + 1] = v[:, :128], v[:, 128:]
        v = nn(ubuf[16:, :], chips(wproj[1, :, :, :, cols]))
        by[2 * h], by[2 * h + 1] = v[:, :128], v[:, 128:]
        return c

    lax.fori_loop(0, 4, project, 0)
    save(bx, o_bx)
    save(by, o_by)
    save(wproj, o_wproj)
    slot(5)

    def conv(g, r0):
        par = o_par[g]
        v = bx[g, pl.ds(r0 + 8, 72), :]
        off = since[pl.ds(r0, 64), :]
        total = par[4:5] + par[0:1] * v[8:72]
        for k in range(1, 4):
            total = total + par[k : k + 1] * jnp.where(off >= k, v[8 - k : 72 - k], 0.0)
        coded[g, pl.ds(r0, 64), :] = total.astype(BF16)

    blocks_loop(8, rows, 64, conv)
    save(coded, o_coded)
    save(wgate, o_wgate)

    def gate_dots(h, c):
        left = lanes(coded, 2 * h, 0, rows)
        v = nn(left, wgate[0, :, h].reshape(256, 256))
        gx[2 * h], gx[2 * h + 1] = v[:, :128], v[:, 128:]
        v = nn(left, wgate[1, :, h].reshape(256, 256))
        ga[2 * h], ga[2 * h + 1] = v[:, :128], v[:, 128:]
        return c

    lax.fori_loop(0, 4, gate_dots, 0)

    def gates(g, r0):
        par = o_par[g]
        at = pl.ds(r0, 64)
        fresh = since[at, :] == 0
        gate_x = jax.nn.sigmoid(gx[g, at, :] + par[5:6])
        gate_a = jax.nn.sigmoid(ga[g, at, :] + par[6:7])
        log_a = -8.0 * gate_a * softplus(par[7:8])
        factor = jnp.where(fresh, 0.0, jnp.exp(log_a))
        scale = jnp.where(fresh, 1.0, jnp.sqrt(one_minus_exp(2.0 * log_a)))
        gx[g, at, :] = gate_x
        ga[g, at, :] = gate_a
        fac[g, at, :] = factor
        sc[g, at, :] = scale
        dr[g, pl.ds(r0 + 8, 64), :] = scale * gate_x * coded[g, at, :].astype(F32)

    blocks_loop(8, rows, 64, gates)
    saved = [save(gx, o_gx), save(ga, o_ga), save(fac, o_fac), save(sc, o_sc)]

    ends = scan_segments(rows, fac, dr, pq, 0, 8, 0, False)
    _, leave = chain(ends, [jnp.zeros((1, 128), F32)] * 8, False)
    whole = products(ends)
    for g in range(8):
        mine[0, g : g + 1, :] = whole[g]
        mine[1, g : g + 1, :] = leave[g]
    carry_send(p, count, reach, 1, mine, inbox, cs, cr)
    slot(6)
    carry_wait(p, count, reach, 1, mine, inbox, cs, cr)
    enter = carry_fold(p, count, reach, 1, inbox)
    inside, _ = chain(ends, enter, False)
    for g in range(8):
        hin[g] = inside[g]
        dr[g, 0:8, :] = jnp.broadcast_to(enter[g], (8, 128))
    step = rows // SEG

    def states(g, c):
        for s in range(SEG):
            lo = s * step
            st = dr[g, lo + 8 : lo + 8 + step, :] + pq[g, lo : lo + step, :] * hin[g, s : s + 1, :]
            dr[g, lo + 8 : lo + 8 + step, :] = st
            mixed[g, lo : lo + step, :] = (st * gelu(by[g, lo : lo + step, :])).astype(BF16)
        return c

    lax.fori_loop(0, 8, states, 0)
    saved.append(save(dr, o_st))
    save(mixed, o_mixed)
    save(wout, o_wout)
    middle[...] = nt(wide(mixed, 4, 0, rows), chips(wout[0])) + nt(
        jnp.concatenate([mixed[g] for g in range(4, 8)], axis=1), chips(wout[1])
    )

    def norm_two(r0):
        at = pl.ds(r0, 32)
        m = middle[at, :] + tokens[at, :].astype(F32)
        middle[at, :] = m
        u2[at, :] = norm_rows(m, 1)

    rows_loop(rows, 32, norm_two)
    for c in saved:
        c.wait()
    fg, fu, fd, acc_out, acc_du = gx, ga, pq, sc, fac

    for k in range(3):
        if k > 0:
            slot(6 + k)
        w0 = flat(wm[k, 0])
        w1 = flat(wm[k, 1])
        wg, wu, wd = w0[:, :768], jnp.concatenate([w0[:, 768:], w1[:, :384]], axis=1), w1[:, 384:]
        put(fg, nt(u2[...], wg), 0, 0)
        put(fu, nt(u2[...], wu), 0, 0)
        put(fd, nt(cot[...], wd), 0, 0)

        def glu(r0):
            at = pl.ds(r0, 32)
            for g in range(6):
                cols = slice(g * 128, (g + 1) * 128)
                act, slope = gelu_parts(fg[g, at, :])
                up, dh = fu[g, at, :], fd[g, at, :]
                hid[at, cols] = (act * up).astype(BF16)
                dgate[at, cols] = (dh * up * slope).astype(BF16)
                dup[at, cols] = (dh * act).astype(BF16)

        rows_loop(rows, 32, glu)
        v = nn(hid[...], wd)
        v2 = nn(dgate[...], wg) + nn(dup[...], wu)
        for g in range(6):
            cols = slice(g * 128, (g + 1) * 128)
            if k == 0:
                acc_out[g, 0:rows, :] = v[:, cols]
                acc_du[g, 0:rows, :] = v2[:, cols]
            else:
                acc_out[g, 0:rows, :] += v[:, cols]
                acc_du[g, 0:rows, :] += v2[:, cols]
        gg = tn(dgate[...], u2[...]).astype(BF16)
        gu = tn(dup[...], u2[...]).astype(BF16)
        gd = tn(hid[...], cot[...]).astype(BF16)
        wm[k, 0, :, :, :, 0:768] = gg.reshape(4, 4, 48, 768)
        wm[k, 0, :, :, :, 768:1152] = gu[:, :384].reshape(4, 4, 48, 384)
        wm[k, 1, :, :, :, 0:384] = gu[:, 384:].reshape(4, 4, 48, 384)
        wm[k, 1, :, :, :, 384:1152] = gd.reshape(4, 4, 48, 768)
        save(wm.at[k], o_gm.at[k])

    o_gg2[...] = jnp.zeros_like(o_gg2)

    def finish(r0):
        at = pl.ds(r0, 32)
        m, c = middle[at, :], cot[at, :].astype(F32)
        out[at, :] = (m + wide(acc_out, 6, r0, 32)).astype(BF16)
        du = wide(acc_du, 6, r0, 32)
        inv = lax.rsqrt(jnp.mean(m * m, axis=1, keepdims=True) + EPSILON)
        o_gg2[...] += fold8(du * m * inv)
        gd_ = du * o_gain[1:2, :]
        back = jnp.mean(gd_ * m, axis=1, keepdims=True)
        dm = c + inv * gd_ - m * (inv * inv * inv * back)
        hid[at, :] = dm.astype(BF16)
        for g in range(6):
            acc_out[g, at, :] = dm[:, g * 128 : (g + 1) * 128]

    rows_loop(rows, 32, finish)
    save(acc_out.at[0:6], o_dmid)
    save(hid, o_db)
    for c in outs:
        if not any(c is s for s in saved):
            c.wait()


def forward_call(count, reach, args):
    tokens = args[0]
    rows, width = tokens.shape
    S = jax.ShapeDtypeStruct
    page = (8, rows, 128)
    outs = [
        (S((rows, width), BF16), VM),
        (S((8, 8, 128), F32), VM),
        (S((8, width), F32), VM),
        (S((8, width), F32), VM),
        (S((2, 4, 4, 48, 1024), BF16), ANY),
        (S((2, 4, 4, 64, 256), BF16), ANY),
        (S((2, 4, 4, 48, 512), BF16), ANY),
        (S((3, 2, 4, 4, 48, 1152), BF16), ANY),
        (S(page, F32), ANY),
        (S(page, F32), ANY),
        (S(page, F32), ANY),
        (S(page, F32), ANY),
        (S(page, F32), ANY),
        (S((8, rows + 8, 128), F32), ANY),
        (S((8, rows + 16, 128), F32), ANY),
        (S(page, BF16), ANY),
        (S(page, BF16), ANY),
        (S((rows, width), BF16), ANY),
        (S((6, rows, 128), F32), ANY),
        (S((rows, width), BF16), ANY),
    ]
    V = pltpu.VMEM
    dma = pltpu.SemaphoreType.DMA
    scratch = [
        V((2, 4, 4, 16, 128), BF16),
        V((2, 4, 4, 48, 1024), BF16),
        V((2, 4, 4, 64, 256), BF16),
        V((2, 4, 4, 48, 512), BF16),
        V((3, 2, 4, 4, 48, 1152), BF16),
        V((8, rows + 16, 128), F32),
        V(page, F32),
        V(page, F32),
        V((8, rows + 8, 128), F32),
        V(page, F32),
        V(page, F32),
        V(page, F32),
        V(page, F32),
        V((rows + 16, width), BF16),
        V(page, BF16),
        V(page, BF16),
        V((rows, width), F32),
        V((rows, width), BF16),
        V((rows, 768), BF16),
        V((rows, 768), BF16),
        V((rows, 768), BF16),
        V((rows, 128), jnp.int32),
        V((16, width), BF16),
        V((32, 128), F32),
        V((32, 128), F32),
        V((2, 24, 1024), F32),
        V((24, 1024), F32),
        V((2, 24, 512), F32),
        V((24, 512), F32),
        V((2, 32, 256), F32),
        V((32, 256), F32),
        V((2, 72, 1152), F32),
        V((72, 1152), F32),
        V((8, 8, 128), F32),
        V((2, 8, 128), F32),
        V((reach, 2, 8, 128), F32),
        dma((7, 10)),
        dma((7, 10)),
        dma((5,)),
        dma((5,)),
        dma((1,)),
        dma((1,)),
        dma((reach,)),
        dma((reach,)),
        dma((18,)),
    ]
    return pl.pallas_call(
        functools.partial(forward_kernel, count, reach),
        out_shape=[o[0] for o in outs],
        in_specs=[VM, VM, SM] + [VM] * 11,
        out_specs=[o[1] for o in outs],
        scratch_shapes=scratch,
        name="forward",
        cost_estimate=pl.CostEstimate(flops=25 * 10**9, bytes_accessed=60 * 10**6, transcendentals=10**7),
        compiler_params=pltpu.CompilerParams(
            collective_id=0, has_side_effects=True, vmem_limit_bytes=62 * MIB
        ),
    )(*args)


class Reduce:
    def __init__(self, p, part, own, own_lead, bufs, lead, ssem, rsem, load=None):
        self.p, self.part, self.load = p, part, load
        self.whole, self.own_lead, self.bufs, self.lead = own, own_lead, bufs, lead
        self.own = own.at[own_lead]
        self.r0, self.ra, self.rb, self.rz, self.tot, self.rc = [b.at[lead] if lead else b for b in bufs]
        self.ssem, self.rsem = ssem, rsem

    def copy(self, slot):
        p, own = self.p, self.own
        src, dst, dev = (
            (lambda: (self.part.at[p.other], self.r0, p.pc)),
            (lambda: (own.at[p.gd], self.ra.at[1], p.pa)),
            (lambda: (own.at[p.ga], self.ra.at[0], p.pa)),
            (lambda: (own.at[p.gb], self.rb, p.pb)),
            (lambda: (own.at[p.yx, p.zs[0]], self.rz.at[0], p.pz[0])),
            (lambda: (own.at[p.yx, p.zs[1]], self.rz.at[1], p.pz[1])),
            (lambda: (own.at[p.yx, p.zs[2]], self.rz.at[2], p.pz[2])),
            (lambda: (self.tot.at[p.other], self.rc, p.pc)),
        )[slot]()
        return remote(src, dst, self.ssem.at[slot], self.rsem.at[slot], dev)

    def add(self, group, which, *index):
        buf = self.bufs[which]
        for z in range(4):
            at = self.own_lead + (group, z)
            other = buf[self.lead + index + (z,)]
            self.whole[at] = (self.whole[at].astype(F32) + other.astype(F32)).astype(BF16)

    def stage(self, n):
        p = self.p
        if n == 0:
            self.copy(0).start()
            if self.load is not None:
                self.load.start()
        elif n == 1:
            if self.load is not None:
                self.load.wait()
            self.copy(0).wait_recv()
            for group, slot in ((p.gd, 1), (p.ga, 2)):
                self.add(group, 0, group)
                self.copy(slot).start()
            for group in (p.gb, p.yx):
                self.add(group, 0, group)
        elif n == 2:
            self.copy(1).wait_recv()
            self.add(p.gb, 1, 1)
            self.copy(3).start()
            self.copy(2).wait_recv()
            self.add(p.yx, 1, 0)
        elif n == 3:
            self.copy(3).wait_recv()
            self.add(p.yx, 2)
            for s in (4, 5, 6):
                self.copy(s).start()
        elif n == 4:
            total = self.whole[self.own_lead + (p.yx, p.z)].astype(F32)
            for d in range(3):
                self.copy(4 + d).wait_recv()
                total = total + self.bufs[3][self.lead + (d,)].astype(F32)
            half = total.shape[0] // 2
            self.bufs[4][self.lead + (0,)] = total[:half]
            self.bufs[4][self.lead + (1,)] = total[half:]
            self.copy(7).start()
        else:
            self.copy(7).wait_recv()
            mine, theirs = self.bufs[4][self.lead + (p.core,)], self.bufs[5][self.lead + (...,)]
            left = jnp.where(p.core == 0, mine, theirs)
            right = jnp.where(p.core == 0, theirs, mine)
            for s in range(8):
                self.copy(s).wait_send()
            return left, right


class Totals:
    def __init__(self, p, v, bufs, ssem, rsem):
        self.p, self.v, self.bufs, self.ssem, self.rsem = p, v, bufs, ssem, rsem

    def copy(self, slot):
        p = self.p
        dev = ([p.pc, p.pa, p.pb] + p.pz)[slot]
        return remote(self.v.at[min(slot, 3)], self.bufs.at[slot], self.ssem.at[slot], self.rsem.at[slot], dev)

    def stage(self, n):
        if n < 3:
            self.copy(n).start()
        if n == 3:
            for s in (3, 4, 5):
                self.copy(s).start()

    def step(self, n):
        if n < 3:
            self.copy(n).wait_recv()
            self.v[n + 1] = self.v[n] + self.bufs[n]
            return None
        total = self.v[3]
        for s in (3, 4, 5):
            self.copy(s).wait_recv()
            total = total + self.bufs[s]
        for s in range(6):
            self.copy(s).wait_send()
        return total


def backward_kernel(count, reach, *refs):
    (tokens, lengths, par, gain, gg2, i_wproj, i_wgate, i_wout, i_gm, i_by, i_fac, i_gx, i_ga, i_sc, i_st, i_bx, i_coded,
     i_mixed, i_u1, i_dmid, i_db,
     grad_tokens, o_proj, o_out, o_gate, o_in, o_down, o_cw, o_cb, o_gb, o_dec, o_g1, o_g2,
     wproj, wgate, wout, adj, fac, st, pp, gslot, coded, mixed, u1, db, dby, dgx, since,
     own_m, gout, gpy, gpx, ggate,
     m_r0, m_ra, m_rb, m_rz, m_tot, m_rc, p_r0, p_ra, p_rb, p_rz, p_tot, p_rc, t_r0, t_ra, t_rb, t_rz, t_tot, t_rc,
     edge, sums, gsum, vsum, vbuf, hin, mine, inbox,
     rs, rr, vs, vr, cs, cr, es, er, isem, gsem, lsem) = refs
    p = Place()
    me = p.me
    rows, width = tokens.shape

    inbox[...] = jnp.zeros_like(inbox)
    edge[...] = jnp.zeros_like(edge)
    entry_barrier(p, count, reach)

    red_m = [
        Reduce(p, i_gm.at[k], own_m, (k,), (m_r0, m_ra, m_rb, m_rz, m_tot, m_rc), (k,), rs.at[k], rr.at[k],
               pltpu.make_async_copy(i_gm.at[k, p.core], own_m.at[k], lsem.at[k]))
        for k in range(3)
    ]
    pbufs = (p_r0, p_ra, p_rb, p_rz, p_tot, p_rc)
    red_out, red_py, red_px = [
        Reduce(p, g, g, (p.core,), pbufs, (k,), rs.at[3 + k], rr.at[3 + k])
        for k, g in enumerate((gout, gpy, gpx))
    ]
    red_gate = Reduce(p, ggate, ggate, (p.core,), (t_r0, t_ra, t_rb, t_rz, t_tot, t_rc), (), rs.at[6], rr.at[6])

    for r in red_m:
        r.stage(0)
    loads = {}
    for i, (name, src, dst) in enumerate((
        ("db", i_db, db), ("wout", i_wout, wout), ("by", i_by, adj.at[:, 0:rows]), ("st", i_st, st), ("mixed", i_mixed, mixed),
        ("u1", i_u1, u1), ("fac", i_fac, fac), ("coded", i_coded, coded), ("wgate", i_wgate, wgate),
        ("wproj", i_wproj, wproj))):
        loads[name] = pltpu.make_async_copy(src, dst, isem.at[i])
        loads[name].start()

    def fetch(g, slot):
        return [
            pltpu.make_async_copy(src.at[g], gslot.at[slot, i, 0:rows], gsem.at[slot, i])
            for i, src in enumerate((i_gx, i_ga, i_sc))
        ]

    def fetch_bx(g, slot):
        return pltpu.make_async_copy(i_bx.at[g], gslot.at[slot, 0], gsem.at[slot, 3])

    for c in fetch(0, 0):
        c.start()
    since[...] = sequence_offset(lengths, me * rows, rows + 8)
    sums[...] = jnp.zeros_like(sums)
    gsum[...] = jnp.zeros_like(gsum)

    loads["db"].wait()
    loads["wout"].wait()

    def mix_dots(h, c):
        cols = pl.ds(pl.multiple_of(lax.rem(h, 2) * 256, 256), 256)
        v = nn(db[...], chips(wout[lax.div(h, 2), :, :, :, cols]))
        pp[2 * h], pp[2 * h + 1] = v[:, :128], v[:, 128:]
        return c

    lax.fori_loop(0, 4, mix_dots, 0)
    loads["by"].wait()
    loads["st"].wait()
    red_m[0].stage(1)

    def branch_y(g, r0):
        at = pl.ds(r0, 64)
        dm = pp[g, at, :]
        act, slope = gelu_parts(adj[g, at, :])
        adj[g, at, :] = dm * act
        dby[g, at, :] = (dm * st[g, pl.ds(r0 + 8, 64), :] * slope).astype(BF16)

    blocks_loop(8, rows, 64, branch_y)
    red_m[1].stage(1)
    loads["mixed"].wait()

    def halves(target, left, page):
        for h in range(2):
            v = tn(left, jnp.concatenate([page[4 * h + i] for i in range(4)], axis=1))
            put_chips(target, h, v.astype(BF16))

    halves(gout, db[...], mixed)
    red_out.stage(0)
    red_m[2].stage(1)
    loads["u1"].wait()
    halves(gpy, u1[...], dby)
    red_py.stage(0)
    red_m[0].stage(2)
    loads["fac"].wait()
    ends = scan_segments(rows, fac, adj, pp, 0, 0, 0, True)
    _, leave = chain(ends, [jnp.zeros((1, 128), F32)] * 8, True)
    whole = products(ends)
    for g in range(8):
        mine[0, g : g + 1, :] = whole[g]
        mine[1, g : g + 1, :] = leave[g]
    carry_send(p, count, reach, -1, mine, inbox, cs, cr)
    red_out.stage(1)
    red_m[0].stage(3)
    carry_wait(p, count, reach, -1, mine, inbox, cs, cr)
    inside, _ = chain(ends, carry_fold(p, count, reach, -1, inbox), True)
    for g in range(8):
        hin[g] = inside[g]
    step = rows // SEG

    def adjoint(g, c):
        for s in range(SEG):
            lo = s * step
            adj[g, lo : lo + step, :] += pp[g, lo : lo + step, :] * hin[g, s : s + 1, :]
        return c

    lax.fori_loop(0, 8, adjoint, 0)
    red_m[1].stage(2)
    red_py.stage(1)
    loads["coded"].wait()
    dga = mixed

    def gate_back(g, slot, last):
        @pl.when(jnp.logical_not(last))
        def _():
            for c_ in fetch(g + 1, 1 - slot):
                c_.start()

        for c_ in fetch(g, slot):
            c_.wait()
        row = par[g]
        sp8 = -8.0 * softplus(row[7:8])

        def block(i, acc):
            r0 = pl.multiple_of(i * 64, 64)
            at = pl.ds(r0, 64)
            a, f = adj[g, at, :], fac[g, at, :]
            gate_x, gate_a, scale = gslot[slot, 0, at, :], gslot[slot, 1, at, :], gslot[slot, 2, at, :]
            code = coded[g, at, :].astype(F32)
            before = st[g, pl.ds(r0, 72), :][7:71]
            d_log = a * f * (before - gate_x * code * f / scale)
            d_a = d_log * gate_a
            d_ga = d_a * sp8 * (1.0 - gate_a)
            d_part = a * scale * gate_x
            d_gx = d_part * code * (1.0 - gate_x)
            dgx[g, at, :] = d_gx.astype(BF16)
            dga[g, at, :] = d_ga.astype(BF16)
            adj[g, at, :] = d_part
            return acc[0] + fold8(d_gx), acc[1] + fold8(d_ga), acc[2] + fold8(d_a)

        zero = jnp.zeros((8, 128), F32)
        acc = lax.fori_loop(0, rows // 64, block, (zero, zero, zero))
        slope = jax.nn.sigmoid(row[7:8])
        sums[g, 5:6, :] = jnp.sum(acc[0], axis=0, keepdims=True)
        sums[g, 6:7, :] = jnp.sum(acc[1], axis=0, keepdims=True)
        sums[g, 7:8, :] = jnp.sum(acc[2], axis=0, keepdims=True) * (-8.0 * slope)

    pairs_loop(gate_back)
    fetch_bx(0, 0).start()
    load_dmid = pltpu.make_async_copy(i_dmid, st.at[0:6, 0:rows], isem.at[10])
    load_dmid.start()
    dbx = dgx
    red_m[2].stage(2)
    red_m[1].stage(3)
    red_m[0].stage(4)
    loads["wgate"].wait()

    def gate_dots(h, c):
        dx, da, code = lanes(dgx, 2 * h, 0, rows), lanes(dga, 2 * h, 0, rows), lanes(coded, 2 * h, 0, rows)
        v = nt(dx, wgate[0, :, h].reshape(256, 256)) + nt(da, wgate[1, :, h].reshape(256, 256))
        adj[2 * h, 0:rows, :] += v[:, :128]
        adj[2 * h + 1, 0:rows, :] += v[:, 128:]
        ggate[0, :, h] = tn(code, dx).astype(BF16).reshape(4, 64, 256)
        ggate[1, :, h] = tn(code, da).astype(BF16).reshape(4, 64, 256)
        return c

    lax.fori_loop(0, 4, gate_dots, 0)
    red_gate.stage(0)
    edge[0] = adj[:, 0:8, :]
    to_prev = remote(edge.at[0], edge.at[1], es.at[0], er.at[0], me - 1)

    @pl.when(me > 0)
    def _():
        to_prev.start()

    red_out.stage(2)
    red_m[2].stage(3)
    red_py.stage(2)
    red_m[1].stage(4)

    @pl.when(me > 0)
    def _():
        to_prev.wait_send()

    @pl.when(me + 1 < count)
    def _():
        to_prev.wait_recv()

    adj[:, rows : rows + 8, :] = edge[1]

    def conv_back(g, slot, last):
        @pl.when(jnp.logical_not(last))
        def _():
            fetch_bx(g + 1, 1 - slot).start()

        fetch_bx(g, slot).wait()
        row = par[g]

        def block(i, acc):
            r0 = pl.multiple_of(i * 64, 64)
            d = adj[g, pl.ds(r0, 72), :]
            off = since[pl.ds(r0, 72), :]
            b = gslot[slot, 0, pl.ds(r0 + 8, 72), :]
            own, off0 = d[0:64], off[0:64]
            total = row[0:1] * own
            out = [acc[0] + fold8(own * b[8:72])]
            for k in range(1, 4):
                total = total + row[k : k + 1] * jnp.where(off[k : 64 + k] >= k, d[k : 64 + k], 0.0)
                out.append(acc[k] + fold8(own * jnp.where(off0 >= k, b[8 - k : 72 - k], 0.0)))
            out.append(acc[4] + fold8(own))
            dbx[g, pl.ds(r0, 64), :] = total.astype(BF16)
            return tuple(out)

        acc = lax.fori_loop(0, rows // 64, block, tuple(jnp.zeros((8, 128), F32) for _ in range(5)))
        for k in range(5):
            sums[g, k : k + 1, :] = jnp.sum(acc[k], axis=0, keepdims=True)

    pairs_loop(conv_back)
    halves(gpx, u1[...], dbx)
    red_px.stage(0)
    red_gate.stage(1)
    red_out.stage(3)
    red_py.stage(3)
    red_m[2].stage(4)
    loads["wproj"].wait()
    du = nt(jnp.concatenate([dbx[g] for g in range(8)], axis=1), chips(wproj[0])) + nt(
        jnp.concatenate([dby[g] for g in range(8)], axis=1), chips(wproj[1])
    )
    put(pp, du, 0, 0)
    red_px.stage(1)
    red_gate.stage(2)
    red_out.stage(4)
    red_py.stage(4)

    load_dmid.wait()

    def finish(r0):
        at = pl.ds(r0, 32)
        x = tokens[at, :].astype(F32)
        d = wide(pp, 6, r0, 32)
        inv = lax.rsqrt(jnp.mean(x * x, axis=1, keepdims=True) + EPSILON)
        gsum[...] += fold8(d * x * inv)
        scaled = d * gain[0:1, :]
        back = jnp.mean(scaled * x, axis=1, keepdims=True)
        grad_tokens[at, :] = (wide(st, 6, r0, 32) + inv * scaled - x * (inv * inv * inv * back)).astype(BF16)

    rows_loop(rows, 32, finish)
    vsum[0] = jnp.zeros((16, 1024), F32)
    for g in range(8):
        vsum[0, 0:8, g * 128 : (g + 1) * 128] = sums[g]
    vsum[0, 8:9, 0:width] = jnp.sum(gsum[...], axis=0, keepdims=True)
    vsum[0, 9:10, 0:width] = jnp.sum(gg2[...], axis=0, keepdims=True)
    tot = Totals(p, vsum, vbuf, vs, vr)
    tot.stage(0)
    red_px.stage(2)
    tot.step(0)
    tot.stage(1)
    red_gate.stage(3)
    tot.step(1)
    tot.stage(2)
    red_px.stage(3)
    tot.step(2)
    tot.stage(3)
    red_gate.stage(4)
    for k in range(3):
        left, right = red_m[k].stage(5)
        lo = 24 * k
        o_in[lo : lo + 24, 0:1152] = left
        o_in[lo : lo + 24, 1152:1536] = right[:, :384]
        o_down[lo : lo + 24, :] = right[:, 384:]
    left, right = red_out.stage(5)
    o_out[:, :512], o_out[:, 512:] = left, right
    left, right = red_py.stage(5)
    o_proj[:, 1024:1536], o_proj[:, 1536:2048] = left, right
    red_px.stage(4)
    left, right = red_gate.stage(5)
    o_gate[:, :256], o_gate[:, 256:] = left, right
    total = tot.step(3)
    chan = pltpu.roll(total[0:8], lax.rem(1024 - 32 * me, 1024), 1)
    o_cw[...] = chan[0:4, 0:32]
    o_cb[...] = chan[4:5, 0:32]
    o_gb[...] = chan[5:7, 0:32]
    o_dec[...] = chan[7:8, 0:32]
    gains = pltpu.roll(total[8:16], lax.rem(1024 - 24 * me, 1024), 1)
    o_g1[...] = gains[0:1, 0:24]
    o_g2[...] = gains[1:2, 0:24]
    left, right = red_px.stage(5)
    o_proj[:, 0:512], o_proj[:, 512:1024] = left, right


def backward_call(count, reach, args):
    tokens = args[0]
    rows, width = tokens.shape
    S = jax.ShapeDtypeStruct
    V = pltpu.VMEM
    dma = pltpu.SemaphoreType.DMA
    page = (8, rows, 128)
    outs = [
        S((rows, width), BF16), S((24, 2048), F32), S((24, 1024), F32), S((32, 512), F32), S((72, 1536), F32),
        S((72, 768), F32), S((4, 32), F32), S((1, 32), F32), S((2, 32), F32), S((1, 32), F32), S((1, 24), F32),
        S((1, 24), F32),
    ]

    def bufs(n, r, c):
        lead = (n,) if n else ()
        return [V(lead + (4, 4, r, c), BF16), V(lead + (2, 4, r, c), BF16), V(lead + (4, r, c), BF16),
                V(lead + (3, r, c), BF16), V(lead + (2, r // 2, c), F32), V(lead + (r // 2, c), F32)]

    scratch = [
        V((2, 4, 4, 48, 1024), BF16), V((2, 4, 4, 64, 256), BF16), V((2, 4, 4, 48, 512), BF16),
        V((8, rows + 8, 128), F32),
        V(page, F32),
        V((8, rows + 8, 128), F32),
        V(page, F32),
        V((2, 3, rows + 16, 128), F32),
        V(page, BF16), V(page, BF16), V((rows, width), BF16), V((rows, width), BF16),
        V(page, BF16), V(page, BF16),
        V((rows + 8, 128), jnp.int32),
        V((3, 4, 4, 48, 1152), BF16),
        V((2, 4, 4, 48, 512), BF16), V((2, 4, 4, 48, 512), BF16), V((2, 4, 4, 48, 512), BF16),
        V((2, 4, 4, 64, 256), BF16),
        *bufs(3, 48, 1152), *bufs(3, 48, 512), *bufs(0, 64, 256),
        V((2, 8, 8, 128), F32),
        V((8, 8, 128), F32), V((8, width), F32), V((4, 16, 1024), F32), V((6, 16, 1024), F32),
        V((8, 8, 128), F32), V((2, 8, 128), F32), V((reach, 2, 8, 128), F32),
        dma((7, 8)), dma((7, 8)), dma((6,)), dma((6,)), dma((reach,)), dma((reach,)), dma((1,)), dma((1,)),
        dma((11,)), dma((2, 4)), dma((3,)),
    ]
    return pl.pallas_call(
        functools.partial(backward_kernel, count, reach),
        out_shape=outs,
        in_specs=[VM, SM, VM, VM, VM] + [ANY] * 16,
        out_specs=[VM] * len(outs),
        scratch_shapes=scratch,
        name="backward",
        cost_estimate=pl.CostEstimate(flops=12 * 10**9, bytes_accessed=60 * 10**6, transcendentals=10**7),
        compiler_params=pltpu.CompilerParams(
            collective_id=1, has_side_effects=True, vmem_limit_bytes=63 * MIB
        ),
    )(*args)


def from_behind(x, axis, by):
    size = lax.axis_size(axis)
    pairs = [(i, i + by) for i in range(size) if 0 <= i + by < size]
    return lax.ppermute(x, axis, pairs)


def prefix(part, axis, combine, identity, reverse):
    count = lax.axis_size(axis)
    place = lax.axis_index(axis)
    ahead = count - 1 - place if reverse else place
    gathered = jax.tree.map(lambda a: lax.all_gather(a, axis), part)
    state = jax.tree.map(lambda a, e: jnp.zeros_like(a) + jnp.asarray(e, a.dtype), part, identity)

    def one(lap, state):
        source = count - 1 - lap if reverse else lap
        return combine(
            state, jax.tree.map(lambda a: lax.dynamic_index_in_dim(a, source, 0, False), gathered)
        )

    return lax.fori_loop(0, ahead, one, state)


def rms_scale(values, gain_row):
    inverse = lax.rsqrt(jnp.mean(values * values, axis=-1, keepdims=True) + EPSILON)
    return values * inverse * gain_row


def combine_steps(earlier, later):
    return (earlier[0] * later[0], later[0] * earlier[1] + later[1])


def smooth_gelu(inputs):
    return jax.nn.gelu(inputs, approximate=True)


def glu_piece(gate_pre, up_value):
    return smooth_gelu(gate_pre) * up_value


def gate_math(gate_pre, bias_rows, decay_vec, coded_rows, fresh_row):
    tok_rows, rnn_width = coded_rows.shape
    block_size = gate_pre.shape[2] // 2
    gate_x = jax.nn.sigmoid(gate_pre[:, :, :block_size].reshape(tok_rows, rnn_width) + bias_rows[0])
    gate_a = jax.nn.sigmoid(gate_pre[:, :, block_size:].reshape(tok_rows, rnn_width) + bias_rows[1])
    log_a = -8.0 * gate_a * jax.nn.softplus(decay_vec)
    factor = jnp.where(fresh_row, 0.0, jnp.exp(log_a))
    scale_term = jnp.where(fresh_row, 1.0, jnp.sqrt(-jnp.expm1(2.0 * log_a)))
    return (factor, scale_term * gate_x * coded_rows)


def per_device(
    tokens,
    cotangent,
    lengths,
    gain_norm1,
    gain_norm2,
    proj_in,
    out_proj,
    gate_blocks,
    conv_weight,
    conv_bias,
    gate_bias,
    decay_param,
    mlp_in,
    mlp_down,
):
    tok_rows, model_width = tokens.shape
    conv_taps = conv_weight.shape[0]
    reach_back = conv_taps - 1
    first_row = lax.axis_index("dp") * tok_rows
    places = first_row + jnp.arange(-reach_back, tok_rows, dtype=jnp.int32)
    bounds = jnp.cumsum(lengths)
    labels = jnp.sum((places[:, None] >= bounds[None, :]).astype(jnp.int32), axis=1)
    labels = jnp.where(places < 0, -1, labels)
    own_label = labels[reach_back:]
    fresh_row = (own_label != labels[reach_back - 1 : reach_back - 1 + tok_rows])[:, None]
    tap_masks = [
        (labels[reach_back - offset : reach_back - offset + tok_rows] == own_label)[:, None].astype(
            jnp.float32
        )
        for offset in range(conv_taps)
    ]
    gathered = (
        lax.all_gather(proj_in, "dp", axis=0, tiled=True),
        lax.all_gather(out_proj, "dp", axis=0, tiled=True),
        lax.all_gather(gate_blocks, "dp", axis=0, tiled=True),
        lax.all_gather(gain_norm1, "dp", axis=0, tiled=True),
        lax.all_gather(gain_norm2, "dp", axis=0, tiled=True),
        lax.all_gather(conv_weight, "dp", axis=1, tiled=True),
        lax.all_gather(conv_bias, "dp", axis=0, tiled=True),
        lax.all_gather(gate_bias, "dp", axis=1, tiled=True),
        lax.all_gather(decay_param, "dp", axis=0, tiled=True),
    )
    w_proj, w_out, w_gates = (gathered[0], gathered[1], gathered[2])
    gain_one = gathered[3].astype(jnp.float32)
    gain_two = gathered[4].astype(jnp.float32)
    w_conv = gathered[5].astype(jnp.float32)
    b_conv = gathered[6].astype(jnp.float32)
    b_gates = gathered[7].astype(jnp.float32)
    w_decay = gathered[8].astype(jnp.float32)
    rnn_width = w_conv.shape[1]
    w_mlp, w_down = (
        lax.all_gather(mlp_in, "dp", axis=0, tiled=True),
        lax.all_gather(mlp_down, "dp", axis=0, tiled=True),
    )
    residual = tokens.astype(jnp.float32)
    normed_one, norm_one_back = jax.vjp(rms_scale, residual, gain_one)
    u_one = normed_one.astype(jnp.bfloat16)
    projected = jnp.dot(u_one, w_proj, preferred_element_type=jnp.float32)
    branch_x = projected[:, :rnn_width].astype(jnp.bfloat16)
    branch_y = projected[:, rnn_width:]
    rim_rows = from_behind(branch_x[tok_rows - reach_back :], "dp", 1)
    padded = jnp.concatenate([rim_rows, branch_x], axis=0)
    conv_sum = jnp.zeros((tok_rows, rnn_width), jnp.float32) + b_conv
    for offset in range(conv_taps):
        conv_sum = (
            conv_sum
            + w_conv[offset]
            * padded[reach_back - offset : reach_back - offset + tok_rows].astype(jnp.float32)
            * tap_masks[offset]
        )
    coded_rows = conv_sum.astype(jnp.bfloat16)
    block_size = w_gates.shape[1] // 2
    head_count = rnn_width // block_size
    blocks_w = w_gates.reshape(head_count, block_size, 2 * block_size)
    coded_heads = coded_rows.reshape(tok_rows, head_count, block_size)
    gate_pre = jnp.einsum("thi,hij->thj", coded_heads, blocks_w, preferred_element_type=jnp.float32)
    gate_fn = functools.partial(gate_math, fresh_row=fresh_row)
    (factor, drive_term), gate_back = jax.vjp(
        gate_fn, gate_pre, b_gates, w_decay, coded_rows.astype(jnp.float32)
    )
    prefix_a, local_h = lax.associative_scan(combine_steps, (factor, drive_term), axis=0)
    unit_pair = (jnp.ones((rnn_width,), jnp.float32), jnp.zeros((rnn_width,), jnp.float32))
    carry_unused, carry_h = prefix(
        (prefix_a[-1], local_h[-1]), "dp", combine_steps, unit_pair, False
    )
    state_rows = local_h + prefix_a * carry_h[None, :]
    y_branch_act, y_back = jax.vjp(smooth_gelu, branch_y)
    mixed_rows = (state_rows * y_branch_act).astype(jnp.bfloat16)
    middle = residual + jnp.einsum(
        "tr,dr->td", mixed_rows, w_out, preferred_element_type=jnp.float32
    )
    normed_two, norm_two_back = jax.vjp(rms_scale, middle, gain_two)
    u_two = normed_two.astype(jnp.bfloat16)
    gate_val = jnp.einsum(
        "td,fd->tf", u_two, w_mlp[:, :model_width], preferred_element_type=jnp.float32
    )
    up_val = jnp.einsum(
        "td,fd->tf", u_two, w_mlp[:, model_width:], preferred_element_type=jnp.float32
    )
    glu_value, glu_back = jax.vjp(glu_piece, gate_val, up_val)
    hidden = glu_value.astype(jnp.bfloat16)
    output = (middle + jnp.dot(hidden, w_down, preferred_element_type=jnp.float32)).astype(
        jnp.bfloat16
    )
    w_proj, w_out, w_gates = (
        lax.all_gather(proj_in, "dp", axis=0, tiled=True),
        lax.all_gather(out_proj, "dp", axis=0, tiled=True),
        lax.all_gather(gate_blocks, "dp", axis=0, tiled=True),
    )
    w_mlp, w_down = (
        lax.all_gather(mlp_in, "dp", axis=0, tiled=True),
        lax.all_gather(mlp_down, "dp", axis=0, tiled=True),
    )
    blocks_w = w_gates.reshape(head_count, block_size, 2 * block_size)
    d_hidden = jnp.einsum("td,fd->tf", cotangent, w_down, preferred_element_type=jnp.float32)
    d_gate_f, d_up_f = glu_back(d_hidden)
    d_gate = d_gate_f.astype(jnp.bfloat16)
    d_up = d_up_f.astype(jnp.bfloat16)
    feed_sum = None
    d_u_two = jnp.einsum(
        "tf,fd->td", d_gate, w_mlp[:, :model_width], preferred_element_type=jnp.float32
    )
    d_u_two = d_u_two + jnp.einsum(
        "tf,fd->td", d_up, w_mlp[:, model_width:], preferred_element_type=jnp.float32
    )
    d_norm_mid, d_gain_two = norm_two_back(d_u_two)
    d_middle = cotangent.astype(jnp.float32) + d_norm_mid
    d_branch = d_middle.astype(jnp.bfloat16)
    d_mixed = jnp.dot(d_branch, w_out, preferred_element_type=jnp.float32)
    d_state = d_mixed * y_branch_act
    d_branch_y = y_back(d_mixed * state_rows)[0].astype(jnp.bfloat16)
    ahead_factor = jnp.concatenate([factor[1:], jnp.ones((1, rnn_width), jnp.float32)], axis=0)
    back_prod, local_g = lax.associative_scan(
        combine_steps, (ahead_factor, d_state), reverse=True, axis=0
    )
    carry_skip, carry_q = prefix(
        (factor[0] * back_prod[0], factor[0] * local_g[0]), "dp", combine_steps, unit_pair, True
    )
    adjoint = local_g + back_prod * carry_q[None, :]
    before = jnp.concatenate([carry_h[None, :], state_rows[:-1]], axis=0)
    d_pre_f, d_shift, d_decay, d_coded_part = gate_back((adjoint * before, adjoint))
    d_pre = d_pre_f.astype(jnp.bfloat16)
    d_coded = d_coded_part + jnp.einsum(
        "thj,hij->thi", d_pre, blocks_w, preferred_element_type=jnp.float32
    ).reshape(tok_rows, rnn_width)
    gate_grad = jnp.einsum(
        "thi,thj->hij", coded_heads, d_pre, preferred_element_type=jnp.float32
    ).reshape(rnn_width, 2 * block_size)
    spread = jnp.zeros((tok_rows + reach_back, rnn_width), jnp.float32)
    tap_grads = []
    for offset in range(conv_taps):
        spread = spread + jnp.pad(
            w_conv[offset] * tap_masks[offset] * d_coded, ((reach_back - offset, offset), (0, 0))
        )
        tap_grads.append(
            jnp.sum(
                d_coded
                * tap_masks[offset]
                * padded[reach_back - offset : reach_back - offset + tok_rows].astype(jnp.float32),
                axis=0,
            )
        )
    d_conv_w = jnp.stack(tap_grads, axis=0)
    d_conv_b = jnp.sum(d_coded, axis=0)
    back_rim = from_behind(spread[:reach_back], "dp", -1)
    d_branch_x = (
        spread[reach_back:] + jnp.pad(back_rim, ((tok_rows - reach_back, 0), (0, 0)))
    ).astype(jnp.bfloat16)
    d_projected = jnp.concatenate([d_branch_x, d_branch_y], axis=1)
    d_u_one = jnp.einsum("tk,dk->td", d_projected, w_proj, preferred_element_type=jnp.float32)
    d_norm_in, d_gain_one = norm_one_back(d_u_one)
    grad_tokens = (d_middle + d_norm_in).astype(jnp.bfloat16)
    part_gate = jnp.einsum("tf,td->fd", d_gate, u_two, preferred_element_type=jnp.float32)
    part_up = jnp.einsum("tf,td->fd", d_up, u_two, preferred_element_type=jnp.float32)
    part_down = jnp.einsum("tf,td->fd", hidden, cotangent, preferred_element_type=jnp.float32)
    feed_sum = lax.psum_scatter(
        jnp.concatenate([part_gate, part_up, part_down], axis=1),
        "dp",
        scatter_dimension=0,
        tiled=True,
    )
    part_proj = jnp.einsum("td,tk->dk", u_one, d_projected, preferred_element_type=jnp.float32)
    part_out = jnp.einsum("td,tr->dr", d_branch, mixed_rows, preferred_element_type=jnp.float32)
    rec_sum = lax.psum_scatter(
        jnp.concatenate([part_proj, part_out], axis=1), "dp", scatter_dimension=0, tiled=True
    )
    channel_sums = (
        lax.psum_scatter(d_gain_one, "dp", scatter_dimension=0, tiled=True),
        lax.psum_scatter(d_gain_two, "dp", scatter_dimension=0, tiled=True),
        lax.psum_scatter(d_conv_w, "dp", scatter_dimension=1, tiled=True),
        lax.psum_scatter(d_conv_b, "dp", scatter_dimension=0, tiled=True),
        lax.psum_scatter(d_shift, "dp", scatter_dimension=1, tiled=True),
        lax.psum_scatter(d_decay, "dp", scatter_dimension=0, tiled=True),
        lax.psum_scatter(gate_grad, "dp", scatter_dimension=0, tiled=True),
    )
    return (
        output,
        grad_tokens,
        channel_sums[0],
        channel_sums[1],
        rec_sum[:, : 2 * rnn_width],
        rec_sum[:, 2 * rnn_width :],
        channel_sums[6],
        channel_sums[2],
        channel_sums[3],
        channel_sums[4],
        channel_sums[5],
        feed_sum[:, : 2 * model_width],
        feed_sum[:, 2 * model_width :],
    )


def kernels_step(
    tokens, cotangent, lengths, gain_norm1, gain_norm2, proj_in, out_proj, gate_blocks, conv_weight, conv_bias, gate_bias,
    decay_param, mlp_in, mlp_down,
):
    count = lax.axis_size("dp")
    rows = tokens.shape[0]
    longest = rows * count // 12
    reach = -(-(longest - 1) // rows)
    (output, par, gain, gg2, wproj, wgate, wout, gm, by, fac, gx, ga, sc, st, bx, coded, mixed, u1, dmid, db) = forward_call(
        count, reach,
        (tokens, cotangent, lengths, conv_weight, conv_bias[None], gate_bias, decay_param[None], gain_norm1[None],
         gain_norm2[None], proj_in, out_proj, gate_blocks, mlp_in, mlp_down),
    )
    (grad_tokens, g_proj, g_out, g_gate, g_in, g_down, g_cw, g_cb, g_gb, g_dec, g_n1, g_n2) = backward_call(
        count, reach,
        (tokens, lengths, par, gain, gg2, wproj, wgate, wout, gm, by, fac, gx, ga, sc, st, bx, coded, mixed, u1, dmid, db),
    )
    return (
        output, grad_tokens, g_n1[0], g_n2[0], g_proj, g_out, g_gate, g_cw, g_cb[0], g_gb, g_dec[0], g_in, g_down,
    )


def fits(mesh):
    return mesh.shape["dp"] == 32


def solution(mesh):
    placed = (
        P("dp", None),
        P("dp", None),
        P(),
        P("dp"),
        P("dp"),
        P("dp", None),
        P("dp", None),
        P("dp", None),
        P(None, "dp"),
        P("dp"),
        P(None, "dp"),
        P("dp"),
        P("dp", None),
        P("dp", None),
    )
    return jax.shard_map(
        kernels_step if fits(mesh) else per_device,
        mesh=mesh,
        in_specs=placed,
        out_specs=(
            P("dp", None),
            P("dp", None),
            P("dp"),
            P("dp"),
            P("dp", None),
            P("dp", None),
            P("dp", None),
            P(None, "dp"),
            P("dp"),
            P(None, "dp"),
            P("dp"),
            P("dp", None),
            P("dp", None),
        ),
        check_vma=False,
    )
```

```python
import functools

import jax
import jax.numpy as jnp
from jax import lax
from jax.experimental import pallas as pl
from jax.experimental.pallas import tpu as pltpu
from jax.sharding import PartitionSpec as P

EPSILON = 1e-06
MESH = pl.DeviceIdType.MESH
F32, BF16 = jnp.float32, jnp.bfloat16
VM = pl.BlockSpec(memory_space=pltpu.VMEM)
ANY = pl.BlockSpec(memory_space=pl.ANY)
SM = pl.BlockSpec(memory_space=pltpu.SMEM)
MIB = 2**20
SEG = 8
STEP = 97
PAD = 8


def nn(a, b):
    return jnp.dot(a, b, preferred_element_type=F32)


def nt(a, b):
    return lax.dot_general(a, b, (((1,), (1,)), ((), ())), preferred_element_type=F32)


def tn(a, b):
    return lax.dot_general(a, b, (((0,), (0,)), ((), ())), preferred_element_type=F32)


class Place:
    def __init__(self):
        me = lax.axis_index("dp")
        self.me = me
        self.core = core = lax.rem(me, 2)
        x = lax.rem(lax.div(me, 2), 2)
        y = lax.rem(lax.div(me, 4), 2)
        self.z = z = lax.div(me, 8)
        self.yx = yx = 2 * y + x
        px, py = me + 2 - 4 * x, me + 4 - 8 * y
        gx, gy = yx + 1 - 2 * x, yx + 2 - 4 * y
        self.pa, self.pb = px + core * (py - px), py + core * (px - py)
        self.ga, self.gb = gx + core * (gy - gx), gy + core * (gx - gy)
        self.gd = 3 - yx
        self.pc = me + 1 - 2 * core
        self.other = 1 - core
        self.zs = [lax.rem(z + d, 4) for d in (1, 2, 3)]
        self.pz = [zz * 8 + lax.rem(me, 8) for zz in self.zs]


def remote(src, dst, ssem, rsem, device):
    return pltpu.make_async_remote_copy(
        src_ref=src, dst_ref=dst, send_sem=ssem, recv_sem=rsem, device_id=(device,), device_id_type=MESH
    )


def entry_barrier(pl_, count, reach):
    me = pl_.me
    bar = pltpu.get_barrier_semaphore()
    for p in [pl_.pc, pl_.pa, pl_.pb] + pl_.pz:
        pl.semaphore_signal(bar, inc=1, device_id=(p,), device_id_type=MESH)
    for d in range(1, reach + 1):

        @pl.when(me >= d)
        def _():
            pl.semaphore_signal(bar, inc=1, device_id=(me - d,), device_id_type=MESH)

        @pl.when(me + d < count)
        def _():
            pl.semaphore_signal(bar, inc=1, device_id=(me + d,), device_id_type=MESH)

    pl.semaphore_wait(bar, 6 + jnp.minimum(me, reach) + jnp.minimum(count - 1 - me, reach))


class Gather:
    def __init__(self, p, buf, ssem, rsem):
        self.p, self.buf, self.ssem, self.rsem = p, buf, ssem, rsem

    def copy(self, slot):
        p = self.p
        if slot < 3:
            src, dev = self.buf.at[p.core, p.yx, p.z], p.pz[slot]
        else:
            group = (p.yx, p.yx, p.ga, p.yx, p.ga, p.gb, p.gd)[slot - 3]
            src, dev = self.buf.at[p.core, group], (p.pa, p.pb, p.pb, p.pc, p.pc, p.pc, p.pc)[slot - 3]
        return remote(src, src, self.ssem.at[slot], self.rsem.at[slot], dev)

    def start(self, *slots):
        for s in slots:
            self.copy(s).start()

    def recv(self, *slots):
        for s in slots:
            self.copy(s).wait_recv()

    def stage(self, n):
        if n == 0:
            self.start(0, 1, 2)
        elif n == 1:
            self.recv(0, 1, 2)
            self.start(3, 4, 6)
        elif n == 2:
            self.recv(3)
            self.start(5, 7)
        elif n == 3:
            self.recv(4)
            self.start(8)
            self.recv(5)
            self.start(9)
        else:
            self.recv(6, 7, 8, 9)
            for s in range(10):
                self.copy(s).wait_send()


def sequence_offset(lengths, first, rows):
    t = first + lax.broadcasted_iota(jnp.int32, (rows, 128), 0)

    def one(i, c):
        bound, start = c
        bound = bound + lengths[i]
        return bound, jnp.where(t >= bound, bound, start)

    _, start = lax.fori_loop(0, lengths.shape[0], one, (jnp.int32(0), jnp.zeros((rows, 128), jnp.int32)))
    return t - start


def one_minus_square(v, root):
    series = 1.0 / 2.0 + v * (1.0 / 6.0 + v * (1.0 / 24.0 + v * (1.0 / 120.0 + v * (1.0 / 720.0))))
    return jnp.where(v > -0.125, -v - v * v * series, 1.0 - root * root)


def root_of(v):
    return v * lax.rsqrt(jnp.maximum(v, 1e-37))


def softplus(v):
    return jnp.maximum(v, 0.0) + jnp.log1p(jnp.exp(-jnp.abs(v)))


GELU_K = 0.7978845608028654


def gelu_parts(v):
    v2 = v * v
    th = jnp.tanh(GELU_K * v * (1.0 + 0.044715 * v2))
    half = 0.5 * (1.0 + th)
    slope = half + 0.5 * v * (1.0 - th * th) * (GELU_K * (1.0 + 3.0 * 0.044715 * v2))
    return v * half, slope


def gelu(v):
    return v * (0.5 * (1.0 + jnp.tanh(GELU_K * v * (1.0 + 0.044715 * (v * v)))))


def flat(v):
    return v.reshape(v.shape[0] * v.shape[1] * v.shape[2], v.shape[3])


def chips(v):
    return jnp.concatenate([v[yx, z] for z in range(4) for yx in range(4)], axis=0)


def whole_w(w):
    return jnp.concatenate([chips(w[0]), chips(w[1])], axis=1)


def put_chips(part, half, v):
    rows = v.shape[0] // 16
    for z in range(4):
        for yx in range(4):
            part[half, yx, z] = v[(4 * z + yx) * rows : (4 * z + yx + 1) * rows]


def put(page, v, row, group):
    for i in range(v.shape[1] // 128):
        page[group + i, row : row + v.shape[0], :] = v[:, i * 128 : (i + 1) * 128]


def rows_loop(total, block, body):
    def one(i, c):
        body(pl.multiple_of(i * block, block))
        return c

    lax.fori_loop(0, total // block, one, 0)


def blocks_loop(groups, total, block, body):
    n = total // block

    def one(i, c):
        body(lax.div(i, n), pl.multiple_of(lax.rem(i, n) * block, block))
        return c

    lax.fori_loop(0, groups * n, one, 0)


def pairs_loop(body):
    def one(i, c):
        body(2 * i, 0, False)
        body(2 * i + 1, 1, i == 3)
        return c

    lax.fori_loop(0, 4, one, 0)


def scan_segments(factor, value, product, factor_row, value_row, product_row, reverse):
    def one(i, c):
        j = STEP - 1 - i if reverse else i
        out = []
        for g in range(8):
            h, q = c[g]
            a = factor[g, pl.ds(factor_row + j, SEG, stride=STEP), :]
            b = value[g, pl.ds(value_row + j, SEG, stride=STEP), :]
            if reverse:
                h = b + h
                value[g, pl.ds(value_row + j, SEG, stride=STEP), :] = h
                product[g, pl.ds(product_row + j, SEG, stride=STEP), :] = q
                h, q = a * h, a * q
            else:
                h, q = a * h + b, a * q
                value[g, pl.ds(value_row + j, SEG, stride=STEP), :] = h
                product[g, pl.ds(product_row + j, SEG, stride=STEP), :] = q
            out.append((h, q))
        return tuple(out)

    first = tuple((jnp.zeros((SEG, 128), F32), jnp.ones((SEG, 128), F32)) for _ in range(8))
    return lax.fori_loop(0, STEP, one, first)


def segment_rows(inside, i, block):
    rest = inside[i : i + 1, :]
    first = jnp.broadcast_to(rest, (8, 128))
    if i:
        spot = lax.broadcasted_iota(jnp.int32, (8, 128), 0)
        first = jnp.where(spot < i, inside[i - 1 : i, :], first)
    return jnp.concatenate([first, jnp.broadcast_to(rest, (block - 8, 128))], axis=0)


def chain(ends, enter, reverse):
    order = range(SEG - 1, -1, -1) if reverse else range(SEG)
    inside, leave = [], []
    for g in range(8):
        h, q = ends[g]
        v = enter[g]
        rows = [None] * SEG
        for s in order:
            rows[s] = v
            v = q[s : s + 1, :] * v + h[s : s + 1, :]
        inside.append(jnp.concatenate(rows, axis=0))
        leave.append(v)
    return inside, leave


def products(ends):
    out = []
    for g in range(8):
        q = ends[g][1]
        v = q[0:1, :]
        for s in range(1, SEG):
            v = v * q[s : s + 1, :]
        out.append(v)
    return out


def carry_send(p, count, reach, sign, mine, inbox, ssem, rsem):
    for d in range(1, reach + 1):

        @pl.when((p.me + d < count) if sign > 0 else (p.me >= d))
        def _(d=d):
            remote(mine, inbox.at[d - 1], ssem.at[d - 1], rsem.at[d - 1], p.me + sign * d).start()


def carry_wait(p, count, reach, sign, mine, inbox, ssem, rsem):
    for d in range(1, reach + 1):
        there = remote(mine, inbox.at[d - 1], ssem.at[d - 1], rsem.at[d - 1], p.me + sign * d)

        @pl.when((p.me + d < count) if sign > 0 else (p.me >= d))
        def _(there=there):
            there.wait_send()

        @pl.when((p.me >= d) if sign > 0 else (p.me + d < count))
        def _(there=there):
            there.wait_recv()


def carry_fold(p, count, reach, sign, inbox):
    v = [jnp.zeros((1, 128), F32) for _ in range(8)]
    for d in range(reach, 0, -1):
        for g in range(8):
            v[g] = inbox[d - 1, 0, g : g + 1, :] * v[g] + inbox[d - 1, 1, g : g + 1, :]
    return v


def lanes(page, group, row, rows):
    return jnp.concatenate([page[group, pl.ds(row, rows), :], page[group + 1, pl.ds(row, rows), :]], axis=1)


def wide(page, groups, row, rows):
    return jnp.concatenate([page[g, pl.ds(row, rows), :] for g in range(groups)], axis=1)


def fold8(v):
    return jnp.sum(v.reshape(v.shape[0] // 8, 8, v.shape[1]), axis=0)


def forward_kernel(count, reach, *refs):
    (tokens, cot, lengths, cw, cb, gb, dec, g1, g2, w_proj, w_out, w_gate, w_in, w_down,
     out, o_par, o_gain, o_gg2, o_wbx, o_wby, o_wgate, o_wout, o_by, o_fac, o_gx, o_ga, o_sc, o_st, o_bx, o_coded,
     o_mixed, o_u1, o_dmid, o_db, o_part0, o_part1, o_part2,
     wsmall, wbx, wby, wgate, wout, wm, bx, by, fac, dr, pq, gx, ga, sc, ubuf, coded, mixed, dup,
     since, rate, xh, ssmall, rsmall, sproj, rproj, sout, rout, sgate, rgate, smlp, rmlp, hin, mine, inbox, m_r0, m_ra, m_rb,
     gs, gr, ps, pr, hs, hr, cs, cr, rs, rr, osem, free) = refs
    p = Place()
    me = p.me
    rows, width = tokens.shape
    core0 = p.core == 0

    xh[...] = jnp.zeros_like(xh)
    inbox[...] = jnp.zeros_like(inbox)
    fac[:, rows:, :] = jnp.ones((8, PAD, 128), F32)
    dr[:, rows + 8 :, :] = jnp.zeros((8, PAD, 128), F32)
    entry_barrier(p, count, reach)

    halo = remote(tokens.at[rows - 16 : rows], xh, hs.at[0], hr.at[0], me + 1)

    @pl.when(me + 1 < count)
    def _():
        halo.start()

    lane = lax.broadcasted_iota(jnp.int32, (32, 128), 1)
    row = lax.broadcasted_iota(jnp.int32, (32, 128), 0)
    spot = jnp.where(lane == lax.rem(me, 4) * 32 + row, 1.0, 0.0).astype(BF16)
    gcol = lax.broadcasted_iota(jnp.int32, (24, width), 1)
    grow = lax.broadcasted_iota(jnp.int32, (24, width), 0)
    gspot = jnp.where(gcol == me * 24 + grow, 1.0, 0.0).astype(BF16)
    ssmall[...] = jnp.zeros_like(ssmall)
    ssmall[0:4, :] = nn(cw[...], spot)
    ssmall[4:5, :] = nn(cb[...], spot)
    ssmall[5:7, :] = nn(gb[...], spot)
    ssmall[7:8, :] = nn(dec[...], spot)
    r1, r2 = nn(g1[...], gspot), nn(g2[...], gspot)
    for j in range(width // 128):
        ssmall[8 + j : 9 + j, :] = r1[:, j * 128 : (j + 1) * 128]
        ssmall[16 + j : 17 + j, :] = r2[:, j * 128 : (j + 1) * 128]
    trades = [
        remote(ssmall, rsmall, ps.at[0], pr.at[0], p.pc),
        remote(sproj.at[0, p.other], rproj.at[0], ps.at[1], pr.at[1], p.pc),
        remote(sgate.at[p.other], rgate, ps.at[2], pr.at[2], p.pc),
        remote(sproj.at[1, p.other], rproj.at[1], ps.at[3], pr.at[3], p.pc),
        remote(sout.at[p.other], rout, ps.at[4], pr.at[4], p.pc),
        remote(smlp.at[p.other], rmlp, ps.at[5], pr.at[5], p.pc),
    ]
    trades[0].start()
    for n in range(2):
        for h in range(2):
            lo = n * 1024 + h * 512
            sproj[n, h] = w_proj[:, lo : lo + 512].astype(F32)
        if n == 0:
            trades[1].start()
    for h in range(2):
        sgate[h] = w_gate[:, h * 256 : (h + 1) * 256].astype(F32)
        sout[h] = w_out[:, h * 512 : (h + 1) * 512].astype(F32)
    trades[2].start()
    trades[3].start()
    trades[4].start()
    smlp[0] = w_in[:, :1152].astype(F32)
    smlp[1] = jnp.concatenate([w_in[:, 1152:], w_down[...]], axis=1).astype(F32)
    trades[5].start()

    g_small, g_bx, g_gate, g_by, g_out = [
        Gather(p, w, gs.at[i], gr.at[i]) for i, w in enumerate((wsmall, wbx, wgate, wby, wout))
    ]
    g_m = [Gather(p, wm.at[k], gs.at[5 + k], gr.at[5 + k]) for k in range(3)]

    def slab(mine_, theirs):
        first = jnp.where(core0, mine_, theirs)
        second = jnp.where(core0, theirs, mine_)
        return jnp.concatenate([first, second], axis=0).astype(BF16)

    trades[0].wait_recv()
    both = ssmall[...] + rsmall[...]
    wsmall[p.core, p.yx, p.z] = jnp.where(core0, both[0:16], both[16:32]).astype(BF16)
    g_small.stage(0)
    trades[1].wait_recv()
    wbx[p.core, p.yx, p.z] = slab(sproj[0, p.core], rproj[0])
    g_bx.stage(0)
    trades[2].wait_recv()
    wgate[p.core, p.yx, p.z] = slab(sgate[p.core], rgate[...])
    trades[3].wait_recv()
    wby[p.core, p.yx, p.z] = slab(sproj[1, p.core], rproj[1])
    trades[4].wait_recv()
    wout[p.core, p.yx, p.z] = slab(sout[p.core], rout[...])
    trades[5].wait_recv()
    for k in range(3):
        wm[k, p.core, p.yx, p.z] = slab(smlp[p.core, 24 * k : 24 * k + 24, :], rmlp[24 * k : 24 * k + 24, :])

    outs = []

    def save(src, dst):
        c = pltpu.make_async_copy(src, dst, osem.at[len(outs)])
        c.start()
        outs.append(c)
        return c

    g_small.stage(1)
    g_bx.stage(1)
    g_gate.stage(0)
    since[...] = sequence_offset(lengths, me * rows, rows)
    for t in trades:
        t.wait_send()
    g_small.stage(2)
    g_bx.stage(2)
    g_gate.stage(1)
    g_by.stage(0)
    g_small.stage(3)
    g_small.stage(4)

    for g in range(8):
        z_, yx_ = g // 2, 2 * (g % 2)
        o_par[g] = wsmall[0, yx_, z_].astype(F32)[0:8] + wsmall[0, yx_ + 1, z_].astype(F32)[0:8]
        rate[g] = -8.0 * softplus(o_par[g])
    gsum = [jnp.zeros((8, 128), F32), jnp.zeros((8, 128), F32)]
    for z_ in range(4):
        for yx_ in range(4):
            gsum[0] = gsum[0] + wsmall[0, yx_, z_].astype(F32)[8:16]
            gsum[1] = gsum[1] + wsmall[1, yx_, z_].astype(F32)[0:8]
    o_gain[...] = jnp.zeros_like(o_gain)
    for n in range(2):
        for j in range(width // 128):
            o_gain[n : n + 1, j * 128 : (j + 1) * 128] = gsum[n][j : j + 1]

    @pl.when(me + 1 < count)
    def _():
        halo.wait_send()

    @pl.when(me > 0)
    def _():
        halo.wait_recv()

    def norm_rows(x, n):
        inv = lax.rsqrt(jnp.mean(x * x, axis=1, keepdims=True) + EPSILON)
        return (x * inv * o_gain[n : n + 1, :]).astype(BF16)

    ubuf[0:16, :] = norm_rows(xh[...].astype(F32), 0)

    def norm_one(r0):
        ubuf[pl.ds(r0 + 16, 32), :] = norm_rows(tokens[pl.ds(r0, 32), :].astype(F32), 0)

    rows_loop(rows, 32, norm_one)
    saved_u1 = save(ubuf.at[16 : rows + 16], o_u1)
    g_bx.stage(3)
    g_gate.stage(2)
    g_by.stage(1)
    g_out.stage(0)
    g_bx.stage(4)

    def project_x(h, c):
        cols = pl.ds(pl.multiple_of(lax.rem(h, 2) * 256, 256), 256)
        v = nn(ubuf[...], chips(wbx[lax.div(h, 2), :, :, :, cols])).astype(BF16).astype(F32)
        bx[2 * h], bx[2 * h + 1] = v[:, :128], v[:, 128:]
        return c

    def project_y(h, c):
        cols = pl.ds(pl.multiple_of(lax.rem(h, 2) * 256, 256), 256)
        v = nn(ubuf[16:, :], chips(wby[lax.div(h, 2), :, :, :, cols]))
        by[2 * h], by[2 * h + 1] = v[:, :128], v[:, 128:]
        return c

    lax.fori_loop(0, 4, project_x, 0)
    saved_bx = save(bx, o_bx)
    save(wbx, o_wbx)
    g_gate.stage(3)
    g_by.stage(2)
    g_out.stage(1)
    g_m[0].stage(0)

    def conv(g, r0):
        par = o_par[g]
        v = bx[g, pl.ds(r0 + 8, 72), :]
        off = since[pl.ds(r0, 64), :]
        total = par[4:5] + par[0:1] * v[8:72]
        for k in range(1, 4):
            total = total + par[k : k + 1] * jnp.where(off >= k, v[8 - k : 72 - k], 0.0)
        coded[g, pl.ds(r0, 64), :] = total.astype(BF16)

    blocks_loop(8, rows, 64, conv)
    saved_c = save(coded, o_coded)
    g_gate.stage(4)
    save(wgate, o_wgate)

    def gate_dots(h, c):
        left = lanes(coded, 2 * h, 0, rows)
        v = nn(left, wgate[0, :, h].reshape(256, 256))
        gx[2 * h], gx[2 * h + 1] = v[:, :128], v[:, 128:]
        v = nn(left, wgate[1, :, h].reshape(256, 256))
        ga[2 * h], ga[2 * h + 1] = v[:, :128], v[:, 128:]
        return c

    lax.fori_loop(0, 4, gate_dots, 0)

    g_by.stage(3)
    g_out.stage(2)
    g_m[0].stage(1)
    g_m[1].stage(0)

    def gates(g, r0):
        par = o_par[g]
        at = pl.ds(r0, 64)
        fresh = since[at, :] == 0
        gate_x = jax.nn.sigmoid(gx[g, at, :] + par[5:6])
        gate_a = jax.nn.sigmoid(ga[g, at, :] + par[6:7])
        log_a = gate_a * rate[g, 7:8, :]
        decay = jnp.exp(log_a)
        factor = jnp.where(fresh, 0.0, decay)
        scale = jnp.where(fresh, 1.0, root_of(one_minus_square(2.0 * log_a, decay)))
        gx[g, at, :] = gate_x
        ga[g, at, :] = gate_a
        fac[g, at, :] = factor
        sc[g, at, :] = scale
        dr[g, pl.ds(r0 + 8, 64), :] = scale * gate_x * coded[g, at, :].astype(F32)

    blocks_loop(8, rows, 64, gates)
    saved = [save(gx, o_gx), save(ga, o_ga), save(fac.at[:, 0:rows], o_fac), save(sc, o_sc)]

    g_by.stage(4)
    g_out.stage(3)
    g_m[0].stage(2)
    ends = scan_segments(fac, dr, pq, 0, 8, 0, False)
    _, leave = chain(ends, [jnp.zeros((1, 128), F32)] * 8, False)
    whole = products(ends)
    for g in range(8):
        mine[0, g : g + 1, :] = whole[g]
        mine[1, g : g + 1, :] = leave[g]
    carry_send(p, count, reach, 1, mine, inbox, cs, cr)
    lax.fori_loop(0, 4, project_y, 0)
    save(by, o_by)
    save(wby, o_wby)
    g_m[0].stage(3)
    g_m[1].stage(1)
    g_m[2].stage(0)
    carry_wait(p, count, reach, 1, mine, inbox, cs, cr)
    enter = carry_fold(p, count, reach, 1, inbox)
    inside, _ = chain(ends, enter, False)
    for g in range(8):
        hin[g] = inside[g]
        dr[g, 0:8, :] = jnp.broadcast_to(enter[g], (8, 128))
    step = rows // SEG

    def states(g, c):
        inside_g = hin[g]
        for s in range(SEG):
            lo = s * step
            st = dr[g, lo + 8 : lo + 8 + step, :] + pq[g, lo : lo + step, :] * segment_rows(inside_g, s, step)
            dr[g, lo + 8 : lo + 8 + step, :] = st
            mixed[g, lo : lo + step, :] = (st * gelu(by[g, lo : lo + step, :])).astype(BF16)
        return c

    lax.fori_loop(0, 8, states, 0)
    saved.append(save(dr.at[:, 0 : rows + 8], o_st))
    saved.append(save(mixed, o_mixed))
    g_out.stage(4)
    save(wout, o_wout)
    for c in (saved_bx, saved_u1, saved_c):
        c.wait()
    middle = bx
    v = nt(wide(mixed, 4, 0, rows), chips(wout[0])) + nt(
        jnp.concatenate([mixed[g] for g in range(4, 8)], axis=1), chips(wout[1])
    )

    put(middle, v, 0, 0)

    def norm_two(r0):
        at = pl.ds(r0, 32)
        m = wide(middle, 6, r0, 32) + tokens[at, :].astype(F32)
        for g in range(6):
            middle[g, at, :] = m[:, g * 128 : (g + 1) * 128]
        ubuf[at, :] = norm_rows(m, 1)

    rows_loop(rows, 32, norm_two)
    g_m[0].stage(4)
    g_m[2].stage(1)
    for c in saved:
        c.wait()
    bufs = (m_r0, m_ra, m_rb, None, None, None)
    red = [
        Reduce(p, wm.at[k], wm, (k, p.core), bufs, ((k % 2,),) + tuple((k,) if k < n else None for n in (2, 1, 0, 0, 0)), rs.at[k],
               rr.at[k])
        for k in range(3)
    ]
    fg, fu, fd, acc_out, acc_du = gx, ga, pq, sc, fac
    hid, dgate = coded, mixed

    for k in range(3):
        if k > 0:
            g_m[k].stage(3)
            g_m[k].stage(4)
        w0 = flat(wm[k, 0])
        w1 = flat(wm[k, 1])
        wg, wu, wd = w0[:, :768], jnp.concatenate([w0[:, 768:], w1[:, :384]], axis=1), w1[:, 384:]
        put(fg, nt(ubuf[0:rows, :], wg), 0, 0)
        put(fu, nt(ubuf[0:rows, :], wu), 0, 0)
        put(fd, nt(cot[...], wd), 0, 0)

        def glu(r0):
            at = pl.ds(r0, 32)
            for g in range(6):
                act, slope = gelu_parts(fg[g, at, :])
                up, dh = fu[g, at, :], fd[g, at, :]
                hid[g, at, :] = (act * up).astype(BF16)
                dgate[g, at, :] = (dh * up * slope).astype(BF16)
                dup[g, at, :] = (dh * act).astype(BF16)

        rows_loop(rows, 32, glu)
        if k < 2:
            g_m[k + 1].stage(2)
        if k > 0:
            red[0].stage(k)
        if k == 1:
            pl.semaphore_signal(free, inc=1, device_id=(p.pc,), device_id_type=MESH)
        if k > 1:
            red[1].stage(1)
        v_hid, v_dg, v_dup = (wide(t, 6, 0, rows) for t in (hid, dgate, dup))
        v = nn(v_hid, wd)
        v2 = nn(v_dg, wg) + nn(v_dup, wu)
        for g in range(6):
            cols = slice(g * 128, (g + 1) * 128)
            if k == 0:
                acc_out[g, 0:rows, :] = v[:, cols]
                acc_du[g, 0:rows, :] = v2[:, cols]
            else:
                acc_out[g, 0:rows, :] += v[:, cols]
                acc_du[g, 0:rows, :] += v2[:, cols]
        gg = tn(v_dg, ubuf[0:rows, :]).astype(BF16)
        gu = tn(v_dup, ubuf[0:rows, :]).astype(BF16)
        gd = tn(v_hid, cot[...]).astype(BF16)
        wm[k, 0, :, :, :, 0:768] = gg.reshape(4, 4, 48, 768)
        wm[k, 0, :, :, :, 768:1152] = gu[:, :384].reshape(4, 4, 48, 384)
        wm[k, 1, :, :, :, 0:384] = gu[:, 384:].reshape(4, 4, 48, 384)
        wm[k, 1, :, :, :, 384:1152] = gd.reshape(4, 4, 48, 768)
        if k == 2:
            pl.semaphore_wait(free, 1)
        red[k].stage(0)

    o_gg2[...] = jnp.zeros_like(o_gg2)

    def finish(r0):
        at = pl.ds(r0, 32)
        m, c = wide(middle, 6, r0, 32), cot[at, :].astype(F32)
        out[at, :] = (m + wide(acc_out, 6, r0, 32)).astype(BF16)
        du = wide(acc_du, 6, r0, 32)
        inv = lax.rsqrt(jnp.mean(m * m, axis=1, keepdims=True) + EPSILON)
        o_gg2[...] += fold8(du * m * inv)
        gd_ = du * o_gain[1:2, :]
        back = jnp.mean(gd_ * m, axis=1, keepdims=True)
        dm = c + inv * gd_ - m * (inv * inv * inv * back)
        ubuf[at, :] = dm.astype(BF16)
        for g in range(6):
            acc_out[g, at, :] = dm[:, g * 128 : (g + 1) * 128]

    rows_loop(rows, 32, finish)
    save(acc_out.at[0:6], o_dmid)
    save(ubuf.at[0:rows], o_db)
    red[0].take(2)
    save(wm.at[0, p.core, p.yx], o_part0)
    red[2].take(0)
    save(wm.at[2, p.core], o_part2)
    red[1].take(1)
    save(wm.at[1, p.core, p.yx], o_part1.at[0])
    save(wm.at[1, p.core, p.gb], o_part1.at[1])
    red[0].close(0, 1, 2, 3)
    red[1].close(0, 1, 2)
    red[2].close(0)
    for c in outs:
        if not any(c is s for s in saved + [saved_bx, saved_u1, saved_c]):
            c.wait()


def forward_call(count, reach, args):
    tokens = args[0]
    rows, width = tokens.shape
    S = jax.ShapeDtypeStruct
    page = (8, rows, 128)
    outs = [
        (S((rows, width), BF16), VM),
        (S((8, 8, 128), F32), VM),
        (S((8, width), F32), VM),
        (S((8, width), F32), VM),
        (S((2, 4, 4, 48, 512), BF16), ANY),
        (S((2, 4, 4, 48, 512), BF16), ANY),
        (S((2, 4, 4, 64, 256), BF16), ANY),
        (S((2, 4, 4, 48, 512), BF16), ANY),
        (S(page, F32), ANY),
        (S(page, F32), ANY),
        (S(page, F32), ANY),
        (S(page, F32), ANY),
        (S(page, F32), ANY),
        (S((8, rows + 8, 128), F32), ANY),
        (S((8, rows + 16, 128), F32), ANY),
        (S(page, BF16), ANY),
        (S(page, BF16), ANY),
        (S((rows, width), BF16), ANY),
        (S((6, rows, 128), F32), ANY),
        (S((rows, width), BF16), ANY),
        (S((4, 48, 1152), BF16), ANY),
        (S((2, 4, 48, 1152), BF16), ANY),
        (S((4, 4, 48, 1152), BF16), ANY),
    ]
    V = pltpu.VMEM
    dma = pltpu.SemaphoreType.DMA
    scratch = [
        V((2, 4, 4, 16, 128), BF16),
        V((2, 4, 4, 48, 512), BF16),
        V((2, 4, 4, 48, 512), BF16),
        V((2, 4, 4, 64, 256), BF16),
        V((2, 4, 4, 48, 512), BF16),
        V((3, 2, 4, 4, 48, 1152), BF16),
        V((8, rows + 16, 128), F32),
        V(page, F32),
        V((8, rows + PAD, 128), F32),
        V((8, rows + 8 + PAD, 128), F32),
        V((8, rows + PAD, 128), F32),
        V(page, F32),
        V(page, F32),
        V(page, F32),
        V((rows + 16, width), BF16),
        V(page, BF16),
        V(page, BF16),
        V(page, BF16),
        V((rows, 128), jnp.int32),
        V((8, 8, 128), F32),
        V((16, width), BF16),
        V((32, 128), F32),
        V((32, 128), F32),
        V((2, 2, 24, 512), F32),
        V((2, 24, 512), F32),
        V((2, 24, 512), F32),
        V((24, 512), F32),
        V((2, 32, 256), F32),
        V((32, 256), F32),
        V((2, 72, 1152), F32),
        V((72, 1152), F32),
        V((8, 8, 128), F32),
        V((2, 8, 128), F32),
        V((reach, 2, 8, 128), F32),
        V((2, 4, 4, 48, 1152), BF16),
        V((2, 2, 4, 48, 1152), BF16),
        V((1, 4, 48, 1152), BF16),
        dma((8, 10)),
        dma((8, 10)),
        dma((6,)),
        dma((6,)),
        dma((1,)),
        dma((1,)),
        dma((reach,)),
        dma((reach,)),
        dma((3, 8)),
        dma((3, 8)),
        dma((20,)),
        pltpu.SemaphoreType.REGULAR,
    ]
    return pl.pallas_call(
        functools.partial(forward_kernel, count, reach),
        out_shape=[o[0] for o in outs],
        in_specs=[VM, VM, SM] + [VM] * 11,
        out_specs=[o[1] for o in outs],
        scratch_shapes=scratch,
        name="forward",
        cost_estimate=pl.CostEstimate(flops=25 * 10**9, bytes_accessed=60 * 10**6, transcendentals=10**7),
        compiler_params=pltpu.CompilerParams(
            collective_id=0, has_side_effects=True, vmem_limit_bytes=62 * MIB
        ),
    )(*args)


class Reduce:
    def __init__(self, p, part, whole, own_lead, bufs, leads, ssem, rsem, groups=None):
        self.p, self.part = p, part
        self.whole, self.own_lead, self.bufs, self.leads = whole, own_lead, bufs, leads
        self.ssem, self.rsem = ssem, rsem
        self.gyx, self.gb = groups or (p.yx, p.gb)

    def own(self, *index):
        return self.whole.at[self.own_lead + index]

    def buf(self, which, *index):
        at = self.leads[which] + index
        return self.bufs[which].at[at] if at else self.bufs[which]

    def copy(self, slot):
        p = self.p
        src, dst, dev = (
            (lambda: (self.part.at[p.other], self.buf(0), p.pc)),
            (lambda: (self.own(p.gd), self.buf(1, 1), p.pa)),
            (lambda: (self.own(p.ga), self.buf(1, 0), p.pa)),
            (lambda: (self.own(self.gb), self.buf(2), p.pb)),
            (lambda: (self.own(self.gyx, p.zs[0]), self.buf(3, 0), p.pz[0])),
            (lambda: (self.own(self.gyx, p.zs[1]), self.buf(3, 1), p.pz[1])),
            (lambda: (self.own(self.gyx, p.zs[2]), self.buf(3, 2), p.pz[2])),
            (lambda: (self.buf(4, p.other), self.buf(5), p.pc)),
        )[slot]()
        return remote(src, dst, self.ssem.at[slot], self.rsem.at[slot], dev)

    def add(self, group, which, *index):
        for z in range(4):
            at = self.own_lead + (group, z)
            other = self.bufs[which][self.leads[which] + index + (z,)]
            self.whole[at] = (self.whole[at].astype(F32) + other.astype(F32)).astype(BF16)

    def take(self, n, send=False):
        p = self.p
        if n == 0:
            self.copy(0).wait_recv()
            for group, slot in ((p.gd, 1), (p.ga, 2)):
                self.add(group, 0, group)
                if send:
                    self.copy(slot).start()
            for group in (self.gb, self.gyx):
                self.add(group, 0, group)
        elif n == 1:
            self.copy(1).wait_recv()
            self.add(self.gb, 1, 1)
            if send:
                self.copy(3).start()
            self.copy(2).wait_recv()
            self.add(self.gyx, 1, 0)
        elif n == 2:
            self.copy(3).wait_recv()
            self.add(self.gyx, 2)
            if send:
                self.send(3)
        elif n == 3:
            total = self.whole[self.own_lead + (self.gyx, p.z)].astype(F32)
            for d in range(3):
                self.copy(4 + d).wait_recv()
                total = total + self.bufs[3][self.leads[3] + (d,)].astype(F32)
            half = total.shape[0] // 2
            self.bufs[4][self.leads[4] + (0,)] = total[:half]
            self.bufs[4][self.leads[4] + (1,)] = total[half:]
            if send:
                self.send(4)

    def send(self, n):
        for slot in ((0,), (1, 2), (3,), (4, 5, 6), (7,))[n]:
            self.copy(slot).start()

    def close(self, *slots):
        for s in slots:
            self.copy(s).wait_send()

    def stage(self, n, first=0):
        if n == 0:
            self.send(0)
        elif n < 5:
            self.take(n - 1, True)
        else:
            p = self.p
            self.copy(7).wait_recv()
            mine, theirs = self.bufs[4][self.leads[4] + (p.core,)], self.bufs[5][self.leads[5] + (...,)]
            left = jnp.where(p.core == 0, mine, theirs)
            right = jnp.where(p.core == 0, theirs, mine)
            self.close(*range(first, 8))
            return left, right


class Totals:
    def __init__(self, p, v, bufs, ssem, rsem):
        self.p, self.v, self.bufs, self.ssem, self.rsem = p, v, bufs, ssem, rsem

    def copy(self, slot):
        p = self.p
        dev = ([p.pc, p.pa, p.pb] + p.pz)[slot]
        return remote(self.v.at[min(slot, 3)], self.bufs.at[slot], self.ssem.at[slot], self.rsem.at[slot], dev)

    def stage(self, n):
        if n < 3:
            self.copy(n).start()
        if n == 3:
            for s in (3, 4, 5):
                self.copy(s).start()

    def step(self, n):
        if n < 3:
            self.copy(n).wait_recv()
            self.v[n + 1] = self.v[n] + self.bufs[n]
            return None
        total = self.v[3]
        for s in (3, 4, 5):
            self.copy(s).wait_recv()
            total = total + self.bufs[s]
        for s in range(6):
            self.copy(s).wait_send()
        return total


def backward_kernel(count, reach, *refs):
    (tokens, lengths, par, gain, gg2, i_wbx, i_wby, i_wgate, i_wout, i_by, i_fac, i_gx, i_ga, i_sc, i_st, i_bx, i_coded,
     i_mixed, i_u1, i_dmid, i_db, i_part0, i_part1, i_part2,
     grad_tokens, o_proj, o_out, o_gate, o_in, o_down, o_cw, o_cb, o_gb, o_dec, o_g1, o_g2,
     wbx, wby, wgate, wout, adj, fac, st, pp, gslot, coded, mixed, u1, db, dby, dgx, since,
     own0, own1, own2, gout, gpy, gpx, ggate,
     m_ra, m_rb, m_rz, m_tot, m_rc, p_r0, p_ra, p_rb, p_rz, p_tot, p_rc, t_r0, t_ra, t_rb, t_rz, t_tot, t_rc,
     edge, sums, gsum, vsum, vbuf, hin, mine, inbox,
     rs, rr, vs, vr, cs, cr, es, er, isem, gsem, lsem) = refs
    p = Place()
    me = p.me
    rows, width = tokens.shape

    inbox[...] = jnp.zeros_like(inbox)
    edge[...] = jnp.zeros_like(edge)
    entry_barrier(p, count, reach)

    mbufs = (None, m_ra, m_rb, m_rz, m_tot, m_rc)
    red_m = [
        Reduce(p, None, own, (), mbufs, (None, (), (max(k - 1, 0),), (k,), (k,), (k,)), rs.at[k], rr.at[k], groups)
        for k, own, groups in ((0, own0, (0, None)), (1, own1, (0, 1)), (2, own2, None))
    ]
    pbufs = (p_r0, p_ra, p_rb, p_rz, p_tot, p_rc)
    red_out, red_py, red_px = [
        Reduce(p, g, g, (p.core,), pbufs, ((k,),) * 6, rs.at[3 + k], rr.at[3 + k]) for k, g in enumerate((gout, gpy, gpx))
    ]
    red_gate = Reduce(
        p, ggate, ggate, (p.core,), (t_r0, t_ra, t_rb, t_rz, t_tot, t_rc), ((),) * 6, rs.at[6], rr.at[6]
    )

    parts = [
        pltpu.make_async_copy(i_part0, own0.at[0], lsem.at[0]),
        pltpu.make_async_copy(i_part1, own1, lsem.at[1]),
        pltpu.make_async_copy(i_part2, own2, lsem.at[2]),
    ]
    for c in parts:
        c.start()
    loads = {}
    for i, (name, src, dst) in enumerate((
        ("db", i_db, db), ("wout", i_wout, wout), ("by", i_by, adj.at[:, 0:rows]), ("st", i_st, st), ("mixed", i_mixed, mixed),
        ("u1", i_u1, u1), ("fac", i_fac, fac.at[:, 0:rows]), ("coded", i_coded, coded), ("wgate", i_wgate, wgate),
        ("wby", i_wby, wby), ("wbx", i_wbx, wbx))):
        loads[name] = pltpu.make_async_copy(src, dst, isem.at[i])
        loads[name].start()

    def fetch(g, slot):
        return [
            pltpu.make_async_copy(src.at[g], gslot.at[slot, i, 0:rows], gsem.at[slot, i])
            for i, src in enumerate((i_gx, i_ga, i_sc))
        ]

    def fetch_bx(g, slot):
        return pltpu.make_async_copy(i_bx.at[g], gslot.at[slot, 0], gsem.at[slot, 3])

    for c in fetch(0, 0):
        c.start()
    since[...] = sequence_offset(lengths, me * rows, rows + 8)
    sums[...] = jnp.zeros_like(sums)
    gsum[...] = jnp.zeros_like(gsum)

    parts[0].wait()
    red_m[0].send(3)
    parts[1].wait()
    red_m[1].send(2)
    parts[2].wait()
    red_m[2].send(1)
    loads["db"].wait()
    loads["wout"].wait()

    def mix_dots(h, c):
        cols = pl.ds(pl.multiple_of(lax.rem(h, 2) * 256, 256), 256)
        v = nn(db[...], chips(wout[lax.div(h, 2), :, :, :, cols]))
        pp[2 * h, 0:rows, :], pp[2 * h + 1, 0:rows, :] = v[:, :128], v[:, 128:]
        return c

    lax.fori_loop(0, 4, mix_dots, 0)
    loads["by"].wait()
    loads["st"].wait()

    def branch_y(g, r0):
        at = pl.ds(r0, 64)
        dm = pp[g, at, :]
        act, slope = gelu_parts(adj[g, at, :])
        adj[g, at, :] = dm * act
        dby[g, at, :] = (dm * st[g, pl.ds(r0 + 8, 64), :] * slope).astype(BF16)

    blocks_loop(8, rows, 64, branch_y)
    loads["fac"].wait()
    fac[:, rows:, :] = jnp.ones((8, PAD, 128), F32)
    adj[:, rows:, :] = jnp.zeros((8, PAD, 128), F32)
    ends = scan_segments(fac, adj, pp, 0, 0, 0, True)
    _, leave = chain(ends, [jnp.zeros((1, 128), F32)] * 8, True)
    whole = products(ends)
    for g in range(8):
        mine[0, g : g + 1, :] = whole[g]
        mine[1, g : g + 1, :] = leave[g]
    carry_send(p, count, reach, -1, mine, inbox, cs, cr)
    red_m[1].stage(3)
    loads["mixed"].wait()

    def halves(target, left, page):
        for h in range(2):
            v = tn(left, jnp.concatenate([page[4 * h + i] for i in range(4)], axis=1))
            put_chips(target, h, v.astype(BF16))

    halves(gout, db[...], mixed)
    red_out.stage(0)
    loads["u1"].wait()
    halves(gpy, u1[...], dby)
    red_py.stage(0)
    red_m[0].stage(4)
    red_m[2].stage(2)
    carry_wait(p, count, reach, -1, mine, inbox, cs, cr)
    inside, _ = chain(ends, carry_fold(p, count, reach, -1, inbox), True)
    for g in range(8):
        hin[g] = inside[g]
    step = rows // SEG

    def adjoint(g, c):
        inside_g = hin[g]
        for s in range(SEG):
            lo = s * step
            adj[g, lo : lo + step, :] += pp[g, lo : lo + step, :] * segment_rows(inside_g, s, step)
        return c

    lax.fori_loop(0, 8, adjoint, 0)
    red_out.stage(1)
    red_py.stage(1)
    loads["coded"].wait()
    dga = mixed

    def gate_back(g, slot, last):
        @pl.when(jnp.logical_not(last))
        def _():
            for c_ in fetch(g + 1, 1 - slot):
                c_.start()

        for c_ in fetch(g, slot):
            c_.wait()
        row = par[g]
        sp8 = -8.0 * softplus(row[7:8])

        def block(i, acc):
            r0 = pl.multiple_of(i * 64, 64)
            at = pl.ds(r0, 64)
            a, f = adj[g, at, :], fac[g, at, :]
            gate_x, gate_a, scale = gslot[slot, 0, at, :], gslot[slot, 1, at, :], gslot[slot, 2, at, :]
            code = coded[g, at, :].astype(F32)
            before = st[g, pl.ds(r0, 72), :][7:71]
            d_log = a * f * (before - gate_x * code * f / scale)
            d_a = d_log * gate_a
            d_ga = d_a * sp8 * (1.0 - gate_a)
            d_part = a * scale * gate_x
            d_gx = d_part * code * (1.0 - gate_x)
            dgx[g, at, :] = d_gx.astype(BF16)
            dga[g, at, :] = d_ga.astype(BF16)
            adj[g, at, :] = d_part
            return acc[0] + fold8(d_gx), acc[1] + fold8(d_ga), acc[2] + fold8(d_a)

        zero = jnp.zeros((8, 128), F32)
        acc = lax.fori_loop(0, rows // 64, block, (zero, zero, zero))
        slope = jax.nn.sigmoid(row[7:8])
        sums[g, 5:6, :] = jnp.sum(acc[0], axis=0, keepdims=True)
        sums[g, 6:7, :] = jnp.sum(acc[1], axis=0, keepdims=True)
        sums[g, 7:8, :] = jnp.sum(acc[2], axis=0, keepdims=True) * (-8.0 * slope)

    pairs_loop(gate_back)
    fetch_bx(0, 0).start()
    load_dmid = pltpu.make_async_copy(i_dmid, st.at[0:6, 0:rows], isem.at[11])
    load_dmid.start()
    dbx = dgx
    red_m[2].stage(3)
    red_m[1].stage(4)
    red_out.stage(2)
    loads["wgate"].wait()

    def gate_dots(h, c):
        dx, da, code = lanes(dgx, 2 * h, 0, rows), lanes(dga, 2 * h, 0, rows), lanes(coded, 2 * h, 0, rows)
        v = nt(dx, wgate[0, :, h].reshape(256, 256)) + nt(da, wgate[1, :, h].reshape(256, 256))
        adj[2 * h, 0:rows, :] += v[:, :128]
        adj[2 * h + 1, 0:rows, :] += v[:, 128:]
        ggate[0, :, h] = tn(code, dx).astype(BF16).reshape(4, 64, 256)
        ggate[1, :, h] = tn(code, da).astype(BF16).reshape(4, 64, 256)
        return c

    lax.fori_loop(0, 4, gate_dots, 0)
    red_gate.stage(0)
    edge[0] = adj[:, 0:8, :]
    to_prev = remote(edge.at[0], edge.at[1], es.at[0], er.at[0], me - 1)

    @pl.when(me > 0)
    def _():
        to_prev.start()

    red_py.stage(2)
    loads["wby"].wait()
    put(pp, nt(jnp.concatenate([dby[g] for g in range(8)], axis=1), whole_w(wby)), 0, 0)
    red_out.stage(3)
    red_m[2].stage(4)

    @pl.when(me > 0)
    def _():
        to_prev.wait_send()

    @pl.when(me + 1 < count)
    def _():
        to_prev.wait_recv()

    adj[:, rows : rows + 8, :] = edge[1]

    def conv_back(g, slot, last):
        @pl.when(jnp.logical_not(last))
        def _():
            fetch_bx(g + 1, 1 - slot).start()

        fetch_bx(g, slot).wait()
        row = par[g]

        def block(i, acc):
            r0 = pl.multiple_of(i * 64, 64)
            d = adj[g, pl.ds(r0, 72), :]
            off = since[pl.ds(r0, 72), :]
            b = gslot[slot, 0, pl.ds(r0 + 8, 72), :]
            own, off0 = d[0:64], off[0:64]
            total = row[0:1] * own
            out = [acc[0] + fold8(own * b[8:72])]
            for k in range(1, 4):
                total = total + row[k : k + 1] * jnp.where(off[k : 64 + k] >= k, d[k : 64 + k], 0.0)
                out.append(acc[k] + fold8(own * jnp.where(off0 >= k, b[8 - k : 72 - k], 0.0)))
            out.append(acc[4] + fold8(own))
            dbx[g, pl.ds(r0, 64), :] = total.astype(BF16)
            return tuple(out)

        acc = lax.fori_loop(0, rows // 64, block, tuple(jnp.zeros((8, 128), F32) for _ in range(5)))
        for k in range(5):
            sums[g, k : k + 1, :] = jnp.sum(acc[k], axis=0, keepdims=True)

    pairs_loop(conv_back)
    halves(gpx, u1[...], dbx)
    red_px.stage(0)
    red_gate.stage(1)
    red_py.stage(3)
    loads["wbx"].wait()
    du = nt(jnp.concatenate([dbx[g] for g in range(8)], axis=1), whole_w(wbx))
    for g in range(6):
        pp[g, 0:rows, :] += du[:, g * 128 : (g + 1) * 128]
    red_px.stage(1)
    red_gate.stage(2)
    red_out.stage(4)
    red_py.stage(4)
    load_dmid.wait()

    def finish(r0):
        at = pl.ds(r0, 32)
        x = tokens[at, :].astype(F32)
        d = wide(pp, 6, r0, 32)
        inv = lax.rsqrt(jnp.mean(x * x, axis=1, keepdims=True) + EPSILON)
        gsum[...] += fold8(d * x * inv)
        scaled = d * gain[0:1, :]
        back = jnp.mean(scaled * x, axis=1, keepdims=True)
        grad_tokens[at, :] = (wide(st, 6, r0, 32) + inv * scaled - x * (inv * inv * inv * back)).astype(BF16)

    rows_loop(rows, 32, finish)
    vsum[0] = jnp.zeros((16, 1024), F32)
    for g in range(8):
        vsum[0, 0:8, g * 128 : (g + 1) * 128] = sums[g]
    vsum[0, 8:9, 0:width] = jnp.sum(gsum[...], axis=0, keepdims=True)
    vsum[0, 9:10, 0:width] = jnp.sum(gg2[...], axis=0, keepdims=True)
    tot = Totals(p, vsum, vbuf, vs, vr)
    tot.stage(0)
    red_px.stage(2)
    tot.step(0)
    tot.stage(1)
    red_gate.stage(3)
    tot.step(1)
    tot.stage(2)
    red_px.stage(3)
    tot.step(2)
    tot.stage(3)
    red_gate.stage(4)
    for k in range(3):
        left, right = red_m[k].stage(5, (4, 3, 1)[k])
        lo = 24 * k
        o_in[lo : lo + 24, 0:1152] = left
        o_in[lo : lo + 24, 1152:1536] = right[:, :384]
        o_down[lo : lo + 24, :] = right[:, 384:]
    left, right = red_out.stage(5)
    o_out[:, :512], o_out[:, 512:] = left, right
    left, right = red_py.stage(5)
    o_proj[:, 1024:1536], o_proj[:, 1536:2048] = left, right
    red_px.stage(4)
    left, right = red_gate.stage(5)
    o_gate[:, :256], o_gate[:, 256:] = left, right
    total = tot.step(3)
    chan = pltpu.roll(total[0:8], lax.rem(1024 - 32 * me, 1024), 1)
    o_cw[...] = chan[0:4, 0:32]
    o_cb[...] = chan[4:5, 0:32]
    o_gb[...] = chan[5:7, 0:32]
    o_dec[...] = chan[7:8, 0:32]
    gains = pltpu.roll(total[8:16], lax.rem(1024 - 24 * me, 1024), 1)
    o_g1[...] = gains[0:1, 0:24]
    o_g2[...] = gains[1:2, 0:24]
    left, right = red_px.stage(5)
    o_proj[:, 0:512], o_proj[:, 512:1024] = left, right


def backward_call(count, reach, args):
    tokens = args[0]
    rows, width = tokens.shape
    S = jax.ShapeDtypeStruct
    V = pltpu.VMEM
    dma = pltpu.SemaphoreType.DMA
    page = (8, rows, 128)
    outs = [
        S((rows, width), BF16), S((24, 2048), F32), S((24, 1024), F32), S((32, 512), F32), S((72, 1536), F32),
        S((72, 768), F32), S((4, 32), F32), S((1, 32), F32), S((2, 32), F32), S((1, 32), F32), S((1, 24), F32),
        S((1, 24), F32),
    ]

    def bufs(n, r, c):
        lead = (n,) if n else ()
        return [V(lead + (4, 4, r, c), BF16), V(lead + (2, 4, r, c), BF16), V(lead + (4, r, c), BF16),
                V(lead + (3, r, c), BF16), V(lead + (2, r // 2, c), F32), V(lead + (r // 2, c), F32)]

    scratch = [
        V((2, 4, 4, 48, 512), BF16), V((2, 4, 4, 48, 512), BF16), V((2, 4, 4, 64, 256), BF16), V((2, 4, 4, 48, 512), BF16),
        V((8, rows + PAD, 128), F32),
        V((8, rows + PAD, 128), F32),
        V((8, rows + 8, 128), F32),
        V((8, rows + PAD, 128), F32),
        V((2, 3, rows + 16, 128), F32),
        V(page, BF16), V(page, BF16), V((rows, width), BF16), V((rows, width), BF16),
        V(page, BF16), V(page, BF16),
        V((rows + 8, 128), jnp.int32),
        V((1, 4, 48, 1152), BF16), V((2, 4, 48, 1152), BF16), V((4, 4, 48, 1152), BF16),
        V((2, 4, 4, 48, 512), BF16), V((2, 4, 4, 48, 512), BF16), V((2, 4, 4, 48, 512), BF16),
        V((2, 4, 4, 64, 256), BF16),
        V((2, 4, 48, 1152), BF16), V((2, 4, 48, 1152), BF16), *bufs(3, 48, 1152)[3:], *bufs(3, 48, 512), *bufs(0, 64, 256),
        V((2, 8, 8, 128), F32),
        V((8, 8, 128), F32), V((8, width), F32), V((4, 16, 1024), F32), V((6, 16, 1024), F32),
        V((8, 8, 128), F32), V((2, 8, 128), F32), V((reach, 2, 8, 128), F32),
        dma((7, 8)), dma((7, 8)), dma((6,)), dma((6,)), dma((reach,)), dma((reach,)), dma((1,)), dma((1,)),
        dma((12,)), dma((2, 4)), dma((3,)),
    ]
    return pl.pallas_call(
        functools.partial(backward_kernel, count, reach),
        out_shape=outs,
        in_specs=[VM, SM, VM, VM, VM] + [ANY] * 19,
        out_specs=[VM] * len(outs),
        scratch_shapes=scratch,
        name="backward",
        cost_estimate=pl.CostEstimate(flops=12 * 10**9, bytes_accessed=60 * 10**6, transcendentals=10**7),
        compiler_params=pltpu.CompilerParams(
            collective_id=1, has_side_effects=True, vmem_limit_bytes=63 * MIB
        ),
    )(*args)


def results_kernel(n, *refs):
    for i in range(n):
        refs[n + i][...] = refs[i][...]


def results_call(arrays):
    n = len(arrays)
    return pl.pallas_call(
        functools.partial(results_kernel, n),
        out_shape=[jax.ShapeDtypeStruct(a.shape, a.dtype) for a in arrays],
        in_specs=[VM] * n,
        out_specs=[VM] * n,
        name="results",
        cost_estimate=pl.CostEstimate(flops=0, bytes_accessed=2 * sum(a.size * a.dtype.itemsize for a in arrays), transcendentals=0),
    )(*arrays)


def from_behind(x, axis, by):
    size = lax.axis_size(axis)
    pairs = [(i, i + by) for i in range(size) if 0 <= i + by < size]
    return lax.ppermute(x, axis, pairs)


def prefix(part, axis, combine, identity, reverse):
    count = lax.axis_size(axis)
    place = lax.axis_index(axis)
    ahead = count - 1 - place if reverse else place
    gathered = jax.tree.map(lambda a: lax.all_gather(a, axis), part)
    state = jax.tree.map(lambda a, e: jnp.zeros_like(a) + jnp.asarray(e, a.dtype), part, identity)

    def one(lap, state):
        source = count - 1 - lap if reverse else lap
        return combine(
            state, jax.tree.map(lambda a: lax.dynamic_index_in_dim(a, source, 0, False), gathered)
        )

    return lax.fori_loop(0, ahead, one, state)


def rms_scale(values, gain_row):
    inverse = lax.rsqrt(jnp.mean(values * values, axis=-1, keepdims=True) + EPSILON)
    return values * inverse * gain_row


def combine_steps(earlier, later):
    return (earlier[0] * later[0], later[0] * earlier[1] + later[1])


def smooth_gelu(inputs):
    return jax.nn.gelu(inputs, approximate=True)


def glu_piece(gate_pre, up_value):
    return smooth_gelu(gate_pre) * up_value


def gate_math(gate_pre, bias_rows, decay_vec, coded_rows, fresh_row):
    tok_rows, rnn_width = coded_rows.shape
    block_size = gate_pre.shape[2] // 2
    gate_x = jax.nn.sigmoid(gate_pre[:, :, :block_size].reshape(tok_rows, rnn_width) + bias_rows[0])
    gate_a = jax.nn.sigmoid(gate_pre[:, :, block_size:].reshape(tok_rows, rnn_width) + bias_rows[1])
    log_a = -8.0 * gate_a * jax.nn.softplus(decay_vec)
    factor = jnp.where(fresh_row, 0.0, jnp.exp(log_a))
    scale_term = jnp.where(fresh_row, 1.0, jnp.sqrt(-jnp.expm1(2.0 * log_a)))
    return (factor, scale_term * gate_x * coded_rows)


def per_device(
    tokens,
    cotangent,
    lengths,
    gain_norm1,
    gain_norm2,
    proj_in,
    out_proj,
    gate_blocks,
    conv_weight,
    conv_bias,
    gate_bias,
    decay_param,
    mlp_in,
    mlp_down,
):
    tok_rows, model_width = tokens.shape
    conv_taps = conv_weight.shape[0]
    reach_back = conv_taps - 1
    first_row = lax.axis_index("dp") * tok_rows
    places = first_row + jnp.arange(-reach_back, tok_rows, dtype=jnp.int32)
    bounds = jnp.cumsum(lengths)
    labels = jnp.sum((places[:, None] >= bounds[None, :]).astype(jnp.int32), axis=1)
    labels = jnp.where(places < 0, -1, labels)
    own_label = labels[reach_back:]
    fresh_row = (own_label != labels[reach_back - 1 : reach_back - 1 + tok_rows])[:, None]
    tap_masks = [
        (labels[reach_back - offset : reach_back - offset + tok_rows] == own_label)[:, None].astype(
            jnp.float32
        )
        for offset in range(conv_taps)
    ]
    gathered = (
        lax.all_gather(proj_in, "dp", axis=0, tiled=True),
        lax.all_gather(out_proj, "dp", axis=0, tiled=True),
        lax.all_gather(gate_blocks, "dp", axis=0, tiled=True),
        lax.all_gather(gain_norm1, "dp", axis=0, tiled=True),
        lax.all_gather(gain_norm2, "dp", axis=0, tiled=True),
        lax.all_gather(conv_weight, "dp", axis=1, tiled=True),
        lax.all_gather(conv_bias, "dp", axis=0, tiled=True),
        lax.all_gather(gate_bias, "dp", axis=1, tiled=True),
        lax.all_gather(decay_param, "dp", axis=0, tiled=True),
    )
    w_proj, w_out, w_gates = (gathered[0], gathered[1], gathered[2])
    gain_one = gathered[3].astype(jnp.float32)
    gain_two = gathered[4].astype(jnp.float32)
    w_conv = gathered[5].astype(jnp.float32)
    b_conv = gathered[6].astype(jnp.float32)
    b_gates = gathered[7].astype(jnp.float32)
    w_decay = gathered[8].astype(jnp.float32)
    rnn_width = w_conv.shape[1]
    w_mlp, w_down = (
        lax.all_gather(mlp_in, "dp", axis=0, tiled=True),
        lax.all_gather(mlp_down, "dp", axis=0, tiled=True),
    )
    residual = tokens.astype(jnp.float32)
    normed_one, norm_one_back = jax.vjp(rms_scale, residual, gain_one)
    u_one = normed_one.astype(jnp.bfloat16)
    projected = jnp.dot(u_one, w_proj, preferred_element_type=jnp.float32)
    branch_x = projected[:, :rnn_width].astype(jnp.bfloat16)
    branch_y = projected[:, rnn_width:]
    rim_rows = from_behind(branch_x[tok_rows - reach_back :], "dp", 1)
    padded = jnp.concatenate([rim_rows, branch_x], axis=0)
    conv_sum = jnp.zeros((tok_rows, rnn_width), jnp.float32) + b_conv
    for offset in range(conv_taps):
        conv_sum = (
            conv_sum
            + w_conv[offset]
            * padded[reach_back - offset : reach_back - offset + tok_rows].astype(jnp.float32)
            * tap_masks[offset]
        )
    coded_rows = conv_sum.astype(jnp.bfloat16)
    block_size = w_gates.shape[1] // 2
    head_count = rnn_width // block_size
    blocks_w = w_gates.reshape(head_count, block_size, 2 * block_size)
    coded_heads = coded_rows.reshape(tok_rows, head_count, block_size)
    gate_pre = jnp.einsum("thi,hij->thj", coded_heads, blocks_w, preferred_element_type=jnp.float32)
    gate_fn = functools.partial(gate_math, fresh_row=fresh_row)
    (factor, drive_term), gate_back = jax.vjp(
        gate_fn, gate_pre, b_gates, w_decay, coded_rows.astype(jnp.float32)
    )
    prefix_a, local_h = lax.associative_scan(combine_steps, (factor, drive_term), axis=0)
    unit_pair = (jnp.ones((rnn_width,), jnp.float32), jnp.zeros((rnn_width,), jnp.float32))
    carry_unused, carry_h = prefix(
        (prefix_a[-1], local_h[-1]), "dp", combine_steps, unit_pair, False
    )
    state_rows = local_h + prefix_a * carry_h[None, :]
    y_branch_act, y_back = jax.vjp(smooth_gelu, branch_y)
    mixed_rows = (state_rows * y_branch_act).astype(jnp.bfloat16)
    middle = residual + jnp.einsum(
        "tr,dr->td", mixed_rows, w_out, preferred_element_type=jnp.float32
    )
    normed_two, norm_two_back = jax.vjp(rms_scale, middle, gain_two)
    u_two = normed_two.astype(jnp.bfloat16)
    gate_val = jnp.einsum(
        "td,fd->tf", u_two, w_mlp[:, :model_width], preferred_element_type=jnp.float32
    )
    up_val = jnp.einsum(
        "td,fd->tf", u_two, w_mlp[:, model_width:], preferred_element_type=jnp.float32
    )
    glu_value, glu_back = jax.vjp(glu_piece, gate_val, up_val)
    hidden = glu_value.astype(jnp.bfloat16)
    output = (middle + jnp.dot(hidden, w_down, preferred_element_type=jnp.float32)).astype(
        jnp.bfloat16
    )
    w_proj, w_out, w_gates = (
        lax.all_gather(proj_in, "dp", axis=0, tiled=True),
        lax.all_gather(out_proj, "dp", axis=0, tiled=True),
        lax.all_gather(gate_blocks, "dp", axis=0, tiled=True),
    )
    w_mlp, w_down = (
        lax.all_gather(mlp_in, "dp", axis=0, tiled=True),
        lax.all_gather(mlp_down, "dp", axis=0, tiled=True),
    )
    blocks_w = w_gates.reshape(head_count, block_size, 2 * block_size)
    d_hidden = jnp.einsum("td,fd->tf", cotangent, w_down, preferred_element_type=jnp.float32)
    d_gate_f, d_up_f = glu_back(d_hidden)
    d_gate = d_gate_f.astype(jnp.bfloat16)
    d_up = d_up_f.astype(jnp.bfloat16)
    feed_sum = None
    d_u_two = jnp.einsum(
        "tf,fd->td", d_gate, w_mlp[:, :model_width], preferred_element_type=jnp.float32
    )
    d_u_two = d_u_two + jnp.einsum(
        "tf,fd->td", d_up, w_mlp[:, model_width:], preferred_element_type=jnp.float32
    )
    d_norm_mid, d_gain_two = norm_two_back(d_u_two)
    d_middle = cotangent.astype(jnp.float32) + d_norm_mid
    d_branch = d_middle.astype(jnp.bfloat16)
    d_mixed = jnp.dot(d_branch, w_out, preferred_element_type=jnp.float32)
    d_state = d_mixed * y_branch_act
    d_branch_y = y_back(d_mixed * state_rows)[0].astype(jnp.bfloat16)
    ahead_factor = jnp.concatenate([factor[1:], jnp.ones((1, rnn_width), jnp.float32)], axis=0)
    back_prod, local_g = lax.associative_scan(
        combine_steps, (ahead_factor, d_state), reverse=True, axis=0
    )
    carry_skip, carry_q = prefix(
        (factor[0] * back_prod[0], factor[0] * local_g[0]), "dp", combine_steps, unit_pair, True
    )
    adjoint = local_g + back_prod * carry_q[None, :]
    before = jnp.concatenate([carry_h[None, :], state_rows[:-1]], axis=0)
    d_pre_f, d_shift, d_decay, d_coded_part = gate_back((adjoint * before, adjoint))
    d_pre = d_pre_f.astype(jnp.bfloat16)
    d_coded = d_coded_part + jnp.einsum(
        "thj,hij->thi", d_pre, blocks_w, preferred_element_type=jnp.float32
    ).reshape(tok_rows, rnn_width)
    gate_grad = jnp.einsum(
        "thi,thj->hij", coded_heads, d_pre, preferred_element_type=jnp.float32
    ).reshape(rnn_width, 2 * block_size)
    spread = jnp.zeros((tok_rows + reach_back, rnn_width), jnp.float32)
    tap_grads = []
    for offset in range(conv_taps):
        spread = spread + jnp.pad(
            w_conv[offset] * tap_masks[offset] * d_coded, ((reach_back - offset, offset), (0, 0))
        )
        tap_grads.append(
            jnp.sum(
                d_coded
                * tap_masks[offset]
                * padded[reach_back - offset : reach_back - offset + tok_rows].astype(jnp.float32),
                axis=0,
            )
        )
    d_conv_w = jnp.stack(tap_grads, axis=0)
    d_conv_b = jnp.sum(d_coded, axis=0)
    back_rim = from_behind(spread[:reach_back], "dp", -1)
    d_branch_x = (
        spread[reach_back:] + jnp.pad(back_rim, ((tok_rows - reach_back, 0), (0, 0)))
    ).astype(jnp.bfloat16)
    d_projected = jnp.concatenate([d_branch_x, d_branch_y], axis=1)
    d_u_one = jnp.einsum("tk,dk->td", d_projected, w_proj, preferred_element_type=jnp.float32)
    d_norm_in, d_gain_one = norm_one_back(d_u_one)
    grad_tokens = (d_middle + d_norm_in).astype(jnp.bfloat16)
    part_gate = jnp.einsum("tf,td->fd", d_gate, u_two, preferred_element_type=jnp.float32)
    part_up = jnp.einsum("tf,td->fd", d_up, u_two, preferred_element_type=jnp.float32)
    part_down = jnp.einsum("tf,td->fd", hidden, cotangent, preferred_element_type=jnp.float32)
    feed_sum = lax.psum_scatter(
        jnp.concatenate([part_gate, part_up, part_down], axis=1),
        "dp",
        scatter_dimension=0,
        tiled=True,
    )
    part_proj = jnp.einsum("td,tk->dk", u_one, d_projected, preferred_element_type=jnp.float32)
    part_out = jnp.einsum("td,tr->dr", d_branch, mixed_rows, preferred_element_type=jnp.float32)
    rec_sum = lax.psum_scatter(
        jnp.concatenate([part_proj, part_out], axis=1), "dp", scatter_dimension=0, tiled=True
    )
    channel_sums = (
        lax.psum_scatter(d_gain_one, "dp", scatter_dimension=0, tiled=True),
        lax.psum_scatter(d_gain_two, "dp", scatter_dimension=0, tiled=True),
        lax.psum_scatter(d_conv_w, "dp", scatter_dimension=1, tiled=True),
        lax.psum_scatter(d_conv_b, "dp", scatter_dimension=0, tiled=True),
        lax.psum_scatter(d_shift, "dp", scatter_dimension=1, tiled=True),
        lax.psum_scatter(d_decay, "dp", scatter_dimension=0, tiled=True),
        lax.psum_scatter(gate_grad, "dp", scatter_dimension=0, tiled=True),
    )
    return (
        output,
        grad_tokens,
        channel_sums[0],
        channel_sums[1],
        rec_sum[:, : 2 * rnn_width],
        rec_sum[:, 2 * rnn_width :],
        channel_sums[6],
        channel_sums[2],
        channel_sums[3],
        channel_sums[4],
        channel_sums[5],
        feed_sum[:, : 2 * model_width],
        feed_sum[:, 2 * model_width :],
    )


def kernels_step(
    tokens, cotangent, lengths, gain_norm1, gain_norm2, proj_in, out_proj, gate_blocks, conv_weight, conv_bias, gate_bias,
    decay_param, mlp_in, mlp_down,
):
    count = lax.axis_size("dp")
    rows = tokens.shape[0]
    longest = rows * count // 12
    reach = -(-(longest - 1) // rows)
    (output, par, gain, gg2, wbx, wby, wgate, wout, by, fac, gx, ga, sc, st, bx, coded, mixed, u1, dmid, db, part0, part1,
     part2) = forward_call(
        count, reach,
        (tokens, cotangent, lengths, conv_weight, conv_bias[None], gate_bias, decay_param[None], gain_norm1[None],
         gain_norm2[None], proj_in, out_proj, gate_blocks, mlp_in, mlp_down),
    )
    grads = backward_call(
        count, reach,
        (tokens, lengths, par, gain, gg2, wbx, wby, wgate, wout, by, fac, gx, ga, sc, st, bx, coded, mixed, u1, dmid, db,
         part0, part1, part2),
    )
    (output, grad_tokens, g_proj, g_out, g_gate, g_in, g_down, g_cw, g_cb, g_gb, g_dec, g_n1, g_n2) = results_call(
        [output, *grads]
    )
    return (
        output, grad_tokens, g_n1[0], g_n2[0], g_proj, g_out, g_gate, g_cw, g_cb[0], g_gb, g_dec[0], g_in, g_down,
    )


def fits(mesh):
    return mesh.shape["dp"] == 32


def solution(mesh):
    placed = (
        P("dp", None),
        P("dp", None),
        P(),
        P("dp"),
        P("dp"),
        P("dp", None),
        P("dp", None),
        P("dp", None),
        P(None, "dp"),
        P("dp"),
        P(None, "dp"),
        P("dp"),
        P("dp", None),
        P("dp", None),
    )
    return jax.shard_map(
        kernels_step if fits(mesh) else per_device,
        mesh=mesh,
        in_specs=placed,
        out_specs=(
            P("dp", None),
            P("dp", None),
            P("dp"),
            P("dp"),
            P("dp", None),
            P("dp", None),
            P("dp", None),
            P(None, "dp"),
            P("dp"),
            P(None, "dp"),
            P("dp"),
            P("dp", None),
            P("dp", None),
        ),
        check_vma=False,
    )
```

```python
import functools

import jax
import jax.numpy as jnp
from jax import lax
from jax.experimental import pallas as pl
from jax.experimental.pallas import tpu as pltpu
from jax.sharding import PartitionSpec as P

EPSILON = 1e-06
MESH = pl.DeviceIdType.MESH
F32, BF16 = jnp.float32, jnp.bfloat16
VM = pl.BlockSpec(memory_space=pltpu.VMEM)
ANY = pl.BlockSpec(memory_space=pl.ANY)
SM = pl.BlockSpec(memory_space=pltpu.SMEM)
MIB = 2**20
SEG = 8
STEP = 97
PAD = 8


def nn(a, b):
    return jnp.dot(a, b, preferred_element_type=F32)


def nt(a, b):
    return lax.dot_general(a, b, (((1,), (1,)), ((), ())), preferred_element_type=F32)


def tn(a, b):
    return lax.dot_general(a, b, (((0,), (0,)), ((), ())), preferred_element_type=F32)


class Place:
    def __init__(self):
        me = lax.axis_index("dp")
        self.me = me
        self.core = core = lax.rem(me, 2)
        x = lax.rem(lax.div(me, 2), 2)
        y = lax.rem(lax.div(me, 4), 2)
        self.z = z = lax.div(me, 8)
        self.yx = yx = 2 * y + x
        px, py = me + 2 - 4 * x, me + 4 - 8 * y
        gx, gy = yx + 1 - 2 * x, yx + 2 - 4 * y
        self.pa, self.pb = px + core * (py - px), py + core * (px - py)
        self.ga, self.gb = gx + core * (gy - gx), gy + core * (gx - gy)
        self.gd = 3 - yx
        self.pc = me + 1 - 2 * core
        self.other = 1 - core
        self.zs = [lax.rem(z + d, 4) for d in (1, 2, 3)]
        self.pz = [zz * 8 + lax.rem(me, 8) for zz in self.zs]


def remote(src, dst, ssem, rsem, device):
    return pltpu.make_async_remote_copy(
        src_ref=src, dst_ref=dst, send_sem=ssem, recv_sem=rsem, device_id=(device,), device_id_type=MESH
    )


def entry_barrier(pl_, count, reach):
    me = pl_.me
    bar = pltpu.get_barrier_semaphore()
    for p in [pl_.pc, pl_.pa, pl_.pb] + pl_.pz:
        pl.semaphore_signal(bar, inc=1, device_id=(p,), device_id_type=MESH)
    for d in range(1, reach + 1):

        @pl.when(me >= d)
        def _():
            pl.semaphore_signal(bar, inc=1, device_id=(me - d,), device_id_type=MESH)

        @pl.when(me + d < count)
        def _():
            pl.semaphore_signal(bar, inc=1, device_id=(me + d,), device_id_type=MESH)

    pl.semaphore_wait(bar, 6 + jnp.minimum(me, reach) + jnp.minimum(count - 1 - me, reach))


class Gather:
    def __init__(self, p, buf, ssem, rsem):
        self.p, self.buf, self.ssem, self.rsem = p, buf, ssem, rsem

    def copy(self, slot):
        p = self.p
        if slot < 3:
            src, dev = self.buf.at[p.core, p.yx, p.z], p.pz[slot]
        else:
            group = (p.yx, p.yx, p.ga, p.yx, p.ga, p.gb, p.gd)[slot - 3]
            src, dev = self.buf.at[p.core, group], (p.pa, p.pb, p.pb, p.pc, p.pc, p.pc, p.pc)[slot - 3]
        return remote(src, src, self.ssem.at[slot], self.rsem.at[slot], dev)

    def start(self, *slots):
        for s in slots:
            self.copy(s).start()

    def recv(self, *slots):
        for s in slots:
            self.copy(s).wait_recv()

    def stage(self, n):
        if n == 0:
            self.start(0, 1, 2)
        elif n == 1:
            self.recv(0, 1, 2)
            self.start(3, 4, 6)
        elif n == 2:
            self.recv(3)
            self.start(5, 7)
        elif n == 3:
            self.recv(4)
            self.start(8)
            self.recv(5)
            self.start(9)
        else:
            self.recv(6, 7, 8, 9)
            for s in range(10):
                self.copy(s).wait_send()


def sequence_offset(lengths, first, rows):
    t = first + lax.broadcasted_iota(jnp.int32, (rows, 128), 0)

    def one(i, c):
        bound, start = c
        bound = bound + lengths[i]
        return bound, jnp.where(t >= bound, bound, start)

    _, start = lax.fori_loop(0, lengths.shape[0], one, (jnp.int32(0), jnp.zeros((rows, 128), jnp.int32)))
    return t - start


def one_minus_square(v, root):
    series = 1.0 / 2.0 + v * (1.0 / 6.0 + v * (1.0 / 24.0 + v * (1.0 / 120.0 + v * (1.0 / 720.0))))
    return jnp.where(v > -0.125, -v - v * v * series, 1.0 - root * root)


def root_of(v):
    return v * lax.rsqrt(jnp.maximum(v, 1e-37))


def softplus(v):
    return jnp.maximum(v, 0.0) + jnp.log1p(jnp.exp(-jnp.abs(v)))


GELU_K = 0.7978845608028654


def gelu_parts(v):
    v2 = v * v
    th = jnp.tanh(GELU_K * v * (1.0 + 0.044715 * v2))
    half = 0.5 * (1.0 + th)
    slope = half + 0.5 * v * (1.0 - th * th) * (GELU_K * (1.0 + 3.0 * 0.044715 * v2))
    return v * half, slope


def gelu(v):
    return v * (0.5 * (1.0 + jnp.tanh(GELU_K * v * (1.0 + 0.044715 * (v * v)))))


def flat(v):
    return v.reshape(v.shape[0] * v.shape[1] * v.shape[2], v.shape[3])


def chips(v):
    return jnp.concatenate([v[yx, z] for z in range(4) for yx in range(4)], axis=0)


def whole_w(w):
    return jnp.concatenate([chips(w[0]), chips(w[1])], axis=1)


def put_chips(part, half, v):
    rows = v.shape[0] // 16
    for z in range(4):
        for yx in range(4):
            part[half, yx, z] = v[(4 * z + yx) * rows : (4 * z + yx + 1) * rows]


def put(page, v, row, group):
    for i in range(v.shape[1] // 128):
        page[group + i, row : row + v.shape[0], :] = v[:, i * 128 : (i + 1) * 128]


def rows_loop(total, block, body):
    def one(i, c):
        body(pl.multiple_of(i * block, block))
        return c

    lax.fori_loop(0, total // block, one, 0)


def blocks_loop(groups, total, block, body):
    n = total // block

    def one(i, c):
        body(lax.div(i, n), pl.multiple_of(lax.rem(i, n) * block, block))
        return c

    lax.fori_loop(0, groups * n, one, 0)


SLOTS = 4


def slots_loop(body):
    def one(i, c):
        for slot in range(SLOTS):
            body(SLOTS * i + slot, slot, False if slot == 0 else i == 8 // SLOTS - 1)
        return c

    lax.fori_loop(0, 8 // SLOTS, one, 0)


def scan_segments(factor, value, product, factor_row, value_row, product_row, reverse):
    def one(i, c):
        j = STEP - 1 - i if reverse else i
        out = []
        for g in range(8):
            h, q = c[g]
            a = factor[g, pl.ds(factor_row + j, SEG, stride=STEP), :]
            b = value[g, pl.ds(value_row + j, SEG, stride=STEP), :]
            if reverse:
                h = b + h
                value[g, pl.ds(value_row + j, SEG, stride=STEP), :] = h
                product[g, pl.ds(product_row + j, SEG, stride=STEP), :] = q
                h, q = a * h, a * q
            else:
                h, q = a * h + b, a * q
                value[g, pl.ds(value_row + j, SEG, stride=STEP), :] = h
                product[g, pl.ds(product_row + j, SEG, stride=STEP), :] = q
            out.append((h, q))
        return tuple(out)

    first = tuple((jnp.zeros((SEG, 128), F32), jnp.ones((SEG, 128), F32)) for _ in range(8))
    return lax.fori_loop(0, STEP, one, first)


def segment_rows(inside, i, block):
    rest = inside[i : i + 1, :]
    first = jnp.broadcast_to(rest, (8, 128))
    if i:
        spot = lax.broadcasted_iota(jnp.int32, (8, 128), 0)
        first = jnp.where(spot < i, inside[i - 1 : i, :], first)
    return jnp.concatenate([first, jnp.broadcast_to(rest, (block - 8, 128))], axis=0)


def chain(ends, enter, reverse):
    order = range(SEG - 1, -1, -1) if reverse else range(SEG)
    inside, leave = [], []
    for g in range(8):
        h, q = ends[g]
        v = enter[g]
        rows = [None] * SEG
        for s in order:
            rows[s] = v
            v = q[s : s + 1, :] * v + h[s : s + 1, :]
        inside.append(jnp.concatenate(rows, axis=0))
        leave.append(v)
    return inside, leave


def products(ends):
    out = []
    for g in range(8):
        q = ends[g][1]
        v = q[0:1, :]
        for s in range(1, SEG):
            v = v * q[s : s + 1, :]
        out.append(v)
    return out


def carry_send(p, count, reach, sign, mine, inbox, ssem, rsem):
    for d in range(1, reach + 1):

        @pl.when((p.me + d < count) if sign > 0 else (p.me >= d))
        def _(d=d):
            remote(mine, inbox.at[d - 1], ssem.at[d - 1], rsem.at[d - 1], p.me + sign * d).start()


def carry_wait(p, count, reach, sign, mine, inbox, ssem, rsem):
    for d in range(1, reach + 1):
        there = remote(mine, inbox.at[d - 1], ssem.at[d - 1], rsem.at[d - 1], p.me + sign * d)

        @pl.when((p.me + d < count) if sign > 0 else (p.me >= d))
        def _(there=there):
            there.wait_send()

        @pl.when((p.me >= d) if sign > 0 else (p.me + d < count))
        def _(there=there):
            there.wait_recv()


def carry_fold(p, count, reach, sign, inbox):
    v = [jnp.zeros((1, 128), F32) for _ in range(8)]
    for d in range(reach, 0, -1):
        for g in range(8):
            v[g] = inbox[d - 1, 0, g : g + 1, :] * v[g] + inbox[d - 1, 1, g : g + 1, :]
    return v


def lanes(page, group, row, rows):
    return jnp.concatenate([page[group, pl.ds(row, rows), :], page[group + 1, pl.ds(row, rows), :]], axis=1)


def wide(page, groups, row, rows):
    return jnp.concatenate([page[g, pl.ds(row, rows), :] for g in range(groups)], axis=1)


def fold8(v):
    return jnp.sum(v.reshape(v.shape[0] // 8, 8, v.shape[1]), axis=0)


SMALL, BX, GATE, BY, OUT, M0, M1, M2, SUM0, SUM1, SUM2, TOT = range(0, 120, 10)

FORWARD_ORDER = (
    (SMALL + 0, GATE + 0),
    (
        SMALL + 1, OUT + 0, SMALL + 2, GATE + 1, BX + 0, OUT + 1, BY + 0, BX + 1, SMALL + 3, SMALL + 4, M0 + 0,
        M1 + 0, BY + 1, OUT + 2,
    ),
    (GATE + 2, BX + 2, OUT + 3, BY + 2, GATE + 3, M0 + 1, BX + 3, BX + 4),
    (),
    (GATE + 4, OUT + 4),
    (M1 + 1, BY + 3),
    (BY + 4, M0 + 2, M2 + 0),
    (),
    (M1 + 2,),
    (M2 + 1, M0 + 3, M0 + 4),
    (),
    (M1 + 3,),
    (M2 + 2, M1 + 4, SUM0 + 0),
    (SUM0 + 1,),
    (M2 + 3,),
    (M2 + 4, SUM1 + 0),
    (SUM1 + 1,),
    (),
    (SUM2 + 0,),
)


def forward_kernel(count, reach, *refs):
    (tokens, cot, lengths, cw, cb, gb, dec, g1, g2, w_proj, w_out, w_gate, w_in, w_down,
     out, o_par, o_gain, o_gg2, o_wbx, o_wby, o_wgate, o_wout, o_by, o_fac, o_gx, o_ga, o_sc, o_st, o_bx, o_coded,
     o_mixed, o_u1, o_dmid, o_db, o_part01, o_part2,
     wsmall, wbx, wby, wgate, wout, wm, bx, by, fac, dr, pq, gx, ga, sc, ubuf, coded, mixed, dup,
     since, rate, xh, ssmall, rsmall, sproj, rproj, sout, rout, sgate, rgate, smlp, rmlp, hin, mine, inbox, m_r0, m_ra,
     gs, gr, ps, pr, hs, hr, cs, cr, rs, rr, osem, free) = refs
    p = Place()
    me = p.me
    rows, width = tokens.shape
    core0 = p.core == 0

    xh[...] = jnp.zeros_like(xh)
    inbox[...] = jnp.zeros_like(inbox)
    fac[:, rows:, :] = jnp.ones((8, PAD, 128), F32)
    dr[:, rows + 8 :, :] = jnp.zeros((8, PAD, 128), F32)
    entry_barrier(p, count, reach)

    halo = remote(tokens.at[rows - 16 : rows], xh, hs.at[0], hr.at[0], me + 1)

    @pl.when(me + 1 < count)
    def _():
        halo.start()

    lane = lax.broadcasted_iota(jnp.int32, (32, 128), 1)
    row = lax.broadcasted_iota(jnp.int32, (32, 128), 0)
    spot = jnp.where(lane == lax.rem(me, 4) * 32 + row, 1.0, 0.0).astype(BF16)
    gcol = lax.broadcasted_iota(jnp.int32, (24, width), 1)
    grow = lax.broadcasted_iota(jnp.int32, (24, width), 0)
    gspot = jnp.where(gcol == me * 24 + grow, 1.0, 0.0).astype(BF16)
    ssmall[...] = jnp.zeros_like(ssmall)
    ssmall[0:4, :] = nn(cw[...], spot)
    ssmall[4:5, :] = nn(cb[...], spot)
    ssmall[5:7, :] = nn(gb[...], spot)
    ssmall[7:8, :] = nn(dec[...], spot)
    r1, r2 = nn(g1[...], gspot), nn(g2[...], gspot)
    for j in range(width // 128):
        ssmall[8 + j : 9 + j, :] = r1[:, j * 128 : (j + 1) * 128]
        ssmall[16 + j : 17 + j, :] = r2[:, j * 128 : (j + 1) * 128]
    trades = [
        remote(ssmall, rsmall, ps.at[0], pr.at[0], p.pc),
        remote(sproj.at[0, p.other], rproj.at[0], ps.at[1], pr.at[1], p.pc),
        remote(sgate.at[p.other], rgate, ps.at[2], pr.at[2], p.pc),
        remote(sproj.at[1, p.other], rproj.at[1], ps.at[3], pr.at[3], p.pc),
        remote(sout.at[p.other], rout, ps.at[4], pr.at[4], p.pc),
        remote(smlp.at[p.other], rmlp, ps.at[5], pr.at[5], p.pc),
    ]
    trades[0].start()
    for n in range(2):
        for h in range(2):
            lo = n * 1024 + h * 512
            sproj[n, h] = w_proj[:, lo : lo + 512].astype(F32)
        if n == 0:
            trades[1].start()
    for h in range(2):
        sgate[h] = w_gate[:, h * 256 : (h + 1) * 256].astype(F32)
        sout[h] = w_out[:, h * 512 : (h + 1) * 512].astype(F32)
    trades[2].start()
    trades[3].start()
    trades[4].start()
    smlp[0] = w_in[:, :1152].astype(F32)
    smlp[1] = jnp.concatenate([w_in[:, 1152:], w_down[...]], axis=1).astype(F32)
    trades[5].start()

    moves = {
        name: Gather(p, w, gs.at[i], gr.at[i])
        for i, (name, w) in enumerate((
            (SMALL, wsmall), (BX, wbx), (GATE, wgate), (BY, wby), (OUT, wout), (M0, wm.at[0]), (M1, wm.at[1]),
            (M2, wm.at[2])))
    }
    bufs = (m_r0, m_ra, None, None, None, None)
    red = [
        Reduce(p, wm.at[k], wm, (k, p.core), bufs, ((k % 2,),) + tuple((k,) if k < n else None for n in (2, 0, 0, 0, 0)),
               rs.at[k], rr.at[k])
        for k in range(3)
    ]

    moves.update({SUM0: red[0], SUM1: red[1], SUM2: red[2]})
    points = iter(FORWARD_ORDER)

    def at_point():
        for step in next(points):
            if step == SUM2:
                pl.semaphore_wait(free, 1)
            moves[step // 10 * 10].stage(step % 10)
            if step == SUM0 + 1:
                pl.semaphore_signal(free, inc=1, device_id=(p.pc,), device_id_type=MESH)

    def slab(mine_, theirs):
        first = jnp.where(core0, mine_, theirs)
        second = jnp.where(core0, theirs, mine_)
        return jnp.concatenate([first, second], axis=0).astype(BF16)

    trades[0].wait_recv()
    both = ssmall[...] + rsmall[...]
    wsmall[p.core, p.yx, p.z] = jnp.where(core0, both[0:16], both[16:32]).astype(BF16)
    trades[1].wait_recv()
    wbx[p.core, p.yx, p.z] = slab(sproj[0, p.core], rproj[0])
    trades[2].wait_recv()
    wgate[p.core, p.yx, p.z] = slab(sgate[p.core], rgate[...])
    trades[3].wait_recv()
    wby[p.core, p.yx, p.z] = slab(sproj[1, p.core], rproj[1])
    trades[4].wait_recv()
    wout[p.core, p.yx, p.z] = slab(sout[p.core], rout[...])
    trades[5].wait_recv()
    for k in range(3):
        wm[k, p.core, p.yx, p.z] = slab(smlp[p.core, 24 * k : 24 * k + 24, :], rmlp[24 * k : 24 * k + 24, :])

    at_point()
    outs = []

    def save(src, dst):
        c = pltpu.make_async_copy(src, dst, osem.at[len(outs)])
        c.start()
        outs.append(c)
        return c

    since[...] = sequence_offset(lengths, me * rows, rows)
    at_point()
    for t in trades:
        t.wait_send()

    for g in range(8):
        z_, yx_ = g // 2, 2 * (g % 2)
        o_par[g] = wsmall[0, yx_, z_].astype(F32)[0:8] + wsmall[0, yx_ + 1, z_].astype(F32)[0:8]
        rate[g] = -8.0 * softplus(o_par[g])
    gsum = [jnp.zeros((8, 128), F32), jnp.zeros((8, 128), F32)]
    for z_ in range(4):
        for yx_ in range(4):
            gsum[0] = gsum[0] + wsmall[0, yx_, z_].astype(F32)[8:16]
            gsum[1] = gsum[1] + wsmall[1, yx_, z_].astype(F32)[0:8]
    o_gain[...] = jnp.zeros_like(o_gain)
    for n in range(2):
        for j in range(width // 128):
            o_gain[n : n + 1, j * 128 : (j + 1) * 128] = gsum[n][j : j + 1]

    @pl.when(me + 1 < count)
    def _():
        halo.wait_send()

    @pl.when(me > 0)
    def _():
        halo.wait_recv()

    def norm_rows(x, n):
        inv = lax.rsqrt(jnp.mean(x * x, axis=1, keepdims=True) + EPSILON)
        return (x * inv * o_gain[n : n + 1, :]).astype(BF16)

    ubuf[0:16, :] = norm_rows(xh[...].astype(F32), 0)

    def norm_one(r0):
        ubuf[pl.ds(r0 + 16, 32), :] = norm_rows(tokens[pl.ds(r0, 32), :].astype(F32), 0)

    rows_loop(rows, 32, norm_one)
    saved_u1 = save(ubuf.at[16 : rows + 16], o_u1)
    at_point()

    def project_x(h, c):
        cols = pl.ds(pl.multiple_of(lax.rem(h, 2) * 256, 256), 256)
        v = nn(ubuf[...], chips(wbx[lax.div(h, 2), :, :, :, cols])).astype(BF16).astype(F32)
        bx[2 * h], bx[2 * h + 1] = v[:, :128], v[:, 128:]
        return c

    def project_y(h, c):
        cols = pl.ds(pl.multiple_of(lax.rem(h, 2) * 256, 256), 256)
        v = nn(ubuf[16:, :], chips(wby[lax.div(h, 2), :, :, :, cols]))
        by[2 * h], by[2 * h + 1] = v[:, :128], v[:, 128:]
        return c

    lax.fori_loop(0, 4, project_x, 0)
    saved_bx = save(bx, o_bx)
    save(wbx, o_wbx)
    at_point()

    def conv(g, r0):
        par = o_par[g]
        v = bx[g, pl.ds(r0 + 8, 72), :]
        off = since[pl.ds(r0, 64), :]
        total = par[4:5] + par[0:1] * v[8:72]
        for k in range(1, 4):
            total = total + par[k : k + 1] * jnp.where(off >= k, v[8 - k : 72 - k], 0.0)
        coded[g, pl.ds(r0, 64), :] = total.astype(BF16)

    blocks_loop(8, rows, 64, conv)
    saved_c = save(coded, o_coded)
    at_point()
    save(wgate, o_wgate)

    def gate_dots(h, c):
        left = lanes(coded, 2 * h, 0, rows)
        v = nn(left, wgate[0, :, h].reshape(256, 256))
        gx[2 * h], gx[2 * h + 1] = v[:, :128], v[:, 128:]
        v = nn(left, wgate[1, :, h].reshape(256, 256))
        ga[2 * h], ga[2 * h + 1] = v[:, :128], v[:, 128:]
        return c

    lax.fori_loop(0, 4, gate_dots, 0)
    at_point()

    def gates(g, r0):
        par = o_par[g]
        at = pl.ds(r0, 64)
        fresh = since[at, :] == 0
        gate_x = jax.nn.sigmoid(gx[g, at, :] + par[5:6])
        gate_a = jax.nn.sigmoid(ga[g, at, :] + par[6:7])
        log_a = gate_a * rate[g, 7:8, :]
        decay = jnp.exp(log_a)
        factor = jnp.where(fresh, 0.0, decay)
        scale = jnp.where(fresh, 1.0, root_of(one_minus_square(2.0 * log_a, decay)))
        gx[g, at, :] = gate_x
        ga[g, at, :] = gate_a
        fac[g, at, :] = factor
        sc[g, at, :] = scale
        dr[g, pl.ds(r0 + 8, 64), :] = scale * gate_x * coded[g, at, :].astype(F32)

    blocks_loop(8, rows, 64, gates)
    saved = [save(gx, o_gx), save(ga, o_ga), save(fac.at[:, 0:rows], o_fac), save(sc, o_sc)]
    at_point()
    ends = scan_segments(fac, dr, pq, 0, 8, 0, False)
    _, leave = chain(ends, [jnp.zeros((1, 128), F32)] * 8, False)
    whole = products(ends)
    for g in range(8):
        mine[0, g : g + 1, :] = whole[g]
        mine[1, g : g + 1, :] = leave[g]
    carry_send(p, count, reach, 1, mine, inbox, cs, cr)
    lax.fori_loop(0, 4, project_y, 0)
    save(by, o_by)
    save(wby, o_wby)
    at_point()
    carry_wait(p, count, reach, 1, mine, inbox, cs, cr)
    enter = carry_fold(p, count, reach, 1, inbox)
    inside, _ = chain(ends, enter, False)
    for g in range(8):
        hin[g] = inside[g]
        dr[g, 0:8, :] = jnp.broadcast_to(enter[g], (8, 128))
    step = rows // SEG

    def states(g, c):
        inside_g = hin[g]
        for s in range(SEG):
            lo = s * step
            st = dr[g, lo + 8 : lo + 8 + step, :] + pq[g, lo : lo + step, :] * segment_rows(inside_g, s, step)
            dr[g, lo + 8 : lo + 8 + step, :] = st
            mixed[g, lo : lo + step, :] = (st * gelu(by[g, lo : lo + step, :])).astype(BF16)
        return c

    lax.fori_loop(0, 8, states, 0)
    saved.append(save(dr.at[:, 0 : rows + 8], o_st))
    saved.append(save(mixed, o_mixed))
    at_point()
    save(wout, o_wout)
    for c in (saved_bx, saved_u1, saved_c):
        c.wait()
    middle = bx
    v = nt(wide(mixed, 4, 0, rows), chips(wout[0])) + nt(
        jnp.concatenate([mixed[g] for g in range(4, 8)], axis=1), chips(wout[1])
    )

    put(middle, v, 0, 0)

    def norm_two(r0):
        at = pl.ds(r0, 32)
        m = wide(middle, 6, r0, 32) + tokens[at, :].astype(F32)
        for g in range(6):
            middle[g, at, :] = m[:, g * 128 : (g + 1) * 128]
        ubuf[at, :] = norm_rows(m, 1)

    rows_loop(rows, 32, norm_two)
    at_point()
    for c in saved:
        c.wait()
    fg, fu, fd, acc_out, acc_du = gx, ga, pq, sc, fac
    hid, dgate = coded, mixed

    for k in range(3):
        w0 = flat(wm[k, 0])
        w1 = flat(wm[k, 1])
        wg, wu, wd = w0[:, :768], jnp.concatenate([w0[:, 768:], w1[:, :384]], axis=1), w1[:, 384:]
        put(fg, nt(ubuf[0:rows, :], wg), 0, 0)
        put(fu, nt(ubuf[0:rows, :], wu), 0, 0)
        put(fd, nt(cot[...], wd), 0, 0)

        def glu(r0):
            at = pl.ds(r0, 32)
            for g in range(6):
                act, slope = gelu_parts(fg[g, at, :])
                up, dh = fu[g, at, :], fd[g, at, :]
                hid[g, at, :] = (act * up).astype(BF16)
                dgate[g, at, :] = (dh * up * slope).astype(BF16)
                dup[g, at, :] = (dh * act).astype(BF16)

        rows_loop(rows, 32, glu)
        at_point()
        v_hid, v_dg, v_dup = (wide(t, 6, 0, rows) for t in (hid, dgate, dup))
        v = nn(v_hid, wd)
        v2 = nn(v_dg, wg) + nn(v_dup, wu)
        for g in range(6):
            cols = slice(g * 128, (g + 1) * 128)
            if k == 0:
                acc_out[g, 0:rows, :] = v[:, cols]
                acc_du[g, 0:rows, :] = v2[:, cols]
            else:
                acc_out[g, 0:rows, :] += v[:, cols]
                acc_du[g, 0:rows, :] += v2[:, cols]
        at_point()
        gg = tn(v_dg, ubuf[0:rows, :]).astype(BF16)
        gu = tn(v_dup, ubuf[0:rows, :]).astype(BF16)
        gd = tn(v_hid, cot[...]).astype(BF16)
        wm[k, 0, :, :, :, 0:768] = gg.reshape(4, 4, 48, 768)
        wm[k, 0, :, :, :, 768:1152] = gu[:, :384].reshape(4, 4, 48, 384)
        wm[k, 1, :, :, :, 0:384] = gu[:, 384:].reshape(4, 4, 48, 384)
        wm[k, 1, :, :, :, 384:1152] = gd.reshape(4, 4, 48, 768)
        at_point()

    o_gg2[...] = jnp.zeros_like(o_gg2)

    def finish(r0):
        at = pl.ds(r0, 32)
        m, c = wide(middle, 6, r0, 32), cot[at, :].astype(F32)
        out[at, :] = (m + wide(acc_out, 6, r0, 32)).astype(BF16)
        du = wide(acc_du, 6, r0, 32)
        inv = lax.rsqrt(jnp.mean(m * m, axis=1, keepdims=True) + EPSILON)
        o_gg2[...] += fold8(du * m * inv)
        gd_ = du * o_gain[1:2, :]
        back = jnp.mean(gd_ * m, axis=1, keepdims=True)
        dm = c + inv * gd_ - m * (inv * inv * inv * back)
        ubuf[at, :] = dm.astype(BF16)
        for g in range(6):
            acc_out[g, at, :] = dm[:, g * 128 : (g + 1) * 128]

    rows_loop(rows, 32, finish)
    save(acc_out.at[0:6], o_dmid)
    save(ubuf.at[0:rows], o_db)
    for k in range(2):
        red[k].take(1)
        save(wm.at[k, p.core, p.yx], o_part01.at[k, 0])
        save(wm.at[k, p.core, p.gb], o_part01.at[k, 1])
    red[2].take(0)
    save(wm.at[2, p.core], o_part2)
    red[0].close(0, 1, 2)
    red[1].close(0, 1, 2)
    red[2].close(0)
    for c in outs:
        if not any(c is s for s in saved + [saved_bx, saved_u1, saved_c]):
            c.wait()


def forward_call(count, reach, args):
    tokens = args[0]
    rows, width = tokens.shape
    S = jax.ShapeDtypeStruct
    page = (8, rows, 128)
    outs = [
        (S((rows, width), BF16), VM),
        (S((8, 8, 128), F32), VM),
        (S((8, width), F32), VM),
        (S((8, width), F32), VM),
        (S((2, 4, 4, 48, 512), BF16), ANY),
        (S((2, 4, 4, 48, 512), BF16), ANY),
        (S((2, 4, 4, 64, 256), BF16), ANY),
        (S((2, 4, 4, 48, 512), BF16), ANY),
        (S(page, F32), ANY),
        (S(page, F32), ANY),
        (S(page, F32), ANY),
        (S(page, F32), ANY),
        (S(page, F32), ANY),
        (S((8, rows + 8, 128), F32), ANY),
        (S((8, rows + 16, 128), F32), ANY),
        (S(page, BF16), ANY),
        (S(page, BF16), ANY),
        (S((rows, width), BF16), ANY),
        (S((6, rows, 128), F32), ANY),
        (S((rows, width), BF16), ANY),
        (S((2, 2, 4, 48, 1152), BF16), ANY),
        (S((4, 4, 48, 1152), BF16), ANY),
    ]
    V = pltpu.VMEM
    dma = pltpu.SemaphoreType.DMA
    scratch = [
        V((2, 4, 4, 16, 128), BF16),
        V((2, 4, 4, 48, 512), BF16),
        V((2, 4, 4, 48, 512), BF16),
        V((2, 4, 4, 64, 256), BF16),
        V((2, 4, 4, 48, 512), BF16),
        V((3, 2, 4, 4, 48, 1152), BF16),
        V((8, rows + 16, 128), F32),
        V(page, F32),
        V((8, rows + PAD, 128), F32),
        V((8, rows + 8 + PAD, 128), F32),
        V((8, rows + PAD, 128), F32),
        V(page, F32),
        V(page, F32),
        V(page, F32),
        V((rows + 16, width), BF16),
        V(page, BF16),
        V(page, BF16),
        V(page, BF16),
        V((rows, 128), jnp.int32),
        V((8, 8, 128), F32),
        V((16, width), BF16),
        V((32, 128), F32),
        V((32, 128), F32),
        V((2, 2, 24, 512), F32),
        V((2, 24, 512), F32),
        V((2, 24, 512), F32),
        V((24, 512), F32),
        V((2, 32, 256), F32),
        V((32, 256), F32),
        V((2, 72, 1152), F32),
        V((72, 1152), F32),
        V((8, 8, 128), F32),
        V((2, 8, 128), F32),
        V((reach, 2, 8, 128), F32),
        V((2, 4, 4, 48, 1152), BF16),
        V((2, 2, 4, 48, 1152), BF16),
        dma((8, 10)),
        dma((8, 10)),
        dma((6,)),
        dma((6,)),
        dma((1,)),
        dma((1,)),
        dma((reach,)),
        dma((reach,)),
        dma((3, 8)),
        dma((3, 8)),
        dma((24,)),
        pltpu.SemaphoreType.REGULAR,
    ]
    return pl.pallas_call(
        functools.partial(forward_kernel, count, reach),
        out_shape=[o[0] for o in outs],
        in_specs=[VM, VM, SM] + [VM] * 11,
        out_specs=[o[1] for o in outs],
        scratch_shapes=scratch,
        name="forward",
        cost_estimate=pl.CostEstimate(flops=25 * 10**9, bytes_accessed=60 * 10**6, transcendentals=10**7),
        compiler_params=pltpu.CompilerParams(
            collective_id=0, has_side_effects=True, vmem_limit_bytes=62 * MIB
        ),
    )(*args)


class Reduce:
    def __init__(self, p, part, whole, own_lead, bufs, leads, ssem, rsem, groups=None):
        self.p, self.part = p, part
        self.whole, self.own_lead, self.bufs, self.leads = whole, own_lead, bufs, leads
        self.ssem, self.rsem = ssem, rsem
        self.gyx, self.gb = groups or (p.yx, p.gb)

    def own(self, *index):
        return self.whole.at[self.own_lead + index]

    def buf(self, which, *index):
        at = self.leads[which] + index
        return self.bufs[which].at[at] if at else self.bufs[which]

    def copy(self, slot):
        p = self.p
        src, dst, dev = (
            (lambda: (self.part.at[p.other], self.buf(0), p.pc)),
            (lambda: (self.own(p.gd), self.buf(1, 1), p.pa)),
            (lambda: (self.own(p.ga), self.buf(1, 0), p.pa)),
            (lambda: (self.own(self.gb), self.buf(2), p.pb)),
            (lambda: (self.own(self.gyx, p.zs[0]), self.buf(3, 0), p.pz[0])),
            (lambda: (self.own(self.gyx, p.zs[1]), self.buf(3, 1), p.pz[1])),
            (lambda: (self.own(self.gyx, p.zs[2]), self.buf(3, 2), p.pz[2])),
            (lambda: (self.buf(4, p.other), self.buf(5), p.pc)),
        )[slot]()
        return remote(src, dst, self.ssem.at[slot], self.rsem.at[slot], dev)

    def add(self, group, which, *index):
        for z in range(4):
            at = self.own_lead + (group, z)
            other = self.bufs[which][self.leads[which] + index + (z,)]
            self.whole[at] = (self.whole[at].astype(F32) + other.astype(F32)).astype(BF16)

    def take(self, n, send=False):
        p = self.p
        if n == 0:
            self.copy(0).wait_recv()
            for group, slot in ((p.gd, 1), (p.ga, 2)):
                self.add(group, 0, group)
                if send:
                    self.copy(slot).start()
            for group in (self.gb, self.gyx):
                self.add(group, 0, group)
        elif n == 1:
            self.copy(1).wait_recv()
            self.add(self.gb, 1, 1)
            if send:
                self.copy(3).start()
            self.copy(2).wait_recv()
            self.add(self.gyx, 1, 0)
        elif n == 2:
            self.copy(3).wait_recv()
            self.add(self.gyx, 2)
            if send:
                self.send(3)
        elif n == 3:
            total = self.whole[self.own_lead + (self.gyx, p.z)].astype(F32)
            for d in range(3):
                self.copy(4 + d).wait_recv()
                total = total + self.bufs[3][self.leads[3] + (d,)].astype(F32)
            half = total.shape[0] // 2
            self.bufs[4][self.leads[4] + (0,)] = total[:half]
            self.bufs[4][self.leads[4] + (1,)] = total[half:]
            if send:
                self.send(4)

    def send(self, n):
        for slot in ((0,), (1, 2), (3,), (4, 5, 6), (7,))[n]:
            self.copy(slot).start()

    def close(self, *slots):
        for s in slots:
            self.copy(s).wait_send()

    def stage(self, n, first=0):
        if n == 0:
            self.send(0)
        elif n < 5:
            self.take(n - 1, True)
        else:
            p = self.p
            self.copy(7).wait_recv()
            mine, theirs = self.bufs[4][self.leads[4] + (p.core,)], self.bufs[5][self.leads[5] + (...,)]
            left = jnp.where(p.core == 0, mine, theirs)
            right = jnp.where(p.core == 0, theirs, mine)
            self.close(*range(first, 8))
            return left, right


class Totals:
    def __init__(self, p, v, bufs, ssem, rsem):
        self.p, self.v, self.bufs, self.ssem, self.rsem = p, v, bufs, ssem, rsem

    def copy(self, slot):
        p = self.p
        dev = ([p.pc, p.pa, p.pb] + p.pz)[slot]
        return remote(self.v.at[min(slot, 3)], self.bufs.at[slot], self.ssem.at[slot], self.rsem.at[slot], dev)

    def stage(self, n):
        if n < 3:
            self.copy(n).start()
        if n == 3:
            for s in (3, 4, 5):
                self.copy(s).start()

    def step(self, n):
        if n < 3:
            self.copy(n).wait_recv()
            self.v[n + 1] = self.v[n] + self.bufs[n]
            return None
        total = self.v[3]
        for s in (3, 4, 5):
            self.copy(s).wait_recv()
            total = total + self.bufs[s]
        for s in range(6):
            self.copy(s).wait_send()
        return total


BACKWARD_ORDER = (
    (M0 + 2, M1 + 2),
    (M2 + 1,),
    (),
    (),
    (OUT + 0, M0 + 3),
    (BY + 0,),
    (OUT + 1, M1 + 3),
    (M2 + 2, BY + 1),
    (GATE + 0, OUT + 2),
    (M2 + 3, GATE + 1),
    (BY + 2,),
    (BX + 0, OUT + 3),
    (BX + 1, GATE + 2, BY + 3),
    (TOT + 0, BX + 2, M0 + 4, M1 + 4),
    (
        TOT + 1, GATE + 3, M0 + 5, M1 + 5, M2 + 4, BX + 3, TOT + 2, OUT + 4, BY + 4, TOT + 3, M2 + 5, OUT + 5,
        BY + 5, GATE + 4, GATE + 5, BX + 4, TOT + 4, BX + 5,
    ),
)


def backward_kernel(count, reach, *refs):
    (tokens, lengths, par, gain, gg2, i_wbx, i_wby, i_wgate, i_wout, i_by, i_fac, i_gx, i_ga, i_sc, i_st, i_bx, i_coded,
     i_mixed, i_u1, i_dmid, i_db, i_part01, i_part2,
     grad_tokens, o_proj, o_out, o_gate, o_in, o_down, o_cw, o_cb, o_gb, o_dec, o_g1, o_g2,
     wbx, wby, wgate, wout, adj, fac, st, pp, gslot, coded, mixed, u1, db, dby, dgx, since,
     own01, own2, gout, gpy, gpx, ggate,
     m_ra, m_rb, m_rz, m_tot, m_rc, p_r0, p_ra, p_rb, p_rz, p_tot, p_rc, t_r0, t_ra, t_rb, t_rz, t_tot, t_rc,
     edge, sums, gsum, vsum, vbuf, hin, mine, inbox,
     rs, rr, vs, vr, cs, cr, es, er, isem, gsem, lsem) = refs
    p = Place()
    me = p.me
    rows, width = tokens.shape

    inbox[...] = jnp.zeros_like(inbox)
    edge[...] = jnp.zeros_like(edge)
    def fetch(g, slot):
        return [
            pltpu.make_async_copy(src.at[g], gslot.at[slot, i, 0:rows], gsem.at[slot, i])
            for i, src in enumerate((i_gx, i_ga, i_sc))
        ]

    def fetch_bx(g, slot):
        return pltpu.make_async_copy(i_bx.at[g], gslot.at[slot, 0], gsem.at[slot, 3])

    parts = [
        pltpu.make_async_copy(i_part01, own01, lsem.at[0]),
        pltpu.make_async_copy(i_part2, own2, lsem.at[1]),
    ]
    parts[0].start()
    (load_db, load_wout, load_by, load_st, load_fac, load_mixed, load_u1, load_coded, load_wgate, load_wby, load_wbx) = loads = [
        pltpu.make_async_copy(src, dst, isem.at[i])
        for i, (src, dst) in enumerate((
            (i_db, db), (i_wout, wout), (i_by, adj.at[:, 0:rows]), (i_st, st), (i_fac, fac.at[:, 0:rows]), (i_mixed, mixed),
            (i_u1, u1), (i_coded, coded), (i_wgate, wgate), (i_wby, wby), (i_wbx, wbx)))
    ]
    for c in loads[:5] + parts[1:] + loads[5:7] + [c for g in range(SLOTS - 1) for c in fetch(g, g)] + loads[7:]:
        c.start()
    entry_barrier(p, count, reach)

    mbufs = (None, m_ra, m_rb, m_rz, m_tot, m_rc)
    red_m = [
        Reduce(p, None, own, lead, mbufs, (None, (), (k,), (k,), (k,), (k,)), rs.at[k], rr.at[k], groups)
        for k, own, lead, groups in ((0, own01, (0,), (0, 1)), (1, own01, (1,), (0, 1)), (2, own2, (), None))
    ]
    pbufs = (p_r0, p_ra, p_rb, p_rz, p_tot, p_rc)
    red_out, red_py, red_px = [
        Reduce(p, g, g, (p.core,), pbufs, ((k,),) * 6, rs.at[3 + k], rr.at[3 + k]) for k, g in enumerate((gout, gpy, gpx))
    ]
    red_gate = Reduce(
        p, ggate, ggate, (p.core,), (t_r0, t_ra, t_rb, t_rz, t_tot, t_rc), ((),) * 6, rs.at[6], rr.at[6]
    )

    since[...] = sequence_offset(lengths, me * rows, rows + 8)
    sums[...] = jnp.zeros_like(sums)
    gsum[...] = jnp.zeros_like(gsum)

    tot = Totals(p, vsum, vbuf, vs, vr)
    sums_of = {M0: red_m[0], M1: red_m[1], M2: red_m[2], OUT: red_out, BY: red_py, BX: red_px, GATE: red_gate}
    began = {M0: 2, M1: 2, M2: 1}
    points = iter(BACKWARD_ORDER)

    def write(name, left, right):
        if name in began:
            lo = 24 * ((name - M0) // 10)
            o_in[lo : lo + 24, 0:1152] = left
            o_in[lo : lo + 24, 1152:1536] = right[:, :384]
            o_down[lo : lo + 24, :] = right[:, 384:]
        elif name == OUT:
            o_out[:, :512], o_out[:, 512:] = left, right
        elif name == BY:
            o_proj[:, 1024:1536], o_proj[:, 1536:2048] = left, right
        elif name == BX:
            o_proj[:, 0:512], o_proj[:, 512:1024] = left, right
        else:
            o_gate[:, :256], o_gate[:, 256:] = left, right

    def write_totals(total):
        chan = pltpu.roll(total[0:8], lax.rem(1024 - 32 * me, 1024), 1)
        o_cw[...] = chan[0:4, 0:32]
        o_cb[...] = chan[4:5, 0:32]
        o_gb[...] = chan[5:7, 0:32]
        o_dec[...] = chan[7:8, 0:32]
        gains = pltpu.roll(total[8:16], lax.rem(1024 - 24 * me, 1024), 1)
        o_g1[...] = gains[0:1, 0:24]
        o_g2[...] = gains[1:2, 0:24]

    def at_point():
        for step in next(points):
            name, n = step // 10 * 10, step % 10
            if name == TOT:
                total = tot.step(n - 1) if n > 0 else None
                if n < 4:
                    tot.stage(n)
                else:
                    write_totals(total)
            elif n == began.get(name):
                sums_of[name].send(n)
            elif n < 5:
                sums_of[name].stage(n)
            else:
                first = began.get(name, 0)
                write(name, *sums_of[name].stage(5, (0, 1, 3)[first]))

    parts[0].wait()
    at_point()
    load_db.wait()
    load_wout.wait()

    def mix_dots(h, c):
        cols = pl.ds(pl.multiple_of(lax.rem(h, 2) * 256, 256), 256)
        v = nn(db[...], chips(wout[lax.div(h, 2), :, :, :, cols]))
        pp[2 * h, 0:rows, :], pp[2 * h + 1, 0:rows, :] = v[:, :128], v[:, 128:]
        return c

    lax.fori_loop(0, 4, mix_dots, 0)
    parts[1].wait()
    at_point()
    load_by.wait()
    load_st.wait()

    def branch_y(g, r0):
        at = pl.ds(r0, 64)
        dm = pp[g, at, :]
        act, slope = gelu_parts(adj[g, at, :])
        adj[g, at, :] = dm * act
        dby[g, at, :] = (dm * st[g, pl.ds(r0 + 8, 64), :] * slope).astype(BF16)

    blocks_loop(8, rows, 64, branch_y)
    at_point()
    load_fac.wait()
    fac[:, rows:, :] = jnp.ones((8, PAD, 128), F32)
    adj[:, rows:, :] = jnp.zeros((8, PAD, 128), F32)
    ends = scan_segments(fac, adj, pp, 0, 0, 0, True)
    _, leave = chain(ends, [jnp.zeros((1, 128), F32)] * 8, True)
    whole = products(ends)
    for g in range(8):
        mine[0, g : g + 1, :] = whole[g]
        mine[1, g : g + 1, :] = leave[g]
    carry_send(p, count, reach, -1, mine, inbox, cs, cr)
    at_point()
    load_mixed.wait()

    def halves(target, left, page):
        for h in range(2):
            v = tn(left, jnp.concatenate([page[4 * h + i] for i in range(4)], axis=1))
            put_chips(target, h, v.astype(BF16))

    halves(gout, db[...], mixed)
    at_point()
    load_u1.wait()
    halves(gpy, u1[...], dby)
    at_point()
    carry_wait(p, count, reach, -1, mine, inbox, cs, cr)
    inside, _ = chain(ends, carry_fold(p, count, reach, -1, inbox), True)
    for g in range(8):
        hin[g] = inside[g]
    step = rows // SEG

    def adjoint(g, c):
        inside_g = hin[g]
        for s in range(SEG):
            lo = s * step
            adj[g, lo : lo + step, :] += pp[g, lo : lo + step, :] * segment_rows(inside_g, s, step)
        return c

    lax.fori_loop(0, 8, adjoint, 0)
    at_point()
    load_coded.wait()
    dga = mixed

    def gate_back(g, slot, last):
        @pl.when(jnp.logical_not(last))
        def _():
            for c_ in fetch(g + SLOTS - 1, (slot + SLOTS - 1) % SLOTS):
                c_.start()

        for c_ in fetch(g, slot):
            c_.wait()
        row = par[g]
        sp8 = -8.0 * softplus(row[7:8])

        def block(i, acc):
            r0 = pl.multiple_of(i * 64, 64)
            at = pl.ds(r0, 64)
            a, f = adj[g, at, :], fac[g, at, :]
            gate_x, gate_a, scale = gslot[slot, 0, at, :], gslot[slot, 1, at, :], gslot[slot, 2, at, :]
            code = coded[g, at, :].astype(F32)
            before = st[g, pl.ds(r0, 72), :][7:71]
            d_log = a * f * (before - gate_x * code * f / scale)
            d_a = d_log * gate_a
            d_ga = d_a * sp8 * (1.0 - gate_a)
            d_part = a * scale * gate_x
            d_gx = d_part * code * (1.0 - gate_x)
            dgx[g, at, :] = d_gx.astype(BF16)
            dga[g, at, :] = d_ga.astype(BF16)
            adj[g, at, :] = d_part
            return acc[0] + fold8(d_gx), acc[1] + fold8(d_ga), acc[2] + fold8(d_a)

        zero = jnp.zeros((8, 128), F32)
        acc = lax.fori_loop(0, rows // 64, block, (zero, zero, zero))
        slope = jax.nn.sigmoid(row[7:8])
        sums[g, 5:6, :] = jnp.sum(acc[0], axis=0, keepdims=True)
        sums[g, 6:7, :] = jnp.sum(acc[1], axis=0, keepdims=True)
        sums[g, 7:8, :] = jnp.sum(acc[2], axis=0, keepdims=True) * (-8.0 * slope)

    slots_loop(gate_back)
    for g in range(SLOTS - 1):
        fetch_bx(g, g).start()
    load_dmid = pltpu.make_async_copy(i_dmid, st.at[0:6, 0:rows], isem.at[11])
    load_dmid.start()
    dbx = dgx
    at_point()
    load_wgate.wait()

    def gate_dots(h, c):
        dx, da, code = lanes(dgx, 2 * h, 0, rows), lanes(dga, 2 * h, 0, rows), lanes(coded, 2 * h, 0, rows)
        v = nt(dx, wgate[0, :, h].reshape(256, 256)) + nt(da, wgate[1, :, h].reshape(256, 256))
        adj[2 * h, 0:rows, :] += v[:, :128]
        adj[2 * h + 1, 0:rows, :] += v[:, 128:]
        ggate[0, :, h] = tn(code, dx).astype(BF16).reshape(4, 64, 256)
        ggate[1, :, h] = tn(code, da).astype(BF16).reshape(4, 64, 256)
        return c

    lax.fori_loop(0, 4, gate_dots, 0)
    edge[0] = adj[:, 0:8, :]
    to_prev = remote(edge.at[0], edge.at[1], es.at[0], er.at[0], me - 1)

    @pl.when(me > 0)
    def _():
        to_prev.start()

    at_point()
    load_wby.wait()
    put(pp, nt(jnp.concatenate([dby[g] for g in range(8)], axis=1), whole_w(wby)), 0, 0)
    at_point()

    @pl.when(me > 0)
    def _():
        to_prev.wait_send()

    @pl.when(me + 1 < count)
    def _():
        to_prev.wait_recv()

    adj[:, rows : rows + 8, :] = edge[1]

    def conv_back(g, slot, last):
        @pl.when(jnp.logical_not(last))
        def _():
            fetch_bx(g + SLOTS - 1, (slot + SLOTS - 1) % SLOTS).start()

        fetch_bx(g, slot).wait()
        row = par[g]

        def block(i, acc):
            r0 = pl.multiple_of(i * 64, 64)
            d = adj[g, pl.ds(r0, 72), :]
            off = since[pl.ds(r0, 72), :]
            b = gslot[slot, 0, pl.ds(r0 + 8, 72), :]
            own, off0 = d[0:64], off[0:64]
            total = row[0:1] * own
            out = [acc[0] + fold8(own * b[8:72])]
            for k in range(1, 4):
                total = total + row[k : k + 1] * jnp.where(off[k : 64 + k] >= k, d[k : 64 + k], 0.0)
                out.append(acc[k] + fold8(own * jnp.where(off0 >= k, b[8 - k : 72 - k], 0.0)))
            out.append(acc[4] + fold8(own))
            dbx[g, pl.ds(r0, 64), :] = total.astype(BF16)
            return tuple(out)

        acc = lax.fori_loop(0, rows // 64, block, tuple(jnp.zeros((8, 128), F32) for _ in range(5)))
        for k in range(5):
            sums[g, k : k + 1, :] = jnp.sum(acc[k], axis=0, keepdims=True)

    slots_loop(conv_back)
    at_point()
    halves(gpx, u1[...], dbx)
    at_point()
    load_wbx.wait()
    du = nt(jnp.concatenate([dbx[g] for g in range(8)], axis=1), whole_w(wbx))
    for g in range(6):
        pp[g, 0:rows, :] += du[:, g * 128 : (g + 1) * 128]
    at_point()
    load_dmid.wait()

    def finish(r0):
        at = pl.ds(r0, 32)
        x = tokens[at, :].astype(F32)
        d = wide(pp, 6, r0, 32)
        inv = lax.rsqrt(jnp.mean(x * x, axis=1, keepdims=True) + EPSILON)
        gsum[...] += fold8(d * x * inv)
        scaled = d * gain[0:1, :]
        back = jnp.mean(scaled * x, axis=1, keepdims=True)
        grad_tokens[at, :] = (wide(st, 6, r0, 32) + inv * scaled - x * (inv * inv * inv * back)).astype(BF16)

    rows_loop(rows, 32, finish)
    vsum[0] = jnp.zeros((16, 1024), F32)
    for g in range(8):
        vsum[0, 0:8, g * 128 : (g + 1) * 128] = sums[g]
    vsum[0, 8:9, 0:width] = jnp.sum(gsum[...], axis=0, keepdims=True)
    vsum[0, 9:10, 0:width] = jnp.sum(gg2[...], axis=0, keepdims=True)
    at_point()
    at_point()


def backward_call(count, reach, args):
    tokens = args[0]
    rows, width = tokens.shape
    S = jax.ShapeDtypeStruct
    V = pltpu.VMEM
    dma = pltpu.SemaphoreType.DMA
    page = (8, rows, 128)
    outs = [
        S((rows, width), BF16), S((24, 2048), F32), S((24, 1024), F32), S((32, 512), F32), S((72, 1536), F32),
        S((72, 768), F32), S((4, 32), F32), S((1, 32), F32), S((2, 32), F32), S((1, 32), F32), S((1, 24), F32),
        S((1, 24), F32),
    ]

    def bufs(n, r, c):
        lead = (n,) if n else ()
        return [V(lead + (4, 4, r, c), BF16), V(lead + (2, 4, r, c), BF16), V(lead + (4, r, c), BF16),
                V(lead + (3, r, c), BF16), V(lead + (2, r // 2, c), F32), V(lead + (r // 2, c), F32)]

    scratch = [
        V((2, 4, 4, 48, 512), BF16), V((2, 4, 4, 48, 512), BF16), V((2, 4, 4, 64, 256), BF16), V((2, 4, 4, 48, 512), BF16),
        V((8, rows + PAD, 128), F32),
        V((8, rows + PAD, 128), F32),
        V((8, rows + 8, 128), F32),
        V((8, rows + PAD, 128), F32),
        V((SLOTS, 3, rows + 16, 128), F32),
        V(page, BF16), V(page, BF16), V((rows, width), BF16), V((rows, width), BF16),
        V(page, BF16), V(page, BF16),
        V((rows + 8, 128), jnp.int32),
        V((2, 2, 4, 48, 1152), BF16), V((4, 4, 48, 1152), BF16),
        V((2, 4, 4, 48, 512), BF16), V((2, 4, 4, 48, 512), BF16), V((2, 4, 4, 48, 512), BF16),
        V((2, 4, 4, 64, 256), BF16),
        V((2, 4, 48, 1152), BF16), *bufs(3, 48, 1152)[2:], *bufs(3, 48, 512), *bufs(0, 64, 256),
        V((2, 8, 8, 128), F32),
        V((8, 8, 128), F32), V((8, width), F32), V((4, 16, 1024), F32), V((6, 16, 1024), F32),
        V((8, 8, 128), F32), V((2, 8, 128), F32), V((reach, 2, 8, 128), F32),
        dma((7, 8)), dma((7, 8)), dma((6,)), dma((6,)), dma((reach,)), dma((reach,)), dma((1,)), dma((1,)),
        dma((12,)), dma((SLOTS, 4)), dma((2,)),
    ]
    return pl.pallas_call(
        functools.partial(backward_kernel, count, reach),
        out_shape=outs,
        in_specs=[VM, SM, VM, VM, VM] + [ANY] * 18,
        out_specs=[VM] * len(outs),
        scratch_shapes=scratch,
        name="backward",
        cost_estimate=pl.CostEstimate(flops=12 * 10**9, bytes_accessed=60 * 10**6, transcendentals=10**7),
        compiler_params=pltpu.CompilerParams(
            collective_id=1, has_side_effects=True, vmem_limit_bytes=63 * MIB
        ),
    )(*args)


def results_kernel(n, *refs):
    for i in range(n):
        refs[n + i][...] = refs[i][...]


def results_call(arrays):
    n = len(arrays)
    return pl.pallas_call(
        functools.partial(results_kernel, n),
        out_shape=[jax.ShapeDtypeStruct(a.shape, a.dtype) for a in arrays],
        in_specs=[VM] * n,
        out_specs=[VM] * n,
        name="results",
        cost_estimate=pl.CostEstimate(flops=0, bytes_accessed=2 * sum(a.size * a.dtype.itemsize for a in arrays), transcendentals=0),
    )(*arrays)


def from_behind(x, axis, by):
    size = lax.axis_size(axis)
    pairs = [(i, i + by) for i in range(size) if 0 <= i + by < size]
    return lax.ppermute(x, axis, pairs)


def prefix(part, axis, combine, identity, reverse):
    count = lax.axis_size(axis)
    place = lax.axis_index(axis)
    ahead = count - 1 - place if reverse else place
    gathered = jax.tree.map(lambda a: lax.all_gather(a, axis), part)
    state = jax.tree.map(lambda a, e: jnp.zeros_like(a) + jnp.asarray(e, a.dtype), part, identity)

    def one(lap, state):
        source = count - 1 - lap if reverse else lap
        return combine(
            state, jax.tree.map(lambda a: lax.dynamic_index_in_dim(a, source, 0, False), gathered)
        )

    return lax.fori_loop(0, ahead, one, state)


def rms_scale(values, gain_row):
    inverse = lax.rsqrt(jnp.mean(values * values, axis=-1, keepdims=True) + EPSILON)
    return values * inverse * gain_row


def combine_steps(earlier, later):
    return (earlier[0] * later[0], later[0] * earlier[1] + later[1])


def smooth_gelu(inputs):
    return jax.nn.gelu(inputs, approximate=True)


def glu_piece(gate_pre, up_value):
    return smooth_gelu(gate_pre) * up_value


def gate_math(gate_pre, bias_rows, decay_vec, coded_rows, fresh_row):
    tok_rows, rnn_width = coded_rows.shape
    block_size = gate_pre.shape[2] // 2
    gate_x = jax.nn.sigmoid(gate_pre[:, :, :block_size].reshape(tok_rows, rnn_width) + bias_rows[0])
    gate_a = jax.nn.sigmoid(gate_pre[:, :, block_size:].reshape(tok_rows, rnn_width) + bias_rows[1])
    log_a = -8.0 * gate_a * jax.nn.softplus(decay_vec)
    factor = jnp.where(fresh_row, 0.0, jnp.exp(log_a))
    scale_term = jnp.where(fresh_row, 1.0, jnp.sqrt(-jnp.expm1(2.0 * log_a)))
    return (factor, scale_term * gate_x * coded_rows)


def per_device(
    tokens,
    cotangent,
    lengths,
    gain_norm1,
    gain_norm2,
    proj_in,
    out_proj,
    gate_blocks,
    conv_weight,
    conv_bias,
    gate_bias,
    decay_param,
    mlp_in,
    mlp_down,
):
    tok_rows, model_width = tokens.shape
    conv_taps = conv_weight.shape[0]
    reach_back = conv_taps - 1
    first_row = lax.axis_index("dp") * tok_rows
    places = first_row + jnp.arange(-reach_back, tok_rows, dtype=jnp.int32)
    bounds = jnp.cumsum(lengths)
    labels = jnp.sum((places[:, None] >= bounds[None, :]).astype(jnp.int32), axis=1)
    labels = jnp.where(places < 0, -1, labels)
    own_label = labels[reach_back:]
    fresh_row = (own_label != labels[reach_back - 1 : reach_back - 1 + tok_rows])[:, None]
    tap_masks = [
        (labels[reach_back - offset : reach_back - offset + tok_rows] == own_label)[:, None].astype(
            jnp.float32
        )
        for offset in range(conv_taps)
    ]
    gathered = (
        lax.all_gather(proj_in, "dp", axis=0, tiled=True),
        lax.all_gather(out_proj, "dp", axis=0, tiled=True),
        lax.all_gather(gate_blocks, "dp", axis=0, tiled=True),
        lax.all_gather(gain_norm1, "dp", axis=0, tiled=True),
        lax.all_gather(gain_norm2, "dp", axis=0, tiled=True),
        lax.all_gather(conv_weight, "dp", axis=1, tiled=True),
        lax.all_gather(conv_bias, "dp", axis=0, tiled=True),
        lax.all_gather(gate_bias, "dp", axis=1, tiled=True),
        lax.all_gather(decay_param, "dp", axis=0, tiled=True),
    )
    w_proj, w_out, w_gates = (gathered[0], gathered[1], gathered[2])
    gain_one = gathered[3].astype(jnp.float32)
    gain_two = gathered[4].astype(jnp.float32)
    w_conv = gathered[5].astype(jnp.float32)
    b_conv = gathered[6].astype(jnp.float32)
    b_gates = gathered[7].astype(jnp.float32)
    w_decay = gathered[8].astype(jnp.float32)
    rnn_width = w_conv.shape[1]
    w_mlp, w_down = (
        lax.all_gather(mlp_in, "dp", axis=0, tiled=True),
        lax.all_gather(mlp_down, "dp", axis=0, tiled=True),
    )
    residual = tokens.astype(jnp.float32)
    normed_one, norm_one_back = jax.vjp(rms_scale, residual, gain_one)
    u_one = normed_one.astype(jnp.bfloat16)
    projected = jnp.dot(u_one, w_proj, preferred_element_type=jnp.float32)
    branch_x = projected[:, :rnn_width].astype(jnp.bfloat16)
    branch_y = projected[:, rnn_width:]
    rim_rows = from_behind(branch_x[tok_rows - reach_back :], "dp", 1)
    padded = jnp.concatenate([rim_rows, branch_x], axis=0)
    conv_sum = jnp.zeros((tok_rows, rnn_width), jnp.float32) + b_conv
    for offset in range(conv_taps):
        conv_sum = (
            conv_sum
            + w_conv[offset]
            * padded[reach_back - offset : reach_back - offset + tok_rows].astype(jnp.float32)
            * tap_masks[offset]
        )
    coded_rows = conv_sum.astype(jnp.bfloat16)
    block_size = w_gates.shape[1] // 2
    head_count = rnn_width // block_size
    blocks_w = w_gates.reshape(head_count, block_size, 2 * block_size)
    coded_heads = coded_rows.reshape(tok_rows, head_count, block_size)
    gate_pre = jnp.einsum("thi,hij->thj", coded_heads, blocks_w, preferred_element_type=jnp.float32)
    gate_fn = functools.partial(gate_math, fresh_row=fresh_row)
    (factor, drive_term), gate_back = jax.vjp(
        gate_fn, gate_pre, b_gates, w_decay, coded_rows.astype(jnp.float32)
    )
    prefix_a, local_h = lax.associative_scan(combine_steps, (factor, drive_term), axis=0)
    unit_pair = (jnp.ones((rnn_width,), jnp.float32), jnp.zeros((rnn_width,), jnp.float32))
    carry_unused, carry_h = prefix(
        (prefix_a[-1], local_h[-1]), "dp", combine_steps, unit_pair, False
    )
    state_rows = local_h + prefix_a * carry_h[None, :]
    y_branch_act, y_back = jax.vjp(smooth_gelu, branch_y)
    mixed_rows = (state_rows * y_branch_act).astype(jnp.bfloat16)
    middle = residual + jnp.einsum(
        "tr,dr->td", mixed_rows, w_out, preferred_element_type=jnp.float32
    )
    normed_two, norm_two_back = jax.vjp(rms_scale, middle, gain_two)
    u_two = normed_two.astype(jnp.bfloat16)
    gate_val = jnp.einsum(
        "td,fd->tf", u_two, w_mlp[:, :model_width], preferred_element_type=jnp.float32
    )
    up_val = jnp.einsum(
        "td,fd->tf", u_two, w_mlp[:, model_width:], preferred_element_type=jnp.float32
    )
    glu_value, glu_back = jax.vjp(glu_piece, gate_val, up_val)
    hidden = glu_value.astype(jnp.bfloat16)
    output = (middle + jnp.dot(hidden, w_down, preferred_element_type=jnp.float32)).astype(
        jnp.bfloat16
    )
    w_proj, w_out, w_gates = (
        lax.all_gather(proj_in, "dp", axis=0, tiled=True),
        lax.all_gather(out_proj, "dp", axis=0, tiled=True),
        lax.all_gather(gate_blocks, "dp", axis=0, tiled=True),
    )
    w_mlp, w_down = (
        lax.all_gather(mlp_in, "dp", axis=0, tiled=True),
        lax.all_gather(mlp_down, "dp", axis=0, tiled=True),
    )
    blocks_w = w_gates.reshape(head_count, block_size, 2 * block_size)
    d_hidden = jnp.einsum("td,fd->tf", cotangent, w_down, preferred_element_type=jnp.float32)
    d_gate_f, d_up_f = glu_back(d_hidden)
    d_gate = d_gate_f.astype(jnp.bfloat16)
    d_up = d_up_f.astype(jnp.bfloat16)
    feed_sum = None
    d_u_two = jnp.einsum(
        "tf,fd->td", d_gate, w_mlp[:, :model_width], preferred_element_type=jnp.float32
    )
    d_u_two = d_u_two + jnp.einsum(
        "tf,fd->td", d_up, w_mlp[:, model_width:], preferred_element_type=jnp.float32
    )
    d_norm_mid, d_gain_two = norm_two_back(d_u_two)
    d_middle = cotangent.astype(jnp.float32) + d_norm_mid
    d_branch = d_middle.astype(jnp.bfloat16)
    d_mixed = jnp.dot(d_branch, w_out, preferred_element_type=jnp.float32)
    d_state = d_mixed * y_branch_act
    d_branch_y = y_back(d_mixed * state_rows)[0].astype(jnp.bfloat16)
    ahead_factor = jnp.concatenate([factor[1:], jnp.ones((1, rnn_width), jnp.float32)], axis=0)
    back_prod, local_g = lax.associative_scan(
        combine_steps, (ahead_factor, d_state), reverse=True, axis=0
    )
    carry_skip, carry_q = prefix(
        (factor[0] * back_prod[0], factor[0] * local_g[0]), "dp", combine_steps, unit_pair, True
    )
    adjoint = local_g + back_prod * carry_q[None, :]
    before = jnp.concatenate([carry_h[None, :], state_rows[:-1]], axis=0)
    d_pre_f, d_shift, d_decay, d_coded_part = gate_back((adjoint * before, adjoint))
    d_pre = d_pre_f.astype(jnp.bfloat16)
    d_coded = d_coded_part + jnp.einsum(
        "thj,hij->thi", d_pre, blocks_w, preferred_element_type=jnp.float32
    ).reshape(tok_rows, rnn_width)
    gate_grad = jnp.einsum(
        "thi,thj->hij", coded_heads, d_pre, preferred_element_type=jnp.float32
    ).reshape(rnn_width, 2 * block_size)
    spread = jnp.zeros((tok_rows + reach_back, rnn_width), jnp.float32)
    tap_grads = []
    for offset in range(conv_taps):
        spread = spread + jnp.pad(
            w_conv[offset] * tap_masks[offset] * d_coded, ((reach_back - offset, offset), (0, 0))
        )
        tap_grads.append(
            jnp.sum(
                d_coded
                * tap_masks[offset]
                * padded[reach_back - offset : reach_back - offset + tok_rows].astype(jnp.float32),
                axis=0,
            )
        )
    d_conv_w = jnp.stack(tap_grads, axis=0)
    d_conv_b = jnp.sum(d_coded, axis=0)
    back_rim = from_behind(spread[:reach_back], "dp", -1)
    d_branch_x = (
        spread[reach_back:] + jnp.pad(back_rim, ((tok_rows - reach_back, 0), (0, 0)))
    ).astype(jnp.bfloat16)
    d_projected = jnp.concatenate([d_branch_x, d_branch_y], axis=1)
    d_u_one = jnp.einsum("tk,dk->td", d_projected, w_proj, preferred_element_type=jnp.float32)
    d_norm_in, d_gain_one = norm_one_back(d_u_one)
    grad_tokens = (d_middle + d_norm_in).astype(jnp.bfloat16)
    part_gate = jnp.einsum("tf,td->fd", d_gate, u_two, preferred_element_type=jnp.float32)
    part_up = jnp.einsum("tf,td->fd", d_up, u_two, preferred_element_type=jnp.float32)
    part_down = jnp.einsum("tf,td->fd", hidden, cotangent, preferred_element_type=jnp.float32)
    feed_sum = lax.psum_scatter(
        jnp.concatenate([part_gate, part_up, part_down], axis=1),
        "dp",
        scatter_dimension=0,
        tiled=True,
    )
    part_proj = jnp.einsum("td,tk->dk", u_one, d_projected, preferred_element_type=jnp.float32)
    part_out = jnp.einsum("td,tr->dr", d_branch, mixed_rows, preferred_element_type=jnp.float32)
    rec_sum = lax.psum_scatter(
        jnp.concatenate([part_proj, part_out], axis=1), "dp", scatter_dimension=0, tiled=True
    )
    channel_sums = (
        lax.psum_scatter(d_gain_one, "dp", scatter_dimension=0, tiled=True),
        lax.psum_scatter(d_gain_two, "dp", scatter_dimension=0, tiled=True),
        lax.psum_scatter(d_conv_w, "dp", scatter_dimension=1, tiled=True),
        lax.psum_scatter(d_conv_b, "dp", scatter_dimension=0, tiled=True),
        lax.psum_scatter(d_shift, "dp", scatter_dimension=1, tiled=True),
        lax.psum_scatter(d_decay, "dp", scatter_dimension=0, tiled=True),
        lax.psum_scatter(gate_grad, "dp", scatter_dimension=0, tiled=True),
    )
    return (
        output,
        grad_tokens,
        channel_sums[0],
        channel_sums[1],
        rec_sum[:, : 2 * rnn_width],
        rec_sum[:, 2 * rnn_width :],
        channel_sums[6],
        channel_sums[2],
        channel_sums[3],
        channel_sums[4],
        channel_sums[5],
        feed_sum[:, : 2 * model_width],
        feed_sum[:, 2 * model_width :],
    )


def kernels_step(
    tokens, cotangent, lengths, gain_norm1, gain_norm2, proj_in, out_proj, gate_blocks, conv_weight, conv_bias, gate_bias,
    decay_param, mlp_in, mlp_down,
):
    count = lax.axis_size("dp")
    rows = tokens.shape[0]
    longest = rows * count // 12
    reach = -(-(longest - 1) // rows)
    (output, par, gain, gg2, wbx, wby, wgate, wout, by, fac, gx, ga, sc, st, bx, coded, mixed, u1, dmid, db, part01,
     part2) = forward_call(
        count, reach,
        (tokens, cotangent, lengths, conv_weight, conv_bias[None], gate_bias, decay_param[None], gain_norm1[None],
         gain_norm2[None], proj_in, out_proj, gate_blocks, mlp_in, mlp_down),
    )
    grads = backward_call(
        count, reach,
        (tokens, lengths, par, gain, gg2, wbx, wby, wgate, wout, by, fac, gx, ga, sc, st, bx, coded, mixed, u1, dmid, db,
         part01, part2),
    )
    (output, grad_tokens, g_proj, g_out, g_gate, g_in, g_down, g_cw, g_cb, g_gb, g_dec, g_n1, g_n2) = results_call(
        [output, *grads]
    )
    return (
        output, grad_tokens, g_n1[0], g_n2[0], g_proj, g_out, g_gate, g_cw, g_cb[0], g_gb, g_dec[0], g_in, g_down,
    )


def fits(mesh):
    return mesh.shape["dp"] == 32


def solution(mesh):
    placed = (
        P("dp", None),
        P("dp", None),
        P(),
        P("dp"),
        P("dp"),
        P("dp", None),
        P("dp", None),
        P("dp", None),
        P(None, "dp"),
        P("dp"),
        P(None, "dp"),
        P("dp"),
        P("dp", None),
        P("dp", None),
    )
    return jax.shard_map(
        kernels_step if fits(mesh) else per_device,
        mesh=mesh,
        in_specs=placed,
        out_specs=(
            P("dp", None),
            P("dp", None),
            P("dp"),
            P("dp"),
            P("dp", None),
            P("dp", None),
            P("dp", None),
            P(None, "dp"),
            P("dp"),
            P(None, "dp"),
            P("dp"),
            P("dp", None),
            P("dp", None),
        ),
        check_vma=False,
    )
```

```python
import functools

import jax
import jax.numpy as jnp
from jax import lax
from jax.experimental import pallas as pl
from jax.experimental.pallas import tpu as pltpu
from jax.sharding import PartitionSpec as P

EPSILON = 1e-06
MESH = pl.DeviceIdType.MESH
F32, BF16 = jnp.float32, jnp.bfloat16
VM = pl.BlockSpec(memory_space=pltpu.VMEM)
ANY = pl.BlockSpec(memory_space=pl.ANY)
SM = pl.BlockSpec(memory_space=pltpu.SMEM)
MIB = 2**20
SEG = 8
STEP = 97
PAD = 8


def nn(a, b):
    return jnp.dot(a, b, preferred_element_type=F32)


def nt(a, b):
    return lax.dot_general(a, b, (((1,), (1,)), ((), ())), preferred_element_type=F32)


def tn(a, b):
    return lax.dot_general(a, b, (((0,), (0,)), ((), ())), preferred_element_type=F32)


class Place:
    def __init__(self):
        me = lax.axis_index("dp")
        self.me = me
        self.core = core = lax.rem(me, 2)
        x = lax.rem(lax.div(me, 2), 2)
        y = lax.rem(lax.div(me, 4), 2)
        self.z = z = lax.div(me, 8)
        self.yx = yx = 2 * y + x
        px, py = me + 2 - 4 * x, me + 4 - 8 * y
        gx, gy = yx + 1 - 2 * x, yx + 2 - 4 * y
        self.pa, self.pb = px + core * (py - px), py + core * (px - py)
        self.ga, self.gb = gx + core * (gy - gx), gy + core * (gx - gy)
        self.gd = 3 - yx
        self.pc = me + 1 - 2 * core
        self.other = 1 - core
        self.zs = [lax.rem(z + d, 4) for d in (1, 2, 3)]
        self.pz = [zz * 8 + lax.rem(me, 8) for zz in self.zs]


def remote(src, dst, ssem, rsem, device):
    return pltpu.make_async_remote_copy(
        src_ref=src, dst_ref=dst, send_sem=ssem, recv_sem=rsem, device_id=(device,), device_id_type=MESH
    )


def entry_barrier(pl_, count, reach):
    me = pl_.me
    bar = pltpu.get_barrier_semaphore()
    for p in [pl_.pc, pl_.pa, pl_.pb] + pl_.pz:
        pl.semaphore_signal(bar, inc=1, device_id=(p,), device_id_type=MESH)
    for d in range(1, reach + 1):

        @pl.when(me >= d)
        def _():
            pl.semaphore_signal(bar, inc=1, device_id=(me - d,), device_id_type=MESH)

        @pl.when(me + d < count)
        def _():
            pl.semaphore_signal(bar, inc=1, device_id=(me + d,), device_id_type=MESH)

    pl.semaphore_wait(bar, 6 + jnp.minimum(me, reach) + jnp.minimum(count - 1 - me, reach))


class Gather:
    def __init__(self, p, buf, ssem, rsem):
        self.p, self.buf, self.ssem, self.rsem = p, buf, ssem, rsem

    def copy(self, slot):
        p = self.p
        if slot < 3:
            src, dev = self.buf.at[p.core, p.yx, p.z], p.pz[slot]
        else:
            group = (p.yx, p.yx, p.ga, p.yx, p.ga, p.gb, p.gd)[slot - 3]
            src, dev = self.buf.at[p.core, group], (p.pa, p.pb, p.pb, p.pc, p.pc, p.pc, p.pc)[slot - 3]
        return remote(src, src, self.ssem.at[slot], self.rsem.at[slot], dev)

    def start(self, *slots):
        for s in slots:
            self.copy(s).start()

    def recv(self, *slots):
        for s in slots:
            self.copy(s).wait_recv()

    def stage(self, n):
        if n == 0:
            self.start(0, 1, 2)
        elif n == 1:
            self.recv(0, 1, 2)
            self.start(3, 4, 6)
        elif n == 2:
            self.recv(3)
            self.start(5, 7)
        elif n == 3:
            self.recv(4)
            self.start(8)
            self.recv(5)
            self.start(9)
        else:
            self.recv(6, 7, 8, 9)
            for s in range(10):
                self.copy(s).wait_send()


def sequence_offset(lengths, first, rows):
    t = first + lax.broadcasted_iota(jnp.int32, (rows, 128), 0)

    def one(i, c):
        bound, start = c
        bound = bound + lengths[i]
        return bound, jnp.where(t >= bound, bound, start)

    _, start = lax.fori_loop(0, lengths.shape[0], one, (jnp.int32(0), jnp.zeros((rows, 128), jnp.int32)))
    return t - start


def one_minus_square(v, root):
    series = 1.0 / 2.0 + v * (1.0 / 6.0 + v * (1.0 / 24.0 + v * (1.0 / 120.0 + v * (1.0 / 720.0))))
    return jnp.where(v > -0.125, -v - v * v * series, 1.0 - root * root)


def root_of(v):
    return v * lax.rsqrt(jnp.maximum(v, 1e-37))


def softplus(v):
    return jnp.maximum(v, 0.0) + jnp.log1p(jnp.exp(-jnp.abs(v)))


GELU_K = 0.7978845608028654


def gelu_parts(v):
    v2 = v * v
    th = jnp.tanh(GELU_K * v * (1.0 + 0.044715 * v2))
    half = 0.5 * (1.0 + th)
    slope = half + 0.5 * v * (1.0 - th * th) * (GELU_K * (1.0 + 3.0 * 0.044715 * v2))
    return v * half, slope


def gelu(v):
    return v * (0.5 * (1.0 + jnp.tanh(GELU_K * v * (1.0 + 0.044715 * (v * v)))))


def flat(v):
    return v.reshape(v.shape[0] * v.shape[1] * v.shape[2], v.shape[3])


def chips(v):
    return jnp.concatenate([v[yx, z] for z in range(4) for yx in range(4)], axis=0)


def whole_w(w):
    return jnp.concatenate([chips(w[0]), chips(w[1])], axis=1)


def put_chips(part, half, v):
    rows = v.shape[0] // 16
    for z in range(4):
        for yx in range(4):
            part[half, yx, z] = v[(4 * z + yx) * rows : (4 * z + yx + 1) * rows]


def put(page, v, row, group):
    for i in range(v.shape[1] // 128):
        page[group + i, row : row + v.shape[0], :] = v[:, i * 128 : (i + 1) * 128]


def rows_loop(total, block, body):
    def one(i, c):
        body(pl.multiple_of(i * block, block))
        return c

    lax.fori_loop(0, total // block, one, 0)


def blocks_loop(groups, total, block, body):
    n = total // block

    def one(i, c):
        body(lax.div(i, n), pl.multiple_of(lax.rem(i, n) * block, block))
        return c

    lax.fori_loop(0, groups * n, one, 0)


SLOTS = 4


def slots_loop(body):
    def one(i, c):
        for slot in range(SLOTS):
            body(SLOTS * i + slot, slot, False if slot == 0 else i == 8 // SLOTS - 1)
        return c

    lax.fori_loop(0, 8 // SLOTS, one, 0)


def scan_segments(factor, value, product, factor_row, value_row, product_row, reverse):
    def one(i, c):
        j = STEP - 1 - i if reverse else i
        out = []
        for g in range(8):
            h, q = c[g]
            a = factor[g, pl.ds(factor_row + j, SEG, stride=STEP), :]
            b = value[g, pl.ds(value_row + j, SEG, stride=STEP), :]
            if reverse:
                h = b + h
                value[g, pl.ds(value_row + j, SEG, stride=STEP), :] = h
                product[g, pl.ds(product_row + j, SEG, stride=STEP), :] = q
                h, q = a * h, a * q
            else:
                h, q = a * h + b, a * q
                value[g, pl.ds(value_row + j, SEG, stride=STEP), :] = h
                product[g, pl.ds(product_row + j, SEG, stride=STEP), :] = q
            out.append((h, q))
        return tuple(out)

    first = tuple((jnp.zeros((SEG, 128), F32), jnp.ones((SEG, 128), F32)) for _ in range(8))
    return lax.fori_loop(0, STEP, one, first)


def segment_rows(inside, i, block):
    rest = inside[i : i + 1, :]
    first = jnp.broadcast_to(rest, (8, 128))
    if i:
        spot = lax.broadcasted_iota(jnp.int32, (8, 128), 0)
        first = jnp.where(spot < i, inside[i - 1 : i, :], first)
    return jnp.concatenate([first, jnp.broadcast_to(rest, (block - 8, 128))], axis=0)


def chain(ends, enter, reverse):
    order = range(SEG - 1, -1, -1) if reverse else range(SEG)
    inside, leave = [], []
    for g in range(8):
        h, q = ends[g]
        v = enter[g]
        rows = [None] * SEG
        for s in order:
            rows[s] = v
            v = q[s : s + 1, :] * v + h[s : s + 1, :]
        inside.append(jnp.concatenate(rows, axis=0))
        leave.append(v)
    return inside, leave


def products(ends):
    out = []
    for g in range(8):
        q = ends[g][1]
        v = q[0:1, :]
        for s in range(1, SEG):
            v = v * q[s : s + 1, :]
        out.append(v)
    return out


def carry_send(p, count, reach, sign, mine, inbox, ssem, rsem):
    for d in range(1, reach + 1):

        @pl.when((p.me + d < count) if sign > 0 else (p.me >= d))
        def _(d=d):
            remote(mine, inbox.at[d - 1], ssem.at[d - 1], rsem.at[d - 1], p.me + sign * d).start()


def carry_wait(p, count, reach, sign, mine, inbox, ssem, rsem):
    for d in range(1, reach + 1):
        there = remote(mine, inbox.at[d - 1], ssem.at[d - 1], rsem.at[d - 1], p.me + sign * d)

        @pl.when((p.me + d < count) if sign > 0 else (p.me >= d))
        def _(there=there):
            there.wait_send()

        @pl.when((p.me >= d) if sign > 0 else (p.me + d < count))
        def _(there=there):
            there.wait_recv()


def carry_fold(p, count, reach, sign, inbox):
    v = [jnp.zeros((1, 128), F32) for _ in range(8)]
    for d in range(reach, 0, -1):
        for g in range(8):
            v[g] = inbox[d - 1, 0, g : g + 1, :] * v[g] + inbox[d - 1, 1, g : g + 1, :]
    return v


def lanes(page, group, row, rows):
    return jnp.concatenate([page[group, pl.ds(row, rows), :], page[group + 1, pl.ds(row, rows), :]], axis=1)


def wide(page, groups, row, rows):
    return jnp.concatenate([page[g, pl.ds(row, rows), :] for g in range(groups)], axis=1)


def fold8(v):
    return jnp.sum(v.reshape(v.shape[0] // 8, 8, v.shape[1]), axis=0)


SMALL, BX, GATE, BY, OUT, M0, M1, M2, SUM0, SUM1, SUM2, TOT = range(0, 120, 10)

FORWARD_ORDER = (
    (),
    (
        SMALL + 1, SMALL + 2, GATE + 1, BX + 0, OUT + 1, BY + 0, BX + 1, SMALL + 3, SMALL + 4, M0 + 0,
        M1 + 0, BY + 1, OUT + 2,
    ),
    (GATE + 2, BX + 2, OUT + 3, BY + 2, GATE + 3, M0 + 1, BX + 3, BX + 4),
    (),
    (GATE + 4, OUT + 4),
    (M1 + 1, BY + 3),
    (BY + 4, M0 + 2, M2 + 0),
    (),
    (M1 + 2,),
    (M2 + 1, M0 + 3, M0 + 4),
    (),
    (M1 + 3,),
    (M2 + 2, M1 + 4, SUM0 + 0),
    (SUM0 + 1,),
    (M2 + 3,),
    (M2 + 4, SUM1 + 0),
    (SUM1 + 1,),
    (),
    (SUM2 + 0,),
)


def forward_kernel(count, reach, *refs):
    (tokens, cot, lengths, cw, cb, gb, dec, g1, g2, w_proj, w_out, w_gate, w_in, w_down,
     out, o_par, o_gain, o_gg2, o_wbx, o_wby, o_wgate, o_wout, o_by, o_fac, o_gx, o_ga, o_sc, o_st, o_bx, o_coded,
     o_mixed, o_u1, o_dmid, o_db, o_part01, o_part2,
     wsmall, wbx, wby, wgate, wout, wm, bx, by, fac, dr, pq, gx, ga, sc, ubuf, coded, mixed, dup,
     since, rate, xh, ssmall, rsmall, sproj, rproj, sout, rout, sgate, rgate, smlp, rmlp, hin, mine, inbox, m_r0, m_ra,
     gs, gr, ps, pr, hs, hr, cs, cr, rs, rr, osem, free) = refs
    p = Place()
    me = p.me
    rows, width = tokens.shape
    core0 = p.core == 0

    xh[...] = jnp.zeros_like(xh)
    inbox[...] = jnp.zeros_like(inbox)
    fac[:, rows:, :] = jnp.ones((8, PAD, 128), F32)
    dr[:, rows + 8 :, :] = jnp.zeros((8, PAD, 128), F32)
    entry_barrier(p, count, reach)

    halo = remote(tokens.at[rows - 16 : rows], xh, hs.at[0], hr.at[0], me + 1)

    @pl.when(me + 1 < count)
    def _():
        halo.start()

    lane = lax.broadcasted_iota(jnp.int32, (32, 128), 1)
    row = lax.broadcasted_iota(jnp.int32, (32, 128), 0)
    spot = jnp.where(lane == lax.rem(me, 4) * 32 + row, 1.0, 0.0).astype(BF16)
    gcol = lax.broadcasted_iota(jnp.int32, (24, width), 1)
    grow = lax.broadcasted_iota(jnp.int32, (24, width), 0)
    gspot = jnp.where(gcol == me * 24 + grow, 1.0, 0.0).astype(BF16)
    ssmall[...] = jnp.zeros_like(ssmall)
    ssmall[0:4, :] = nn(cw[...], spot)
    ssmall[4:5, :] = nn(cb[...], spot)
    ssmall[5:7, :] = nn(gb[...], spot)
    ssmall[7:8, :] = nn(dec[...], spot)
    r1, r2 = nn(g1[...], gspot), nn(g2[...], gspot)
    for j in range(width // 128):
        ssmall[8 + j : 9 + j, :] = r1[:, j * 128 : (j + 1) * 128]
        ssmall[16 + j : 17 + j, :] = r2[:, j * 128 : (j + 1) * 128]
    trades = [
        remote(ssmall, rsmall, ps.at[0], pr.at[0], p.pc),
        remote(sproj.at[0, p.other], rproj.at[0], ps.at[1], pr.at[1], p.pc),
        remote(sgate.at[p.other], rgate, ps.at[2], pr.at[2], p.pc),
        remote(sproj.at[1, p.other], rproj.at[1], ps.at[3], pr.at[3], p.pc),
        remote(sout.at[p.other], rout, ps.at[4], pr.at[4], p.pc),
        remote(smlp.at[p.other], rmlp, ps.at[5], pr.at[5], p.pc),
    ]
    trades[0].start()
    for h in range(2):
        sgate[h] = w_gate[:, h * 256 : (h + 1) * 256].astype(F32)
    trades[2].start()
    for h in range(2):
        sout[h] = w_out[:, h * 512 : (h + 1) * 512].astype(F32)
    trades[4].start()
    for n in range(2):
        for h in range(2):
            lo = n * 1024 + h * 512
            sproj[n, h] = w_proj[:, lo : lo + 512].astype(F32)
        trades[1 + 2 * n].start()
    smlp[0] = w_in[:, :1152].astype(F32)
    smlp[1] = jnp.concatenate([w_in[:, 1152:], w_down[...]], axis=1).astype(F32)
    trades[5].start()

    moves = {
        name: Gather(p, w, gs.at[i], gr.at[i])
        for i, (name, w) in enumerate((
            (SMALL, wsmall), (BX, wbx), (GATE, wgate), (BY, wby), (OUT, wout), (M0, wm.at[0]), (M1, wm.at[1]),
            (M2, wm.at[2])))
    }
    bufs = (m_r0, m_ra, None, None, None, None)
    red = [
        Reduce(p, wm.at[k], wm, (k, p.core), bufs, ((k % 2,),) + tuple((k,) if k < n else None for n in (2, 0, 0, 0, 0)),
               rs.at[k], rr.at[k])
        for k in range(3)
    ]

    moves.update({SUM0: red[0], SUM1: red[1], SUM2: red[2]})
    points = iter(FORWARD_ORDER)

    def at_point():
        for step in next(points):
            if step == SUM2:
                pl.semaphore_wait(free, 1)
            moves[step // 10 * 10].stage(step % 10)
            if step == SUM0 + 1:
                pl.semaphore_signal(free, inc=1, device_id=(p.pc,), device_id_type=MESH)

    def slab(mine_, theirs):
        first = jnp.where(core0, mine_, theirs)
        second = jnp.where(core0, theirs, mine_)
        return jnp.concatenate([first, second], axis=0).astype(BF16)

    trades[0].wait_recv()
    both = ssmall[...] + rsmall[...]
    wsmall[p.core, p.yx, p.z] = jnp.where(core0, both[0:16], both[16:32]).astype(BF16)
    moves[SMALL].stage(0)
    trades[2].wait_recv()
    wgate[p.core, p.yx, p.z] = slab(sgate[p.core], rgate[...])
    moves[GATE].stage(0)
    trades[4].wait_recv()
    wout[p.core, p.yx, p.z] = slab(sout[p.core], rout[...])
    moves[OUT].stage(0)
    trades[1].wait_recv()
    wbx[p.core, p.yx, p.z] = slab(sproj[0, p.core], rproj[0])
    trades[3].wait_recv()
    wby[p.core, p.yx, p.z] = slab(sproj[1, p.core], rproj[1])
    trades[5].wait_recv()
    for k in range(3):
        wm[k, p.core, p.yx, p.z] = slab(smlp[p.core, 24 * k : 24 * k + 24, :], rmlp[24 * k : 24 * k + 24, :])

    at_point()
    outs = []

    def save(src, dst):
        c = pltpu.make_async_copy(src, dst, osem.at[len(outs)])
        c.start()
        outs.append(c)
        return c

    since[...] = sequence_offset(lengths, me * rows, rows)
    at_point()
    for t in trades:
        t.wait_send()

    for g in range(8):
        z_, yx_ = g // 2, 2 * (g % 2)
        o_par[g] = wsmall[0, yx_, z_].astype(F32)[0:8] + wsmall[0, yx_ + 1, z_].astype(F32)[0:8]
        rate[g] = -8.0 * softplus(o_par[g])
    gsum = [jnp.zeros((8, 128), F32), jnp.zeros((8, 128), F32)]
    for z_ in range(4):
        for yx_ in range(4):
            gsum[0] = gsum[0] + wsmall[0, yx_, z_].astype(F32)[8:16]
            gsum[1] = gsum[1] + wsmall[1, yx_, z_].astype(F32)[0:8]
    o_gain[...] = jnp.zeros_like(o_gain)
    for n in range(2):
        for j in range(width // 128):
            o_gain[n : n + 1, j * 128 : (j + 1) * 128] = gsum[n][j : j + 1]

    @pl.when(me + 1 < count)
    def _():
        halo.wait_send()

    @pl.when(me > 0)
    def _():
        halo.wait_recv()

    def norm_rows(x, n):
        inv = lax.rsqrt(jnp.mean(x * x, axis=1, keepdims=True) + EPSILON)
        return (x * inv * o_gain[n : n + 1, :]).astype(BF16)

    ubuf[0:16, :] = norm_rows(xh[...].astype(F32), 0)

    def norm_one(r0):
        ubuf[pl.ds(r0 + 16, 32), :] = norm_rows(tokens[pl.ds(r0, 32), :].astype(F32), 0)

    rows_loop(rows, 32, norm_one)
    saved_u1 = save(ubuf.at[16 : rows + 16], o_u1)
    at_point()

    def project_x(h, c):
        cols = pl.ds(pl.multiple_of(lax.rem(h, 2) * 256, 256), 256)
        v = nn(ubuf[...], chips(wbx[lax.div(h, 2), :, :, :, cols])).astype(BF16).astype(F32)
        bx[2 * h], bx[2 * h + 1] = v[:, :128], v[:, 128:]
        return c

    def project_y(h, c):
        cols = pl.ds(pl.multiple_of(lax.rem(h, 2) * 256, 256), 256)
        v = nn(ubuf[16:, :], chips(wby[lax.div(h, 2), :, :, :, cols]))
        by[2 * h], by[2 * h + 1] = v[:, :128], v[:, 128:]
        return c

    lax.fori_loop(0, 4, project_x, 0)
    saved_bx = save(bx, o_bx)
    save(wbx, o_wbx)
    at_point()

    def conv(g, r0):
        par = o_par[g]
        v = bx[g, pl.ds(r0 + 8, 72), :]
        off = since[pl.ds(r0, 64), :]
        total = par[4:5] + par[0:1] * v[8:72]
        for k in range(1, 4):
            total = total + par[k : k + 1] * jnp.where(off >= k, v[8 - k : 72 - k], 0.0)
        coded[g, pl.ds(r0, 64), :] = total.astype(BF16)

    blocks_loop(8, rows, 64, conv)
    saved_c = save(coded, o_coded)
    at_point()
    save(wgate, o_wgate)

    def gate_dots(h, c):
        left = lanes(coded, 2 * h, 0, rows)
        v = nn(left, wgate[0, :, h].reshape(256, 256))
        gx[2 * h], gx[2 * h + 1] = v[:, :128], v[:, 128:]
        v = nn(left, wgate[1, :, h].reshape(256, 256))
        ga[2 * h], ga[2 * h + 1] = v[:, :128], v[:, 128:]
        return c

    lax.fori_loop(0, 4, gate_dots, 0)
    at_point()

    def gates(g, r0):
        par = o_par[g]
        at = pl.ds(r0, 64)
        fresh = since[at, :] == 0
        gate_x = jax.nn.sigmoid(gx[g, at, :] + par[5:6])
        gate_a = jax.nn.sigmoid(ga[g, at, :] + par[6:7])
        log_a = gate_a * rate[g, 7:8, :]
        decay = jnp.exp(log_a)
        factor = jnp.where(fresh, 0.0, decay)
        scale = jnp.where(fresh, 1.0, root_of(one_minus_square(2.0 * log_a, decay)))
        gx[g, at, :] = gate_x
        ga[g, at, :] = gate_a
        fac[g, at, :] = factor
        sc[g, at, :] = scale
        dr[g, pl.ds(r0 + 8, 64), :] = scale * gate_x * coded[g, at, :].astype(F32)

    blocks_loop(8, rows, 64, gates)
    saved = [save(gx, o_gx), save(ga, o_ga), save(fac.at[:, 0:rows], o_fac), save(sc, o_sc)]
    at_point()
    ends = scan_segments(fac, dr, pq, 0, 8, 0, False)
    _, leave = chain(ends, [jnp.zeros((1, 128), F32)] * 8, False)
    whole = products(ends)
    for g in range(8):
        mine[0, g : g + 1, :] = whole[g]
        mine[1, g : g + 1, :] = leave[g]
    carry_send(p, count, reach, 1, mine, inbox, cs, cr)
    lax.fori_loop(0, 4, project_y, 0)
    save(by, o_by)
    save(wby, o_wby)
    at_point()
    carry_wait(p, count, reach, 1, mine, inbox, cs, cr)
    enter = carry_fold(p, count, reach, 1, inbox)
    inside, _ = chain(ends, enter, False)
    for g in range(8):
        hin[g] = inside[g]
        dr[g, 0:8, :] = jnp.broadcast_to(enter[g], (8, 128))
    step = rows // SEG

    def states(g, c):
        inside_g = hin[g]
        for s in range(SEG):
            lo = s * step
            st = dr[g, lo + 8 : lo + 8 + step, :] + pq[g, lo : lo + step, :] * segment_rows(inside_g, s, step)
            dr[g, lo + 8 : lo + 8 + step, :] = st
            mixed[g, lo : lo + step, :] = (st * gelu(by[g, lo : lo + step, :])).astype(BF16)
        return c

    lax.fori_loop(0, 8, states, 0)
    saved.append(save(dr.at[:, 0 : rows + 8], o_st))
    saved.append(save(mixed, o_mixed))
    at_point()
    save(wout, o_wout)
    for c in (saved_bx, saved_u1, saved_c):
        c.wait()
    middle = bx
    v = nt(wide(mixed, 4, 0, rows), chips(wout[0])) + nt(
        jnp.concatenate([mixed[g] for g in range(4, 8)], axis=1), chips(wout[1])
    )

    put(middle, v, 0, 0)

    def norm_two(r0):
        at = pl.ds(r0, 32)
        m = wide(middle, 6, r0, 32) + tokens[at, :].astype(F32)
        for g in range(6):
            middle[g, at, :] = m[:, g * 128 : (g + 1) * 128]
        ubuf[at, :] = norm_rows(m, 1)

    rows_loop(rows, 32, norm_two)
    at_point()
    for c in saved:
        c.wait()
    fg, fu, fd, acc_out, acc_du = gx, ga, pq, sc, fac
    hid, dgate = coded, mixed

    for k in range(3):
        w0 = flat(wm[k, 0])
        w1 = flat(wm[k, 1])
        wg, wu, wd = w0[:, :768], jnp.concatenate([w0[:, 768:], w1[:, :384]], axis=1), w1[:, 384:]
        put(fg, nt(ubuf[0:rows, :], wg), 0, 0)
        put(fu, nt(ubuf[0:rows, :], wu), 0, 0)
        put(fd, nt(cot[...], wd), 0, 0)

        def glu(r0):
            at = pl.ds(r0, 32)
            for g in range(6):
                act, slope = gelu_parts(fg[g, at, :])
                up, dh = fu[g, at, :], fd[g, at, :]
                hid[g, at, :] = (act * up).astype(BF16)
                dgate[g, at, :] = (dh * up * slope).astype(BF16)
                dup[g, at, :] = (dh * act).astype(BF16)

        rows_loop(rows, 32, glu)
        at_point()
        v_hid, v_dg, v_dup = (wide(t, 6, 0, rows) for t in (hid, dgate, dup))
        v = nn(v_hid, wd)
        v2 = nn(v_dg, wg) + nn(v_dup, wu)
        for g in range(6):
            cols = slice(g * 128, (g + 1) * 128)
            if k == 0:
                acc_out[g, 0:rows, :] = v[:, cols]
                acc_du[g, 0:rows, :] = v2[:, cols]
            else:
                acc_out[g, 0:rows, :] += v[:, cols]
                acc_du[g, 0:rows, :] += v2[:, cols]
        at_point()
        gg = tn(v_dg, ubuf[0:rows, :]).astype(BF16)
        gu = tn(v_dup, ubuf[0:rows, :]).astype(BF16)
        gd = tn(v_hid, cot[...]).astype(BF16)
        wm[k, 0, :, :, :, 0:768] = gg.reshape(4, 4, 48, 768)
        wm[k, 0, :, :, :, 768:1152] = gu[:, :384].reshape(4, 4, 48, 384)
        wm[k, 1, :, :, :, 0:384] = gu[:, 384:].reshape(4, 4, 48, 384)
        wm[k, 1, :, :, :, 384:1152] = gd.reshape(4, 4, 48, 768)
        at_point()

    o_gg2[...] = jnp.zeros_like(o_gg2)

    def finish(r0):
        at = pl.ds(r0, 32)
        m, c = wide(middle, 6, r0, 32), cot[at, :].astype(F32)
        out[at, :] = (m + wide(acc_out, 6, r0, 32)).astype(BF16)
        du = wide(acc_du, 6, r0, 32)
        inv = lax.rsqrt(jnp.mean(m * m, axis=1, keepdims=True) + EPSILON)
        o_gg2[...] += fold8(du * m * inv)
        gd_ = du * o_gain[1:2, :]
        back = jnp.mean(gd_ * m, axis=1, keepdims=True)
        dm = c + inv * gd_ - m * (inv * inv * inv * back)
        ubuf[at, :] = dm.astype(BF16)
        for g in range(6):
            acc_out[g, at, :] = dm[:, g * 128 : (g + 1) * 128]

    rows_loop(rows, 32, finish)
    save(acc_out.at[0:6], o_dmid)
    save(ubuf.at[0:rows], o_db)
    for k in range(2):
        red[k].take(1)
        save(wm.at[k, p.core, p.yx], o_part01.at[k, 0])
        save(wm.at[k, p.core, p.gb], o_part01.at[k, 1])
    red[2].take(0)
    save(wm.at[2, p.core], o_part2)
    red[0].close(0, 1, 2)
    red[1].close(0, 1, 2)
    red[2].close(0)
    for c in outs:
        if not any(c is s for s in saved + [saved_bx, saved_u1, saved_c]):
            c.wait()


def forward_call(count, reach, args):
    tokens = args[0]
    rows, width = tokens.shape
    S = jax.ShapeDtypeStruct
    page = (8, rows, 128)
    outs = [
        (S((rows, width), BF16), VM),
        (S((8, 8, 128), F32), VM),
        (S((8, width), F32), VM),
        (S((8, width), F32), VM),
        (S((2, 4, 4, 48, 512), BF16), ANY),
        (S((2, 4, 4, 48, 512), BF16), ANY),
        (S((2, 4, 4, 64, 256), BF16), ANY),
        (S((2, 4, 4, 48, 512), BF16), ANY),
        (S(page, F32), ANY),
        (S(page, F32), ANY),
        (S(page, F32), ANY),
        (S(page, F32), ANY),
        (S(page, F32), ANY),
        (S((8, rows + 8, 128), F32), ANY),
        (S((8, rows + 16, 128), F32), ANY),
        (S(page, BF16), ANY),
        (S(page, BF16), ANY),
        (S((rows, width), BF16), ANY),
        (S((6, rows, 128), F32), ANY),
        (S((rows, width), BF16), ANY),
        (S((2, 2, 4, 48, 1152), BF16), ANY),
        (S((4, 4, 48, 1152), BF16), ANY),
    ]
    V = pltpu.VMEM
    dma = pltpu.SemaphoreType.DMA
    scratch = [
        V((2, 4, 4, 16, 128), BF16),
        V((2, 4, 4, 48, 512), BF16),
        V((2, 4, 4, 48, 512), BF16),
        V((2, 4, 4, 64, 256), BF16),
        V((2, 4, 4, 48, 512), BF16),
        V((3, 2, 4, 4, 48, 1152), BF16),
        V((8, rows + 16, 128), F32),
        V(page, F32),
        V((8, rows + PAD, 128), F32),
        V((8, rows + 8 + PAD, 128), F32),
        V((8, rows + PAD, 128), F32),
        V(page, F32),
        V(page, F32),
        V(page, F32),
        V((rows + 16, width), BF16),
        V(page, BF16),
        V(page, BF16),
        V(page, BF16),
        V((rows, 128), jnp.int32),
        V((8, 8, 128), F32),
        V((16, width), BF16),
        V((32, 128), F32),
        V((32, 128), F32),
        V((2, 2, 24, 512), F32),
        V((2, 24, 512), F32),
        V((2, 24, 512), F32),
        V((24, 512), F32),
        V((2, 32, 256), F32),
        V((32, 256), F32),
        V((2, 72, 1152), F32),
        V((72, 1152), F32),
        V((8, 8, 128), F32),
        V((2, 8, 128), F32),
        V((reach, 2, 8, 128), F32),
        V((2, 4, 4, 48, 1152), BF16),
        V((2, 2, 4, 48, 1152), BF16),
        dma((8, 10)),
        dma((8, 10)),
        dma((6,)),
        dma((6,)),
        dma((1,)),
        dma((1,)),
        dma((reach,)),
        dma((reach,)),
        dma((3, 8)),
        dma((3, 8)),
        dma((24,)),
        pltpu.SemaphoreType.REGULAR,
    ]
    return pl.pallas_call(
        functools.partial(forward_kernel, count, reach),
        out_shape=[o[0] for o in outs],
        in_specs=[VM, VM, SM] + [VM] * 11,
        out_specs=[o[1] for o in outs],
        scratch_shapes=scratch,
        name="forward",
        cost_estimate=pl.CostEstimate(flops=25 * 10**9, bytes_accessed=60 * 10**6, transcendentals=10**7),
        compiler_params=pltpu.CompilerParams(
            collective_id=0, has_side_effects=True, vmem_limit_bytes=62 * MIB
        ),
    )(*args)


class Reduce:
    def __init__(self, p, part, whole, own_lead, bufs, leads, ssem, rsem, groups=None):
        self.p, self.part = p, part
        self.whole, self.own_lead, self.bufs, self.leads = whole, own_lead, bufs, leads
        self.ssem, self.rsem = ssem, rsem
        self.gyx, self.gb = groups or (p.yx, p.gb)

    def own(self, *index):
        return self.whole.at[self.own_lead + index]

    def buf(self, which, *index):
        at = self.leads[which] + index
        return self.bufs[which].at[at] if at else self.bufs[which]

    def copy(self, slot):
        p = self.p
        src, dst, dev = (
            (lambda: (self.part.at[p.other], self.buf(0), p.pc)),
            (lambda: (self.own(p.gd), self.buf(1, 1), p.pa)),
            (lambda: (self.own(p.ga), self.buf(1, 0), p.pa)),
            (lambda: (self.own(self.gb), self.buf(2), p.pb)),
            (lambda: (self.own(self.gyx, p.zs[0]), self.buf(3, 0), p.pz[0])),
            (lambda: (self.own(self.gyx, p.zs[1]), self.buf(3, 1), p.pz[1])),
            (lambda: (self.own(self.gyx, p.zs[2]), self.buf(3, 2), p.pz[2])),
            (lambda: (self.buf(4, p.other), self.buf(5), p.pc)),
        )[slot]()
        return remote(src, dst, self.ssem.at[slot], self.rsem.at[slot], dev)

    def add(self, group, which, *index):
        for z in range(4):
            at = self.own_lead + (group, z)
            other = self.bufs[which][self.leads[which] + index + (z,)]
            self.whole[at] = (self.whole[at].astype(F32) + other.astype(F32)).astype(BF16)

    def take(self, n, send=False):
        p = self.p
        if n == 0:
            self.copy(0).wait_recv()
            for group, slot in ((p.gd, 1), (p.ga, 2)):
                self.add(group, 0, group)
                if send:
                    self.copy(slot).start()
            for group in (self.gb, self.gyx):
                self.add(group, 0, group)
        elif n == 1:
            self.copy(1).wait_recv()
            self.add(self.gb, 1, 1)
            if send:
                self.copy(3).start()
            self.copy(2).wait_recv()
            self.add(self.gyx, 1, 0)
        elif n == 2:
            self.copy(3).wait_recv()
            self.add(self.gyx, 2)
            if send:
                self.send(3)
        elif n == 3:
            total = self.whole[self.own_lead + (self.gyx, p.z)].astype(F32)
            for d in range(3):
                self.copy(4 + d).wait_recv()
                total = total + self.bufs[3][self.leads[3] + (d,)].astype(F32)
            half = total.shape[0] // 2
            self.bufs[4][self.leads[4] + (0,)] = total[:half]
            self.bufs[4][self.leads[4] + (1,)] = total[half:]
            if send:
                self.send(4)

    def send(self, n):
        for slot in ((0,), (1, 2), (3,), (4, 5, 6), (7,))[n]:
            self.copy(slot).start()

    def close(self, *slots):
        for s in slots:
            self.copy(s).wait_send()

    def stage(self, n, first=0):
        if n == 0:
            self.send(0)
        elif n < 5:
            self.take(n - 1, True)
        else:
            p = self.p
            self.copy(7).wait_recv()
            mine, theirs = self.bufs[4][self.leads[4] + (p.core,)], self.bufs[5][self.leads[5] + (...,)]
            left = jnp.where(p.core == 0, mine, theirs)
            right = jnp.where(p.core == 0, theirs, mine)
            self.close(*range(first, 8))
            return left, right


class Totals:
    def __init__(self, p, v, bufs, ssem, rsem):
        self.p, self.v, self.bufs, self.ssem, self.rsem = p, v, bufs, ssem, rsem

    def copy(self, slot):
        p = self.p
        dev = ([p.pc, p.pa, p.pb] + p.pz)[slot]
        return remote(self.v.at[min(slot, 3)], self.bufs.at[slot], self.ssem.at[slot], self.rsem.at[slot], dev)

    def stage(self, n):
        if n < 3:
            self.copy(n).start()
        if n == 3:
            for s in (3, 4, 5):
                self.copy(s).start()

    def step(self, n):
        if n < 3:
            self.copy(n).wait_recv()
            self.v[n + 1] = self.v[n] + self.bufs[n]
            return None
        total = self.v[3]
        for s in (3, 4, 5):
            self.copy(s).wait_recv()
            total = total + self.bufs[s]
        for s in range(6):
            self.copy(s).wait_send()
        return total


BACKWARD_ORDER = (
    (M0 + 2, M1 + 2),
    (M2 + 1,),
    (),
    (),
    (OUT + 0, M0 + 3),
    (BY + 0,),
    (OUT + 1, M1 + 3),
    (M2 + 2, BY + 1),
    (GATE + 0, OUT + 2),
    (M2 + 3, GATE + 1),
    (BY + 2,),
    (BX + 0, OUT + 3),
    (BX + 1, GATE + 2, BY + 3),
    (TOT + 0, BX + 2, M0 + 4, M1 + 4),
    (
        TOT + 1, GATE + 3, M0 + 5, M1 + 5, M2 + 4, BX + 3, TOT + 2, OUT + 4, BY + 4, TOT + 3, M2 + 5, OUT + 5,
        BY + 5, GATE + 4, GATE + 5, BX + 4, TOT + 4, BX + 5,
    ),
)


def backward_kernel(count, reach, *refs):
    (tokens, lengths, par, gain, gg2, i_wbx, i_wby, i_wgate, i_wout, i_by, i_fac, i_gx, i_ga, i_sc, i_st, i_bx, i_coded,
     i_mixed, i_u1, i_dmid, i_db, i_part01, i_part2,
     grad_tokens, o_proj, o_out, o_gate, o_in, o_down, o_cw, o_cb, o_gb, o_dec, o_g1, o_g2,
     wbx, wby, wgate, wout, adj, fac, st, pp, gslot, coded, mixed, u1, db, dby, dgx, since,
     own01, own2, gout, gpy, gpx, ggate,
     m_ra, m_rb, m_rz, m_tot, m_rc, p_r0, p_ra, p_rb, p_rz, p_tot, p_rc, t_r0, t_ra, t_rb, t_rz, t_tot, t_rc,
     edge, sums, gsum, vsum, vbuf, hin, mine, inbox,
     rs, rr, vs, vr, cs, cr, es, er, isem, gsem, lsem) = refs
    p = Place()
    me = p.me
    rows, width = tokens.shape

    inbox[...] = jnp.zeros_like(inbox)
    edge[...] = jnp.zeros_like(edge)
    def fetch(g, slot):
        return [
            pltpu.make_async_copy(src.at[g], gslot.at[slot, i, 0:rows], gsem.at[slot, i])
            for i, src in enumerate((i_gx, i_ga, i_sc))
        ]

    def fetch_bx(g, slot):
        return pltpu.make_async_copy(i_bx.at[g], gslot.at[slot, 0], gsem.at[slot, 3])

    parts = [
        pltpu.make_async_copy(i_part01, own01, lsem.at[0]),
        pltpu.make_async_copy(i_part2, own2, lsem.at[1]),
    ]
    parts[0].start()
    (load_db, load_wout, load_by, load_st, load_fac, load_mixed, load_u1, load_coded, load_wgate, load_wby, load_wbx) = loads = [
        pltpu.make_async_copy(src, dst, isem.at[i])
        for i, (src, dst) in enumerate((
            (i_db, db), (i_wout, wout), (i_by, adj.at[:, 0:rows]), (i_st, st), (i_fac, fac.at[:, 0:rows]), (i_mixed, mixed),
            (i_u1, u1), (i_coded, coded), (i_wgate, wgate), (i_wby, wby), (i_wbx, wbx)))
    ]
    for c in loads[:5] + parts[1:] + loads[5:7] + [c for g in range(SLOTS - 1) for c in fetch(g, g)] + loads[7:]:
        c.start()
    entry_barrier(p, count, reach)

    mbufs = (None, m_ra, m_rb, m_rz, m_tot, m_rc)
    red_m = [
        Reduce(p, None, own, lead, mbufs, (None, (), (k,), (k,), (k,), (k,)), rs.at[k], rr.at[k], groups)
        for k, own, lead, groups in ((0, own01, (0,), (0, 1)), (1, own01, (1,), (0, 1)), (2, own2, (), None))
    ]
    pbufs = (p_r0, p_ra, p_rb, p_rz, p_tot, p_rc)
    red_out, red_py, red_px = [
        Reduce(p, g, g, (p.core,), pbufs, ((k,),) * 6, rs.at[3 + k], rr.at[3 + k]) for k, g in enumerate((gout, gpy, gpx))
    ]
    red_gate = Reduce(
        p, ggate, ggate, (p.core,), (t_r0, t_ra, t_rb, t_rz, t_tot, t_rc), ((),) * 6, rs.at[6], rr.at[6]
    )

    since[...] = sequence_offset(lengths, me * rows, rows + 8)
    sums[...] = jnp.zeros_like(sums)
    gsum[...] = jnp.zeros_like(gsum)

    tot = Totals(p, vsum, vbuf, vs, vr)
    sums_of = {M0: red_m[0], M1: red_m[1], M2: red_m[2], OUT: red_out, BY: red_py, BX: red_px, GATE: red_gate}
    began = {M0: 2, M1: 2, M2: 1}
    points = iter(BACKWARD_ORDER)

    def write(name, left, right):
        if name in began:
            lo = 24 * ((name - M0) // 10)
            o_in[lo : lo + 24, 0:1152] = left
            o_in[lo : lo + 24, 1152:1536] = right[:, :384]
            o_down[lo : lo + 24, :] = right[:, 384:]
        elif name == OUT:
            o_out[:, :512], o_out[:, 512:] = left, right
        elif name == BY:
            o_proj[:, 1024:1536], o_proj[:, 1536:2048] = left, right
        elif name == BX:
            o_proj[:, 0:512], o_proj[:, 512:1024] = left, right
        else:
            o_gate[:, :256], o_gate[:, 256:] = left, right

    def write_totals(total):
        chan = pltpu.roll(total[0:8], lax.rem(1024 - 32 * me, 1024), 1)
        o_cw[...] = chan[0:4, 0:32]
        o_cb[...] = chan[4:5, 0:32]
        o_gb[...] = chan[5:7, 0:32]
        o_dec[...] = chan[7:8, 0:32]
        gains = pltpu.roll(total[8:16], lax.rem(1024 - 24 * me, 1024), 1)
        o_g1[...] = gains[0:1, 0:24]
        o_g2[...] = gains[1:2, 0:24]

    def at_point():
        for step in next(points):
            name, n = step // 10 * 10, step % 10
            if name == TOT:
                total = tot.step(n - 1) if n > 0 else None
                if n < 4:
                    tot.stage(n)
                else:
                    write_totals(total)
            elif n == began.get(name):
                sums_of[name].send(n)
            elif n < 5:
                sums_of[name].stage(n)
            else:
                first = began.get(name, 0)
                write(name, *sums_of[name].stage(5, (0, 1, 3)[first]))

    parts[0].wait()
    at_point()
    load_db.wait()
    load_wout.wait()

    def mix_dots(h, c):
        cols = pl.ds(pl.multiple_of(lax.rem(h, 2) * 256, 256), 256)
        v = nn(db[...], chips(wout[lax.div(h, 2), :, :, :, cols]))
        pp[2 * h, 0:rows, :], pp[2 * h + 1, 0:rows, :] = v[:, :128], v[:, 128:]
        return c

    lax.fori_loop(0, 4, mix_dots, 0)
    parts[1].wait()
    at_point()
    load_by.wait()
    load_st.wait()

    def branch_y(g, r0):
        at = pl.ds(r0, 64)
        dm = pp[g, at, :]
        act, slope = gelu_parts(adj[g, at, :])
        adj[g, at, :] = dm * act
        dby[g, at, :] = (dm * st[g, pl.ds(r0 + 8, 64), :] * slope).astype(BF16)

    blocks_loop(8, rows, 64, branch_y)
    at_point()
    load_fac.wait()
    fac[:, rows:, :] = jnp.ones((8, PAD, 128), F32)
    adj[:, rows:, :] = jnp.zeros((8, PAD, 128), F32)
    ends = scan_segments(fac, adj, pp, 0, 0, 0, True)
    _, leave = chain(ends, [jnp.zeros((1, 128), F32)] * 8, True)
    whole = products(ends)
    for g in range(8):
        mine[0, g : g + 1, :] = whole[g]
        mine[1, g : g + 1, :] = leave[g]
    carry_send(p, count, reach, -1, mine, inbox, cs, cr)
    at_point()
    load_mixed.wait()

    def halves(target, left, page):
        for h in range(2):
            v = tn(left, jnp.concatenate([page[4 * h + i] for i in range(4)], axis=1))
            put_chips(target, h, v.astype(BF16))

    halves(gout, db[...], mixed)
    at_point()
    load_u1.wait()
    halves(gpy, u1[...], dby)
    at_point()
    carry_wait(p, count, reach, -1, mine, inbox, cs, cr)
    inside, _ = chain(ends, carry_fold(p, count, reach, -1, inbox), True)
    for g in range(8):
        hin[g] = inside[g]
    step = rows // SEG

    def adjoint(g, c):
        inside_g = hin[g]
        for s in range(SEG):
            lo = s * step
            adj[g, lo : lo + step, :] += pp[g, lo : lo + step, :] * segment_rows(inside_g, s, step)
        return c

    lax.fori_loop(0, 8, adjoint, 0)
    at_point()
    load_coded.wait()
    dga = mixed

    def gate_back(g, slot, last):
        @pl.when(jnp.logical_not(last))
        def _():
            for c_ in fetch(g + SLOTS - 1, (slot + SLOTS - 1) % SLOTS):
                c_.start()

        for c_ in fetch(g, slot):
            c_.wait()
        row = par[g]
        sp8 = -8.0 * softplus(row[7:8])

        def block(i, acc):
            r0 = pl.multiple_of(i * 64, 64)
            at = pl.ds(r0, 64)
            a, f = adj[g, at, :], fac[g, at, :]
            gate_x, gate_a, scale = gslot[slot, 0, at, :], gslot[slot, 1, at, :], gslot[slot, 2, at, :]
            code = coded[g, at, :].astype(F32)
            before = st[g, pl.ds(r0, 72), :][7:71]
            d_log = a * f * (before - gate_x * code * f / scale)
            d_a = d_log * gate_a
            d_ga = d_a * sp8 * (1.0 - gate_a)
            d_part = a * scale * gate_x
            d_gx = d_part * code * (1.0 - gate_x)
            dgx[g, at, :] = d_gx.astype(BF16)
            dga[g, at, :] = d_ga.astype(BF16)
            adj[g, at, :] = d_part
            return acc[0] + fold8(d_gx), acc[1] + fold8(d_ga), acc[2] + fold8(d_a)

        zero = jnp.zeros((8, 128), F32)
        acc = lax.fori_loop(0, rows // 64, block, (zero, zero, zero))
        slope = jax.nn.sigmoid(row[7:8])
        sums[g, 5:6, :] = jnp.sum(acc[0], axis=0, keepdims=True)
        sums[g, 6:7, :] = jnp.sum(acc[1], axis=0, keepdims=True)
        sums[g, 7:8, :] = jnp.sum(acc[2], axis=0, keepdims=True) * (-8.0 * slope)

    slots_loop(gate_back)
    for g in range(SLOTS - 1):
        fetch_bx(g, g).start()
    load_dmid = pltpu.make_async_copy(i_dmid, st.at[0:6, 0:rows], isem.at[11])
    load_dmid.start()
    dbx = dgx
    at_point()
    load_wgate.wait()

    def gate_dots(h, c):
        dx, da, code = lanes(dgx, 2 * h, 0, rows), lanes(dga, 2 * h, 0, rows), lanes(coded, 2 * h, 0, rows)
        v = nt(dx, wgate[0, :, h].reshape(256, 256)) + nt(da, wgate[1, :, h].reshape(256, 256))
        adj[2 * h, 0:rows, :] += v[:, :128]
        adj[2 * h + 1, 0:rows, :] += v[:, 128:]
        ggate[0, :, h] = tn(code, dx).astype(BF16).reshape(4, 64, 256)
        ggate[1, :, h] = tn(code, da).astype(BF16).reshape(4, 64, 256)
        return c

    lax.fori_loop(0, 4, gate_dots, 0)
    edge[0] = adj[:, 0:8, :]
    to_prev = remote(edge.at[0], edge.at[1], es.at[0], er.at[0], me - 1)

    @pl.when(me > 0)
    def _():
        to_prev.start()

    at_point()
    load_wby.wait()
    put(pp, nt(jnp.concatenate([dby[g] for g in range(8)], axis=1), whole_w(wby)), 0, 0)
    at_point()

    @pl.when(me > 0)
    def _():
        to_prev.wait_send()

    @pl.when(me + 1 < count)
    def _():
        to_prev.wait_recv()

    adj[:, rows : rows + 8, :] = edge[1]

    def conv_back(g, slot, last):
        @pl.when(jnp.logical_not(last))
        def _():
            fetch_bx(g + SLOTS - 1, (slot + SLOTS - 1) % SLOTS).start()

        fetch_bx(g, slot).wait()
        row = par[g]

        def block(i, acc):
            r0 = pl.multiple_of(i * 64, 64)
            d = adj[g, pl.ds(r0, 72), :]
            off = since[pl.ds(r0, 72), :]
            b = gslot[slot, 0, pl.ds(r0 + 8, 72), :]
            own, off0 = d[0:64], off[0:64]
            total = row[0:1] * own
            out = [acc[0] + fold8(own * b[8:72])]
            for k in range(1, 4):
                total = total + row[k : k + 1] * jnp.where(off[k : 64 + k] >= k, d[k : 64 + k], 0.0)
                out.append(acc[k] + fold8(own * jnp.where(off0 >= k, b[8 - k : 72 - k], 0.0)))
            out.append(acc[4] + fold8(own))
            dbx[g, pl.ds(r0, 64), :] = total.astype(BF16)
            return tuple(out)

        acc = lax.fori_loop(0, rows // 64, block, tuple(jnp.zeros((8, 128), F32) for _ in range(5)))
        for k in range(5):
            sums[g, k : k + 1, :] = jnp.sum(acc[k], axis=0, keepdims=True)

    slots_loop(conv_back)
    at_point()
    halves(gpx, u1[...], dbx)
    at_point()
    load_wbx.wait()
    du = nt(jnp.concatenate([dbx[g] for g in range(8)], axis=1), whole_w(wbx))
    for g in range(6):
        pp[g, 0:rows, :] += du[:, g * 128 : (g + 1) * 128]
    at_point()
    load_dmid.wait()

    def finish(r0):
        at = pl.ds(r0, 32)
        x = tokens[at, :].astype(F32)
        d = wide(pp, 6, r0, 32)
        inv = lax.rsqrt(jnp.mean(x * x, axis=1, keepdims=True) + EPSILON)
        gsum[...] += fold8(d * x * inv)
        scaled = d * gain[0:1, :]
        back = jnp.mean(scaled * x, axis=1, keepdims=True)
        grad_tokens[at, :] = (wide(st, 6, r0, 32) + inv * scaled - x * (inv * inv * inv * back)).astype(BF16)

    rows_loop(rows, 32, finish)
    vsum[0] = jnp.zeros((16, 1024), F32)
    for g in range(8):
        vsum[0, 0:8, g * 128 : (g + 1) * 128] = sums[g]
    vsum[0, 8:9, 0:width] = jnp.sum(gsum[...], axis=0, keepdims=True)
    vsum[0, 9:10, 0:width] = jnp.sum(gg2[...], axis=0, keepdims=True)
    at_point()
    at_point()


def backward_call(count, reach, args):
    tokens = args[0]
    rows, width = tokens.shape
    S = jax.ShapeDtypeStruct
    V = pltpu.VMEM
    dma = pltpu.SemaphoreType.DMA
    page = (8, rows, 128)
    outs = [
        S((rows, width), BF16), S((24, 2048), F32), S((24, 1024), F32), S((32, 512), F32), S((72, 1536), F32),
        S((72, 768), F32), S((4, 32), F32), S((1, 32), F32), S((2, 32), F32), S((1, 32), F32), S((1, 24), F32),
        S((1, 24), F32),
    ]

    def bufs(n, r, c):
        lead = (n,) if n else ()
        return [V(lead + (4, 4, r, c), BF16), V(lead + (2, 4, r, c), BF16), V(lead + (4, r, c), BF16),
                V(lead + (3, r, c), BF16), V(lead + (2, r // 2, c), F32), V(lead + (r // 2, c), F32)]

    scratch = [
        V((2, 4, 4, 48, 512), BF16), V((2, 4, 4, 48, 512), BF16), V((2, 4, 4, 64, 256), BF16), V((2, 4, 4, 48, 512), BF16),
        V((8, rows + PAD, 128), F32),
        V((8, rows + PAD, 128), F32),
        V((8, rows + 8, 128), F32),
        V((8, rows + PAD, 128), F32),
        V((SLOTS, 3, rows + 16, 128), F32),
        V(page, BF16), V(page, BF16), V((rows, width), BF16), V((rows, width), BF16),
        V(page, BF16), V(page, BF16),
        V((rows + 8, 128), jnp.int32),
        V((2, 2, 4, 48, 1152), BF16), V((4, 4, 48, 1152), BF16),
        V((2, 4, 4, 48, 512), BF16), V((2, 4, 4, 48, 512), BF16), V((2, 4, 4, 48, 512), BF16),
        V((2, 4, 4, 64, 256), BF16),
        V((2, 4, 48, 1152), BF16), *bufs(3, 48, 1152)[2:], *bufs(3, 48, 512), *bufs(0, 64, 256),
        V((2, 8, 8, 128), F32),
        V((8, 8, 128), F32), V((8, width), F32), V((4, 16, 1024), F32), V((6, 16, 1024), F32),
        V((8, 8, 128), F32), V((2, 8, 128), F32), V((reach, 2, 8, 128), F32),
        dma((7, 8)), dma((7, 8)), dma((6,)), dma((6,)), dma((reach,)), dma((reach,)), dma((1,)), dma((1,)),
        dma((12,)), dma((SLOTS, 4)), dma((2,)),
    ]
    return pl.pallas_call(
        functools.partial(backward_kernel, count, reach),
        out_shape=outs,
        in_specs=[VM, SM, VM, VM, VM] + [ANY] * 18,
        out_specs=[VM] * len(outs),
        scratch_shapes=scratch,
        name="backward",
        cost_estimate=pl.CostEstimate(flops=12 * 10**9, bytes_accessed=60 * 10**6, transcendentals=10**7),
        compiler_params=pltpu.CompilerParams(
            collective_id=1, has_side_effects=True, vmem_limit_bytes=63 * MIB
        ),
    )(*args)


def results_kernel(n, *refs):
    for i in range(n):
        refs[n + i][...] = refs[i][...]


def results_call(arrays):
    n = len(arrays)
    return pl.pallas_call(
        functools.partial(results_kernel, n),
        out_shape=[jax.ShapeDtypeStruct(a.shape, a.dtype) for a in arrays],
        in_specs=[VM] * n,
        out_specs=[VM] * n,
        name="results",
        cost_estimate=pl.CostEstimate(flops=0, bytes_accessed=2 * sum(a.size * a.dtype.itemsize for a in arrays), transcendentals=0),
    )(*arrays)


def from_behind(x, axis, by):
    size = lax.axis_size(axis)
    pairs = [(i, i + by) for i in range(size) if 0 <= i + by < size]
    return lax.ppermute(x, axis, pairs)


def prefix(part, axis, combine, identity, reverse):
    count = lax.axis_size(axis)
    place = lax.axis_index(axis)
    ahead = count - 1 - place if reverse else place
    gathered = jax.tree.map(lambda a: lax.all_gather(a, axis), part)
    state = jax.tree.map(lambda a, e: jnp.zeros_like(a) + jnp.asarray(e, a.dtype), part, identity)

    def one(lap, state):
        source = count - 1 - lap if reverse else lap
        return combine(
            state, jax.tree.map(lambda a: lax.dynamic_index_in_dim(a, source, 0, False), gathered)
        )

    return lax.fori_loop(0, ahead, one, state)


def rms_scale(values, gain_row):
    inverse = lax.rsqrt(jnp.mean(values * values, axis=-1, keepdims=True) + EPSILON)
    return values * inverse * gain_row


def combine_steps(earlier, later):
    return (earlier[0] * later[0], later[0] * earlier[1] + later[1])


def smooth_gelu(inputs):
    return jax.nn.gelu(inputs, approximate=True)


def glu_piece(gate_pre, up_value):
    return smooth_gelu(gate_pre) * up_value


def gate_math(gate_pre, bias_rows, decay_vec, coded_rows, fresh_row):
    tok_rows, rnn_width = coded_rows.shape
    block_size = gate_pre.shape[2] // 2
    gate_x = jax.nn.sigmoid(gate_pre[:, :, :block_size].reshape(tok_rows, rnn_width) + bias_rows[0])
    gate_a = jax.nn.sigmoid(gate_pre[:, :, block_size:].reshape(tok_rows, rnn_width) + bias_rows[1])
    log_a = -8.0 * gate_a * jax.nn.softplus(decay_vec)
    factor = jnp.where(fresh_row, 0.0, jnp.exp(log_a))
    scale_term = jnp.where(fresh_row, 1.0, jnp.sqrt(-jnp.expm1(2.0 * log_a)))
    return (factor, scale_term * gate_x * coded_rows)


def per_device(
    tokens,
    cotangent,
    lengths,
    gain_norm1,
    gain_norm2,
    proj_in,
    out_proj,
    gate_blocks,
    conv_weight,
    conv_bias,
    gate_bias,
    decay_param,
    mlp_in,
    mlp_down,
):
    tok_rows, model_width = tokens.shape
    conv_taps = conv_weight.shape[0]
    reach_back = conv_taps - 1
    first_row = lax.axis_index("dp") * tok_rows
    places = first_row + jnp.arange(-reach_back, tok_rows, dtype=jnp.int32)
    bounds = jnp.cumsum(lengths)
    labels = jnp.sum((places[:, None] >= bounds[None, :]).astype(jnp.int32), axis=1)
    labels = jnp.where(places < 0, -1, labels)
    own_label = labels[reach_back:]
    fresh_row = (own_label != labels[reach_back - 1 : reach_back - 1 + tok_rows])[:, None]
    tap_masks = [
        (labels[reach_back - offset : reach_back - offset + tok_rows] == own_label)[:, None].astype(
            jnp.float32
        )
        for offset in range(conv_taps)
    ]
    gathered = (
        lax.all_gather(proj_in, "dp", axis=0, tiled=True),
        lax.all_gather(out_proj, "dp", axis=0, tiled=True),
        lax.all_gather(gate_blocks, "dp", axis=0, tiled=True),
        lax.all_gather(gain_norm1, "dp", axis=0, tiled=True),
        lax.all_gather(gain_norm2, "dp", axis=0, tiled=True),
        lax.all_gather(conv_weight, "dp", axis=1, tiled=True),
        lax.all_gather(conv_bias, "dp", axis=0, tiled=True),
        lax.all_gather(gate_bias, "dp", axis=1, tiled=True),
        lax.all_gather(decay_param, "dp", axis=0, tiled=True),
    )
    w_proj, w_out, w_gates = (gathered[0], gathered[1], gathered[2])
    gain_one = gathered[3].astype(jnp.float32)
    gain_two = gathered[4].astype(jnp.float32)
    w_conv = gathered[5].astype(jnp.float32)
    b_conv = gathered[6].astype(jnp.float32)
    b_gates = gathered[7].astype(jnp.float32)
    w_decay = gathered[8].astype(jnp.float32)
    rnn_width = w_conv.shape[1]
    w_mlp, w_down = (
        lax.all_gather(mlp_in, "dp", axis=0, tiled=True),
        lax.all_gather(mlp_down, "dp", axis=0, tiled=True),
    )
    residual = tokens.astype(jnp.float32)
    normed_one, norm_one_back = jax.vjp(rms_scale, residual, gain_one)
    u_one = normed_one.astype(jnp.bfloat16)
    projected = jnp.dot(u_one, w_proj, preferred_element_type=jnp.float32)
    branch_x = projected[:, :rnn_width].astype(jnp.bfloat16)
    branch_y = projected[:, rnn_width:]
    rim_rows = from_behind(branch_x[tok_rows - reach_back :], "dp", 1)
    padded = jnp.concatenate([rim_rows, branch_x], axis=0)
    conv_sum = jnp.zeros((tok_rows, rnn_width), jnp.float32) + b_conv
    for offset in range(conv_taps):
        conv_sum = (
            conv_sum
            + w_conv[offset]
            * padded[reach_back - offset : reach_back - offset + tok_rows].astype(jnp.float32)
            * tap_masks[offset]
        )
    coded_rows = conv_sum.astype(jnp.bfloat16)
    block_size = w_gates.shape[1] // 2
    head_count = rnn_width // block_size
    blocks_w = w_gates.reshape(head_count, block_size, 2 * block_size)
    coded_heads = coded_rows.reshape(tok_rows, head_count, block_size)
    gate_pre = jnp.einsum("thi,hij->thj", coded_heads, blocks_w, preferred_element_type=jnp.float32)
    gate_fn = functools.partial(gate_math, fresh_row=fresh_row)
    (factor, drive_term), gate_back = jax.vjp(
        gate_fn, gate_pre, b_gates, w_decay, coded_rows.astype(jnp.float32)
    )
    prefix_a, local_h = lax.associative_scan(combine_steps, (factor, drive_term), axis=0)
    unit_pair = (jnp.ones((rnn_width,), jnp.float32), jnp.zeros((rnn_width,), jnp.float32))
    carry_unused, carry_h = prefix(
        (prefix_a[-1], local_h[-1]), "dp", combine_steps, unit_pair, False
    )
    state_rows = local_h + prefix_a * carry_h[None, :]
    y_branch_act, y_back = jax.vjp(smooth_gelu, branch_y)
    mixed_rows = (state_rows * y_branch_act).astype(jnp.bfloat16)
    middle = residual + jnp.einsum(
        "tr,dr->td", mixed_rows, w_out, preferred_element_type=jnp.float32
    )
    normed_two, norm_two_back = jax.vjp(rms_scale, middle, gain_two)
    u_two = normed_two.astype(jnp.bfloat16)
    gate_val = jnp.einsum(
        "td,fd->tf", u_two, w_mlp[:, :model_width], preferred_element_type=jnp.float32
    )
    up_val = jnp.einsum(
        "td,fd->tf", u_two, w_mlp[:, model_width:], preferred_element_type=jnp.float32
    )
    glu_value, glu_back = jax.vjp(glu_piece, gate_val, up_val)
    hidden = glu_value.astype(jnp.bfloat16)
    output = (middle + jnp.dot(hidden, w_down, preferred_element_type=jnp.float32)).astype(
        jnp.bfloat16
    )
    w_proj, w_out, w_gates = (
        lax.all_gather(proj_in, "dp", axis=0, tiled=True),
        lax.all_gather(out_proj, "dp", axis=0, tiled=True),
        lax.all_gather(gate_blocks, "dp", axis=0, tiled=True),
    )
    w_mlp, w_down = (
        lax.all_gather(mlp_in, "dp", axis=0, tiled=True),
        lax.all_gather(mlp_down, "dp", axis=0, tiled=True),
    )
    blocks_w = w_gates.reshape(head_count, block_size, 2 * block_size)
    d_hidden = jnp.einsum("td,fd->tf", cotangent, w_down, preferred_element_type=jnp.float32)
    d_gate_f, d_up_f = glu_back(d_hidden)
    d_gate = d_gate_f.astype(jnp.bfloat16)
    d_up = d_up_f.astype(jnp.bfloat16)
    feed_sum = None
    d_u_two = jnp.einsum(
        "tf,fd->td", d_gate, w_mlp[:, :model_width], preferred_element_type=jnp.float32
    )
    d_u_two = d_u_two + jnp.einsum(
        "tf,fd->td", d_up, w_mlp[:, model_width:], preferred_element_type=jnp.float32
    )
    d_norm_mid, d_gain_two = norm_two_back(d_u_two)
    d_middle = cotangent.astype(jnp.float32) + d_norm_mid
    d_branch = d_middle.astype(jnp.bfloat16)
    d_mixed = jnp.dot(d_branch, w_out, preferred_element_type=jnp.float32)
    d_state = d_mixed * y_branch_act
    d_branch_y = y_back(d_mixed * state_rows)[0].astype(jnp.bfloat16)
    ahead_factor = jnp.concatenate([factor[1:], jnp.ones((1, rnn_width), jnp.float32)], axis=0)
    back_prod, local_g = lax.associative_scan(
        combine_steps, (ahead_factor, d_state), reverse=True, axis=0
    )
    carry_skip, carry_q = prefix(
        (factor[0] * back_prod[0], factor[0] * local_g[0]), "dp", combine_steps, unit_pair, True
    )
    adjoint = local_g + back_prod * carry_q[None, :]
    before = jnp.concatenate([carry_h[None, :], state_rows[:-1]], axis=0)
    d_pre_f, d_shift, d_decay, d_coded_part = gate_back((adjoint * before, adjoint))
    d_pre = d_pre_f.astype(jnp.bfloat16)
    d_coded = d_coded_part + jnp.einsum(
        "thj,hij->thi", d_pre, blocks_w, preferred_element_type=jnp.float32
    ).reshape(tok_rows, rnn_width)
    gate_grad = jnp.einsum(
        "thi,thj->hij", coded_heads, d_pre, preferred_element_type=jnp.float32
    ).reshape(rnn_width, 2 * block_size)
    spread = jnp.zeros((tok_rows + reach_back, rnn_width), jnp.float32)
    tap_grads = []
    for offset in range(conv_taps):
        spread = spread + jnp.pad(
            w_conv[offset] * tap_masks[offset] * d_coded, ((reach_back - offset, offset), (0, 0))
        )
        tap_grads.append(
            jnp.sum(
                d_coded
                * tap_masks[offset]
                * padded[reach_back - offset : reach_back - offset + tok_rows].astype(jnp.float32),
                axis=0,
            )
        )
    d_conv_w = jnp.stack(tap_grads, axis=0)
    d_conv_b = jnp.sum(d_coded, axis=0)
    back_rim = from_behind(spread[:reach_back], "dp", -1)
    d_branch_x = (
        spread[reach_back:] + jnp.pad(back_rim, ((tok_rows - reach_back, 0), (0, 0)))
    ).astype(jnp.bfloat16)
    d_projected = jnp.concatenate([d_branch_x, d_branch_y], axis=1)
    d_u_one = jnp.einsum("tk,dk->td", d_projected, w_proj, preferred_element_type=jnp.float32)
    d_norm_in, d_gain_one = norm_one_back(d_u_one)
    grad_tokens = (d_middle + d_norm_in).astype(jnp.bfloat16)
    part_gate = jnp.einsum("tf,td->fd", d_gate, u_two, preferred_element_type=jnp.float32)
    part_up = jnp.einsum("tf,td->fd", d_up, u_two, preferred_element_type=jnp.float32)
    part_down = jnp.einsum("tf,td->fd", hidden, cotangent, preferred_element_type=jnp.float32)
    feed_sum = lax.psum_scatter(
        jnp.concatenate([part_gate, part_up, part_down], axis=1),
        "dp",
        scatter_dimension=0,
        tiled=True,
    )
    part_proj = jnp.einsum("td,tk->dk", u_one, d_projected, preferred_element_type=jnp.float32)
    part_out = jnp.einsum("td,tr->dr", d_branch, mixed_rows, preferred_element_type=jnp.float32)
    rec_sum = lax.psum_scatter(
        jnp.concatenate([part_proj, part_out], axis=1), "dp", scatter_dimension=0, tiled=True
    )
    channel_sums = (
        lax.psum_scatter(d_gain_one, "dp", scatter_dimension=0, tiled=True),
        lax.psum_scatter(d_gain_two, "dp", scatter_dimension=0, tiled=True),
        lax.psum_scatter(d_conv_w, "dp", scatter_dimension=1, tiled=True),
        lax.psum_scatter(d_conv_b, "dp", scatter_dimension=0, tiled=True),
        lax.psum_scatter(d_shift, "dp", scatter_dimension=1, tiled=True),
        lax.psum_scatter(d_decay, "dp", scatter_dimension=0, tiled=True),
        lax.psum_scatter(gate_grad, "dp", scatter_dimension=0, tiled=True),
    )
    return (
        output,
        grad_tokens,
        channel_sums[0],
        channel_sums[1],
        rec_sum[:, : 2 * rnn_width],
        rec_sum[:, 2 * rnn_width :],
        channel_sums[6],
        channel_sums[2],
        channel_sums[3],
        channel_sums[4],
        channel_sums[5],
        feed_sum[:, : 2 * model_width],
        feed_sum[:, 2 * model_width :],
    )


def kernels_step(
    tokens, cotangent, lengths, gain_norm1, gain_norm2, proj_in, out_proj, gate_blocks, conv_weight, conv_bias, gate_bias,
    decay_param, mlp_in, mlp_down,
):
    count = lax.axis_size("dp")
    rows = tokens.shape[0]
    longest = rows * count // 12
    reach = -(-(longest - 1) // rows)
    (output, par, gain, gg2, wbx, wby, wgate, wout, by, fac, gx, ga, sc, st, bx, coded, mixed, u1, dmid, db, part01,
     part2) = forward_call(
        count, reach,
        (tokens, cotangent, lengths, conv_weight, conv_bias[None], gate_bias, decay_param[None], gain_norm1[None],
         gain_norm2[None], proj_in, out_proj, gate_blocks, mlp_in, mlp_down),
    )
    grads = backward_call(
        count, reach,
        (tokens, lengths, par, gain, gg2, wbx, wby, wgate, wout, by, fac, gx, ga, sc, st, bx, coded, mixed, u1, dmid, db,
         part01, part2),
    )
    (output, grad_tokens, g_proj, g_out, g_gate, g_in, g_down, g_cw, g_cb, g_gb, g_dec, g_n1, g_n2) = results_call(
        [output, *grads]
    )
    return (
        output, grad_tokens, g_n1[0], g_n2[0], g_proj, g_out, g_gate, g_cw, g_cb[0], g_gb, g_dec[0], g_in, g_down,
    )


def fits(mesh):
    return mesh.shape["dp"] == 32


def solution(mesh):
    placed = (
        P("dp", None),
        P("dp", None),
        P(),
        P("dp"),
        P("dp"),
        P("dp", None),
        P("dp", None),
        P("dp", None),
        P(None, "dp"),
        P("dp"),
        P(None, "dp"),
        P("dp"),
        P("dp", None),
        P("dp", None),
    )
    return jax.shard_map(
        kernels_step if fits(mesh) else per_device,
        mesh=mesh,
        in_specs=placed,
        out_specs=(
            P("dp", None),
            P("dp", None),
            P("dp"),
            P("dp"),
            P("dp", None),
            P("dp", None),
            P("dp", None),
            P(None, "dp"),
            P("dp"),
            P(None, "dp"),
            P("dp"),
            P("dp", None),
            P("dp", None),
        ),
        check_vma=False,
    )
```

```python
import functools

import jax
import jax.numpy as jnp
from jax import lax
from jax.experimental import pallas as pl
from jax.experimental.pallas import tpu as pltpu
from jax.sharding import PartitionSpec as P

EPSILON = 1e-06
MESH = pl.DeviceIdType.MESH
F32, BF16 = jnp.float32, jnp.bfloat16
VM = pl.BlockSpec(memory_space=pltpu.VMEM)
ANY = pl.BlockSpec(memory_space=pl.ANY)
SM = pl.BlockSpec(memory_space=pltpu.SMEM)
MIB = 2**20
SEG = 8
STEP = 97
PAD = 8


def nn(a, b):
    return jnp.dot(a, b, preferred_element_type=F32)


def nt(a, b):
    return lax.dot_general(a, b, (((1,), (1,)), ((), ())), preferred_element_type=F32)


def tn(a, b):
    return lax.dot_general(a, b, (((0,), (0,)), ((), ())), preferred_element_type=F32)


class Place:
    def __init__(self):
        me = lax.axis_index("dp")
        self.me = me
        self.core = core = lax.rem(me, 2)
        x = lax.rem(lax.div(me, 2), 2)
        y = lax.rem(lax.div(me, 4), 2)
        self.z = z = lax.div(me, 8)
        self.yx = yx = 2 * y + x
        px, py = me + 2 - 4 * x, me + 4 - 8 * y
        gx, gy = yx + 1 - 2 * x, yx + 2 - 4 * y
        self.pa, self.pb = px + core * (py - px), py + core * (px - py)
        self.ga, self.gb = gx + core * (gy - gx), gy + core * (gx - gy)
        self.gd = 3 - yx
        self.pc = me + 1 - 2 * core
        self.other = 1 - core
        self.zs = [lax.rem(z + d, 4) for d in (1, 2, 3)]
        self.pz = [zz * 8 + lax.rem(me, 8) for zz in self.zs]


def remote(src, dst, ssem, rsem, device):
    return pltpu.make_async_remote_copy(
        src_ref=src, dst_ref=dst, send_sem=ssem, recv_sem=rsem, device_id=(device,), device_id_type=MESH
    )


def entry_barrier(pl_, count, reach):
    me = pl_.me
    bar = pltpu.get_barrier_semaphore()
    for p in [pl_.pc, pl_.pa, pl_.pb] + pl_.pz:
        pl.semaphore_signal(bar, inc=1, device_id=(p,), device_id_type=MESH)
    for d in range(1, reach + 1):

        @pl.when(me >= d)
        def _():
            pl.semaphore_signal(bar, inc=1, device_id=(me - d,), device_id_type=MESH)

        @pl.when(me + d < count)
        def _():
            pl.semaphore_signal(bar, inc=1, device_id=(me + d,), device_id_type=MESH)

    pl.semaphore_wait(bar, 6 + jnp.minimum(me, reach) + jnp.minimum(count - 1 - me, reach))


class Gather:
    def __init__(self, p, buf, ssem, rsem):
        self.p, self.buf, self.ssem, self.rsem = p, buf, ssem, rsem

    def copy(self, slot):
        p = self.p
        if slot < 3:
            src, dev = self.buf.at[p.core, p.yx, p.z], p.pz[slot]
        else:
            group = (p.yx, p.yx, p.ga, p.yx, p.ga, p.gb, p.gd)[slot - 3]
            src, dev = self.buf.at[p.core, group], (p.pa, p.pb, p.pb, p.pc, p.pc, p.pc, p.pc)[slot - 3]
        return remote(src, src, self.ssem.at[slot], self.rsem.at[slot], dev)

    def start(self, *slots):
        for s in slots:
            self.copy(s).start()

    def recv(self, *slots):
        for s in slots:
            self.copy(s).wait_recv()

    def stage(self, n):
        if n == 0:
            self.start(0, 1, 2)
        elif n == 1:
            self.recv(0, 1, 2)
            self.start(3, 4, 6)
        elif n == 2:
            self.recv(3)
            self.start(5, 7)
        elif n == 3:
            self.recv(4)
            self.start(8)
            self.recv(5)
            self.start(9)
        else:
            self.recv(6, 7, 8, 9)
            for s in range(10):
                self.copy(s).wait_send()


def sequence_offset(lengths, first, rows):
    t = first + lax.broadcasted_iota(jnp.int32, (rows, 128), 0)

    def one(i, c):
        bound, start = c
        bound = bound + lengths[i]
        return bound, jnp.where(t >= bound, bound, start)

    _, start = lax.fori_loop(0, lengths.shape[0], one, (jnp.int32(0), jnp.zeros((rows, 128), jnp.int32)))
    return t - start


def one_minus_square(v, root):
    series = 1.0 / 2.0 + v * (1.0 / 6.0 + v * (1.0 / 24.0 + v * (1.0 / 120.0 + v * (1.0 / 720.0))))
    return jnp.where(v > -0.125, -v - v * v * series, 1.0 - root * root)


def root_of(v):
    return v * lax.rsqrt(jnp.maximum(v, 1e-37))


def softplus(v):
    return jnp.maximum(v, 0.0) + jnp.log1p(jnp.exp(-jnp.abs(v)))


GELU_K = 0.7978845608028654


def gelu_parts(v):
    v2 = v * v
    th = jnp.tanh(GELU_K * v * (1.0 + 0.044715 * v2))
    half = 0.5 * (1.0 + th)
    slope = half + 0.5 * v * (1.0 - th * th) * (GELU_K * (1.0 + 3.0 * 0.044715 * v2))
    return v * half, slope


def gelu(v):
    return v * (0.5 * (1.0 + jnp.tanh(GELU_K * v * (1.0 + 0.044715 * (v * v)))))


def flat(v):
    return v.reshape(v.shape[0] * v.shape[1] * v.shape[2], v.shape[3])


def chips(v):
    return jnp.concatenate([v[yx, z] for z in range(4) for yx in range(4)], axis=0)


def whole_w(w):
    return jnp.concatenate([chips(w[0]), chips(w[1])], axis=1)


def put_chips(part, half, v):
    rows = v.shape[0] // 16
    for z in range(4):
        for yx in range(4):
            part[half, yx, z] = v[(4 * z + yx) * rows : (4 * z + yx + 1) * rows]


def put(page, v, row, group):
    for i in range(v.shape[1] // 128):
        page[group + i, row : row + v.shape[0], :] = v[:, i * 128 : (i + 1) * 128]


def rows_loop(total, block, body):
    def one(i, c):
        body(pl.multiple_of(i * block, block))
        return c

    lax.fori_loop(0, total // block, one, 0)


def blocks_loop(groups, total, block, body):
    n = total // block

    def one(i, c):
        body(lax.div(i, n), pl.multiple_of(lax.rem(i, n) * block, block))
        return c

    lax.fori_loop(0, groups * n, one, 0)


SLOTS = 4


def slots_loop(body):
    def one(i, c):
        for slot in range(SLOTS):
            body(SLOTS * i + slot, slot, False if slot == 0 else i == 8 // SLOTS - 1)
        return c

    lax.fori_loop(0, 8 // SLOTS, one, 0)


def scan_segments(factor, value, product, factor_row, value_row, product_row, reverse):
    def one(i, c):
        j = STEP - 1 - i if reverse else i
        out = []
        for g in range(8):
            h, q = c[g]
            a = factor[g, pl.ds(factor_row + j, SEG, stride=STEP), :]
            b = value[g, pl.ds(value_row + j, SEG, stride=STEP), :]
            if reverse:
                h = b + h
                value[g, pl.ds(value_row + j, SEG, stride=STEP), :] = h
                product[g, pl.ds(product_row + j, SEG, stride=STEP), :] = q
                h, q = a * h, a * q
            else:
                h, q = a * h + b, a * q
                value[g, pl.ds(value_row + j, SEG, stride=STEP), :] = h
                product[g, pl.ds(product_row + j, SEG, stride=STEP), :] = q
            out.append((h, q))
        return tuple(out)

    first = tuple((jnp.zeros((SEG, 128), F32), jnp.ones((SEG, 128), F32)) for _ in range(8))
    return lax.fori_loop(0, STEP, one, first)


def segment_rows(inside, i, block):
    rest = inside[i : i + 1, :]
    first = jnp.broadcast_to(rest, (8, 128))
    if i:
        spot = lax.broadcasted_iota(jnp.int32, (8, 128), 0)
        first = jnp.where(spot < i, inside[i - 1 : i, :], first)
    return jnp.concatenate([first, jnp.broadcast_to(rest, (block - 8, 128))], axis=0)


def chain(ends, enter, reverse):
    order = range(SEG - 1, -1, -1) if reverse else range(SEG)
    inside, leave = [], []
    for g in range(8):
        h, q = ends[g]
        v = enter[g]
        rows = [None] * SEG
        for s in order:
            rows[s] = v
            v = q[s : s + 1, :] * v + h[s : s + 1, :]
        inside.append(jnp.concatenate(rows, axis=0))
        leave.append(v)
    return inside, leave


def products(ends):
    out = []
    for g in range(8):
        q = ends[g][1]
        v = q[0:1, :]
        for s in range(1, SEG):
            v = v * q[s : s + 1, :]
        out.append(v)
    return out


def carry_send(p, count, reach, sign, mine, inbox, ssem, rsem):
    for d in range(1, reach + 1):

        @pl.when((p.me + d < count) if sign > 0 else (p.me >= d))
        def _(d=d):
            remote(mine, inbox.at[d - 1], ssem.at[d - 1], rsem.at[d - 1], p.me + sign * d).start()


def carry_wait(p, count, reach, sign, mine, inbox, ssem, rsem):
    for d in range(1, reach + 1):
        there = remote(mine, inbox.at[d - 1], ssem.at[d - 1], rsem.at[d - 1], p.me + sign * d)

        @pl.when((p.me + d < count) if sign > 0 else (p.me >= d))
        def _(there=there):
            there.wait_send()

        @pl.when((p.me >= d) if sign > 0 else (p.me + d < count))
        def _(there=there):
            there.wait_recv()


def carry_fold(p, count, reach, sign, inbox):
    v = [jnp.zeros((1, 128), F32) for _ in range(8)]
    for d in range(reach, 0, -1):
        for g in range(8):
            v[g] = inbox[d - 1, 0, g : g + 1, :] * v[g] + inbox[d - 1, 1, g : g + 1, :]
    return v


def lanes(page, group, row, rows):
    return jnp.concatenate([page[group, pl.ds(row, rows), :], page[group + 1, pl.ds(row, rows), :]], axis=1)


def wide(page, groups, row, rows):
    return jnp.concatenate([page[g, pl.ds(row, rows), :] for g in range(groups)], axis=1)


def fold8(v):
    return jnp.sum(v.reshape(v.shape[0] // 8, 8, v.shape[1]), axis=0)


SMALL, BX, GATE, BY, OUT, M0, M1, M2, SUM0, SUM1, SUM2, TOT = range(0, 120, 10)

FORWARD_ORDER = (
    (),
    (
        SMALL + 1, SMALL + 2, GATE + 1, BX + 0, OUT + 1, BY + 0, BX + 1, SMALL + 3, SMALL + 4, M0 + 0,
        M1 + 0, BY + 1, OUT + 2,
    ),
    (GATE + 2, BX + 2, OUT + 3, BY + 2, GATE + 3, M0 + 1, BX + 3, BX + 4),
    (),
    (GATE + 4, OUT + 4),
    (M1 + 1, BY + 3),
    (BY + 4, M0 + 2, M2 + 0),
    (),
    (M1 + 2,),
    (M2 + 1, M0 + 3, M0 + 4),
    (),
    (M1 + 3,),
    (M2 + 2, M1 + 4, SUM0 + 0),
    (SUM0 + 1,),
    (M2 + 3,),
    (M2 + 4, SUM1 + 0),
    (SUM1 + 1,),
    (),
    (SUM2 + 0,),
)


def forward_kernel(count, reach, *refs):
    (tokens, cot, lengths, cw, cb, gb, dec, g1, g2, w_proj, w_out, w_gate, w_in, w_down,
     out, o_par, o_gain, o_gg2, o_wbx, o_wby, o_wgate, o_wout, o_by, o_fac, o_gx, o_ga, o_sc, o_st, o_bx, o_coded,
     o_mixed, o_u1, o_dmid, o_db, o_part01, o_part2,
     wsmall, wbx, wby, wgate, wout, wm, bx, by, fac, dr, pq, gx, ga, sc, ubuf, coded, mixed, dup,
     since, rate, xh, ssmall, rsmall, sproj, rproj, sout, rout, sgate, rgate, smlp, rmlp, hin, mine, inbox, m_r0, m_ra,
     gs, gr, ps, pr, hs, hr, cs, cr, rs, rr, osem, free) = refs
    p = Place()
    me = p.me
    rows, width = tokens.shape
    core0 = p.core == 0

    xh[...] = jnp.zeros_like(xh)
    inbox[...] = jnp.zeros_like(inbox)
    fac[:, rows:, :] = jnp.ones((8, PAD, 128), F32)
    dr[:, rows + 8 :, :] = jnp.zeros((8, PAD, 128), F32)
    entry_barrier(p, count, reach)

    halo = remote(tokens.at[rows - 16 : rows], xh, hs.at[0], hr.at[0], me + 1)

    @pl.when(me + 1 < count)
    def _():
        halo.start()

    lane = lax.broadcasted_iota(jnp.int32, (32, 128), 1)
    row = lax.broadcasted_iota(jnp.int32, (32, 128), 0)
    spot = jnp.where(lane == lax.rem(me, 4) * 32 + row, 1.0, 0.0).astype(BF16)
    gcol = lax.broadcasted_iota(jnp.int32, (24, width), 1)
    grow = lax.broadcasted_iota(jnp.int32, (24, width), 0)
    gspot = jnp.where(gcol == me * 24 + grow, 1.0, 0.0).astype(BF16)
    ssmall[...] = jnp.zeros_like(ssmall)
    ssmall[0:4, :] = nn(cw[...], spot)
    ssmall[4:5, :] = nn(cb[...], spot)
    ssmall[5:7, :] = nn(gb[...], spot)
    ssmall[7:8, :] = nn(dec[...], spot)
    r1, r2 = nn(g1[...], gspot), nn(g2[...], gspot)
    for j in range(width // 128):
        ssmall[8 + j : 9 + j, :] = r1[:, j * 128 : (j + 1) * 128]
        ssmall[16 + j : 17 + j, :] = r2[:, j * 128 : (j + 1) * 128]
    trades = [
        remote(ssmall, rsmall, ps.at[0], pr.at[0], p.pc),
        remote(sproj.at[0, p.other], rproj.at[0], ps.at[1], pr.at[1], p.pc),
        remote(sgate.at[p.other], rgate, ps.at[2], pr.at[2], p.pc),
        remote(sproj.at[1, p.other], rproj.at[1], ps.at[3], pr.at[3], p.pc),
        remote(sout.at[p.other], rout, ps.at[4], pr.at[4], p.pc),
        remote(smlp.at[p.other], rmlp, ps.at[5], pr.at[5], p.pc),
    ]
    trades[0].start()
    for h in range(2):
        sgate[h] = w_gate[:, h * 256 : (h + 1) * 256].astype(F32)
    trades[2].start()
    for h in range(2):
        sout[h] = w_out[:, h * 512 : (h + 1) * 512].astype(F32)
    trades[4].start()
    for n in range(2):
        for h in range(2):
            lo = n * 1024 + h * 512
            sproj[n, h] = w_proj[:, lo : lo + 512].astype(F32)
        trades[1 + 2 * n].start()
    smlp[0] = w_in[:, :1152].astype(F32)
    smlp[1] = jnp.concatenate([w_in[:, 1152:], w_down[...]], axis=1).astype(F32)
    trades[5].start()

    moves = {
        name: Gather(p, w, gs.at[i], gr.at[i])
        for i, (name, w) in enumerate((
            (SMALL, wsmall), (BX, wbx), (GATE, wgate), (BY, wby), (OUT, wout), (M0, wm.at[0]), (M1, wm.at[1]),
            (M2, wm.at[2])))
    }
    bufs = (m_r0, m_ra, None, None, None, None)
    red = [
        Reduce(p, wm.at[k], wm, (k, p.core), bufs, ((k % 2,),) + tuple((k,) if k < n else None for n in (2, 0, 0, 0, 0)),
               rs.at[k], rr.at[k])
        for k in range(3)
    ]

    moves.update({SUM0: red[0], SUM1: red[1], SUM2: red[2]})
    points = iter(FORWARD_ORDER)

    def at_point():
        for step in next(points):
            if step == SUM2:
                pl.semaphore_wait(free, 1)
            moves[step // 10 * 10].stage(step % 10)
            if step == SUM0 + 1:
                pl.semaphore_signal(free, inc=1, device_id=(p.pc,), device_id_type=MESH)

    def slab(mine_, theirs):
        first = jnp.where(core0, mine_, theirs)
        second = jnp.where(core0, theirs, mine_)
        return jnp.concatenate([first, second], axis=0).astype(BF16)

    trades[0].wait_recv()
    both = ssmall[...] + rsmall[...]
    wsmall[p.core, p.yx, p.z] = jnp.where(core0, both[0:16], both[16:32]).astype(BF16)
    moves[SMALL].stage(0)
    trades[2].wait_recv()
    wgate[p.core, p.yx, p.z] = slab(sgate[p.core], rgate[...])
    moves[GATE].stage(0)
    trades[4].wait_recv()
    wout[p.core, p.yx, p.z] = slab(sout[p.core], rout[...])
    moves[OUT].stage(0)
    trades[1].wait_recv()
    wbx[p.core, p.yx, p.z] = slab(sproj[0, p.core], rproj[0])
    trades[3].wait_recv()
    wby[p.core, p.yx, p.z] = slab(sproj[1, p.core], rproj[1])
    trades[5].wait_recv()
    for k in range(3):
        wm[k, p.core, p.yx, p.z] = slab(smlp[p.core, 24 * k : 24 * k + 24, :], rmlp[24 * k : 24 * k + 24, :])

    at_point()
    outs = []

    def save(src, dst):
        c = pltpu.make_async_copy(src, dst, osem.at[len(outs)])
        c.start()
        outs.append(c)
        return c

    since[...] = sequence_offset(lengths, me * rows, rows)
    at_point()
    for t in trades:
        t.wait_send()

    for g in range(8):
        z_, yx_ = g // 2, 2 * (g % 2)
        o_par[g] = wsmall[0, yx_, z_].astype(F32)[0:8] + wsmall[0, yx_ + 1, z_].astype(F32)[0:8]
        rate[g] = -8.0 * softplus(o_par[g])
    gsum = [jnp.zeros((8, 128), F32), jnp.zeros((8, 128), F32)]
    for z_ in range(4):
        for yx_ in range(4):
            gsum[0] = gsum[0] + wsmall[0, yx_, z_].astype(F32)[8:16]
            gsum[1] = gsum[1] + wsmall[1, yx_, z_].astype(F32)[0:8]
    o_gain[...] = jnp.zeros_like(o_gain)
    for n in range(2):
        for j in range(width // 128):
            o_gain[n : n + 1, j * 128 : (j + 1) * 128] = gsum[n][j : j + 1]

    @pl.when(me + 1 < count)
    def _():
        halo.wait_send()

    @pl.when(me > 0)
    def _():
        halo.wait_recv()

    def norm_rows(x, n):
        inv = lax.rsqrt(jnp.mean(x * x, axis=1, keepdims=True) + EPSILON)
        return (x * inv * o_gain[n : n + 1, :]).astype(BF16)

    ubuf[0:16, :] = norm_rows(xh[...].astype(F32), 0)

    def norm_one(r0):
        ubuf[pl.ds(r0 + 16, 32), :] = norm_rows(tokens[pl.ds(r0, 32), :].astype(F32), 0)

    rows_loop(rows, 32, norm_one)
    saved_u1 = save(ubuf.at[16 : rows + 16], o_u1)
    at_point()

    def project_x(h, c):
        cols = pl.ds(pl.multiple_of(lax.rem(h, 2) * 256, 256), 256)
        v = nn(ubuf[...], chips(wbx[lax.div(h, 2), :, :, :, cols])).astype(BF16).astype(F32)
        bx[2 * h], bx[2 * h + 1] = v[:, :128], v[:, 128:]
        return c

    def project_y(h, c):
        cols = pl.ds(pl.multiple_of(lax.rem(h, 2) * 256, 256), 256)
        v = nn(ubuf[16:, :], chips(wby[lax.div(h, 2), :, :, :, cols]))
        by[2 * h], by[2 * h + 1] = v[:, :128], v[:, 128:]
        return c

    lax.fori_loop(0, 4, project_x, 0)
    saved_bx = save(bx, o_bx)
    save(wbx, o_wbx)
    at_point()

    def conv(g, r0):
        par = o_par[g]
        v = bx[g, pl.ds(r0 + 8, 72), :]
        off = since[pl.ds(r0, 64), :]
        total = par[4:5] + par[0:1] * v[8:72]
        for k in range(1, 4):
            total = total + par[k : k + 1] * jnp.where(off >= k, v[8 - k : 72 - k], 0.0)
        coded[g, pl.ds(r0, 64), :] = total.astype(BF16)

    blocks_loop(8, rows, 64, conv)
    saved_c = save(coded, o_coded)
    at_point()
    save(wgate, o_wgate)

    def gate_dots(h, c):
        left = lanes(coded, 2 * h, 0, rows)
        v = nn(left, wgate[0, :, h].reshape(256, 256))
        gx[2 * h], gx[2 * h + 1] = v[:, :128], v[:, 128:]
        v = nn(left, wgate[1, :, h].reshape(256, 256))
        ga[2 * h], ga[2 * h + 1] = v[:, :128], v[:, 128:]
        return c

    lax.fori_loop(0, 4, gate_dots, 0)
    at_point()

    def gates(g, r0):
        par = o_par[g]
        at = pl.ds(r0, 64)
        fresh = since[at, :] == 0
        gate_x = jax.nn.sigmoid(gx[g, at, :] + par[5:6])
        gate_a = jax.nn.sigmoid(ga[g, at, :] + par[6:7])
        log_a = gate_a * rate[g, 7:8, :]
        decay = jnp.exp(log_a)
        factor = jnp.where(fresh, 0.0, decay)
        scale = jnp.where(fresh, 1.0, root_of(one_minus_square(2.0 * log_a, decay)))
        gx[g, at, :] = gate_x
        ga[g, at, :] = gate_a
        fac[g, at, :] = factor
        sc[g, at, :] = scale
        dr[g, pl.ds(r0 + 8, 64), :] = scale * gate_x * coded[g, at, :].astype(F32)

    blocks_loop(8, rows, 64, gates)
    saved = [save(gx, o_gx), save(ga, o_ga), save(fac.at[:, 0:rows], o_fac), save(sc, o_sc)]
    at_point()
    ends = scan_segments(fac, dr, pq, 0, 8, 0, False)
    _, leave = chain(ends, [jnp.zeros((1, 128), F32)] * 8, False)
    whole = products(ends)
    for g in range(8):
        mine[0, g : g + 1, :] = whole[g]
        mine[1, g : g + 1, :] = leave[g]
    carry_send(p, count, reach, 1, mine, inbox, cs, cr)
    lax.fori_loop(0, 4, project_y, 0)
    save(by, o_by)
    save(wby, o_wby)
    at_point()
    carry_wait(p, count, reach, 1, mine, inbox, cs, cr)
    enter = carry_fold(p, count, reach, 1, inbox)
    inside, _ = chain(ends, enter, False)
    for g in range(8):
        hin[g] = inside[g]
        dr[g, 0:8, :] = jnp.broadcast_to(enter[g], (8, 128))
    step = rows // SEG

    def states(g, c):
        inside_g = hin[g]
        for s in range(SEG):
            lo = s * step
            st = dr[g, lo + 8 : lo + 8 + step, :] + pq[g, lo : lo + step, :] * segment_rows(inside_g, s, step)
            dr[g, lo + 8 : lo + 8 + step, :] = st
            mixed[g, lo : lo + step, :] = (st * gelu(by[g, lo : lo + step, :])).astype(BF16)
        return c

    lax.fori_loop(0, 8, states, 0)
    saved.append(save(dr.at[:, 0 : rows + 8], o_st))
    saved.append(save(mixed, o_mixed))
    at_point()
    save(wout, o_wout)
    for c in (saved_bx, saved_u1, saved_c):
        c.wait()
    middle = bx
    v = nt(wide(mixed, 4, 0, rows), chips(wout[0])) + nt(
        jnp.concatenate([mixed[g] for g in range(4, 8)], axis=1), chips(wout[1])
    )

    put(middle, v, 0, 0)

    def norm_two(r0):
        at = pl.ds(r0, 32)
        m = wide(middle, 6, r0, 32) + tokens[at, :].astype(F32)
        for g in range(6):
            middle[g, at, :] = m[:, g * 128 : (g + 1) * 128]
        ubuf[at, :] = norm_rows(m, 1)

    rows_loop(rows, 32, norm_two)
    at_point()
    for c in saved:
        c.wait()
    fg, fu, fd, acc_out, acc_du = gx, ga, pq, sc, fac
    hid, dgate = coded, mixed

    for k in range(3):
        w0 = flat(wm[k, 0])
        w1 = flat(wm[k, 1])
        wg, wu, wd = w0[:, :768], jnp.concatenate([w0[:, 768:], w1[:, :384]], axis=1), w1[:, 384:]
        put(fg, nt(ubuf[0:rows, :], wg), 0, 0)
        put(fu, nt(ubuf[0:rows, :], wu), 0, 0)
        put(fd, nt(cot[...], wd), 0, 0)

        def glu(r0):
            at = pl.ds(r0, 32)
            for g in range(6):
                act, slope = gelu_parts(fg[g, at, :])
                up, dh = fu[g, at, :], fd[g, at, :]
                hid[g, at, :] = (act * up).astype(BF16)
                dgate[g, at, :] = (dh * up * slope).astype(BF16)
                dup[g, at, :] = (dh * act).astype(BF16)

        rows_loop(rows, 32, glu)
        at_point()
        v_hid, v_dg, v_dup = (wide(t, 6, 0, rows) for t in (hid, dgate, dup))
        v = nn(v_hid, wd)
        v2 = nn(v_dg, wg) + nn(v_dup, wu)
        for g in range(6):
            cols = slice(g * 128, (g + 1) * 128)
            if k == 0:
                acc_out[g, 0:rows, :] = v[:, cols]
                acc_du[g, 0:rows, :] = v2[:, cols]
            else:
                acc_out[g, 0:rows, :] += v[:, cols]
                acc_du[g, 0:rows, :] += v2[:, cols]
        at_point()
        gg = tn(v_dg, ubuf[0:rows, :]).astype(BF16)
        gu = tn(v_dup, ubuf[0:rows, :]).astype(BF16)
        gd = tn(v_hid, cot[...]).astype(BF16)
        wm[k, 0, :, :, :, 0:768] = gg.reshape(4, 4, 48, 768)
        wm[k, 0, :, :, :, 768:1152] = gu[:, :384].reshape(4, 4, 48, 384)
        wm[k, 1, :, :, :, 0:384] = gu[:, 384:].reshape(4, 4, 48, 384)
        wm[k, 1, :, :, :, 384:1152] = gd.reshape(4, 4, 48, 768)
        at_point()

    o_gg2[...] = jnp.zeros_like(o_gg2)

    def finish(r0):
        at = pl.ds(r0, 32)
        m, c = wide(middle, 6, r0, 32), cot[at, :].astype(F32)
        out[at, :] = (m + wide(acc_out, 6, r0, 32)).astype(BF16)
        du = wide(acc_du, 6, r0, 32)
        inv = lax.rsqrt(jnp.mean(m * m, axis=1, keepdims=True) + EPSILON)
        o_gg2[...] += fold8(du * m * inv)
        gd_ = du * o_gain[1:2, :]
        back = jnp.mean(gd_ * m, axis=1, keepdims=True)
        dm = c + inv * gd_ - m * (inv * inv * inv * back)
        ubuf[at, :] = dm.astype(BF16)
        for g in range(6):
            acc_out[g, at, :] = dm[:, g * 128 : (g + 1) * 128]

    rows_loop(rows, 32, finish)
    save(acc_out.at[0:6], o_dmid)
    save(ubuf.at[0:rows], o_db)
    for k in range(2):
        red[k].take(1)
        save(wm.at[k, p.core, p.yx], o_part01.at[k, 0])
        save(wm.at[k, p.core, p.gb], o_part01.at[k, 1])
    red[2].take(0)
    save(wm.at[2, p.core], o_part2)
    red[0].close(0, 1, 2)
    red[1].close(0, 1, 2)
    red[2].close(0)
    for c in outs:
        if not any(c is s for s in saved + [saved_bx, saved_u1, saved_c]):
            c.wait()


def forward_call(count, reach, args):
    tokens = args[0]
    rows, width = tokens.shape
    S = jax.ShapeDtypeStruct
    page = (8, rows, 128)
    outs = [
        (S((rows, width), BF16), VM),
        (S((8, 8, 128), F32), VM),
        (S((8, width), F32), VM),
        (S((8, width), F32), VM),
        (S((2, 4, 4, 48, 512), BF16), ANY),
        (S((2, 4, 4, 48, 512), BF16), ANY),
        (S((2, 4, 4, 64, 256), BF16), ANY),
        (S((2, 4, 4, 48, 512), BF16), ANY),
        (S(page, F32), ANY),
        (S(page, F32), ANY),
        (S(page, F32), ANY),
        (S(page, F32), ANY),
        (S(page, F32), ANY),
        (S((8, rows + 8, 128), F32), ANY),
        (S((8, rows + 16, 128), F32), ANY),
        (S(page, BF16), ANY),
        (S(page, BF16), ANY),
        (S((rows, width), BF16), ANY),
        (S((6, rows, 128), F32), ANY),
        (S((rows, width), BF16), ANY),
        (S((2, 2, 4, 48, 1152), BF16), ANY),
        (S((4, 4, 48, 1152), BF16), ANY),
    ]
    V = pltpu.VMEM
    dma = pltpu.SemaphoreType.DMA
    scratch = [
        V((2, 4, 4, 16, 128), BF16),
        V((2, 4, 4, 48, 512), BF16),
        V((2, 4, 4, 48, 512), BF16),
        V((2, 4, 4, 64, 256), BF16),
        V((2, 4, 4, 48, 512), BF16),
        V((3, 2, 4, 4, 48, 1152), BF16),
        V((8, rows + 16, 128), F32),
        V(page, F32),
        V((8, rows + PAD, 128), F32),
        V((8, rows + 8 + PAD, 128), F32),
        V((8, rows + PAD, 128), F32),
        V(page, F32),
        V(page, F32),
        V(page, F32),
        V((rows + 16, width), BF16),
        V(page, BF16),
        V(page, BF16),
        V(page, BF16),
        V((rows, 128), jnp.int32),
        V((8, 8, 128), F32),
        V((16, width), BF16),
        V((32, 128), F32),
        V((32, 128), F32),
        V((2, 2, 24, 512), F32),
        V((2, 24, 512), F32),
        V((2, 24, 512), F32),
        V((24, 512), F32),
        V((2, 32, 256), F32),
        V((32, 256), F32),
        V((2, 72, 1152), F32),
        V((72, 1152), F32),
        V((8, 8, 128), F32),
        V((2, 8, 128), F32),
        V((reach, 2, 8, 128), F32),
        V((2, 4, 4, 48, 1152), BF16),
        V((2, 2, 4, 48, 1152), BF16),
        dma((8, 10)),
        dma((8, 10)),
        dma((6,)),
        dma((6,)),
        dma((1,)),
        dma((1,)),
        dma((reach,)),
        dma((reach,)),
        dma((3, 8)),
        dma((3, 8)),
        dma((24,)),
        pltpu.SemaphoreType.REGULAR,
    ]
    return pl.pallas_call(
        functools.partial(forward_kernel, count, reach),
        out_shape=[o[0] for o in outs],
        in_specs=[VM, VM, SM] + [VM] * 11,
        out_specs=[o[1] for o in outs],
        scratch_shapes=scratch,
        name="forward",
        cost_estimate=pl.CostEstimate(flops=25 * 10**9, bytes_accessed=60 * 10**6, transcendentals=10**7),
        compiler_params=pltpu.CompilerParams(
            collective_id=0, has_side_effects=True, vmem_limit_bytes=62 * MIB
        ),
    )(*args)


class Reduce:
    def __init__(self, p, part, whole, own_lead, bufs, leads, ssem, rsem, groups=None):
        self.p, self.part = p, part
        self.whole, self.own_lead, self.bufs, self.leads = whole, own_lead, bufs, leads
        self.ssem, self.rsem = ssem, rsem
        self.gyx, self.gb = groups or (p.yx, p.gb)

    def own(self, *index):
        return self.whole.at[self.own_lead + index]

    def buf(self, which, *index):
        at = self.leads[which] + index
        return self.bufs[which].at[at] if at else self.bufs[which]

    def copy(self, slot):
        p = self.p
        src, dst, dev = (
            (lambda: (self.part.at[p.other], self.buf(0), p.pc)),
            (lambda: (self.own(p.gd), self.buf(1, 1), p.pa)),
            (lambda: (self.own(p.ga), self.buf(1, 0), p.pa)),
            (lambda: (self.own(self.gb), self.buf(2), p.pb)),
            (lambda: (self.own(self.gyx, p.zs[0]), self.buf(3, 0), p.pz[0])),
            (lambda: (self.own(self.gyx, p.zs[1]), self.buf(3, 1), p.pz[1])),
            (lambda: (self.own(self.gyx, p.zs[2]), self.buf(3, 2), p.pz[2])),
            (lambda: (self.buf(4, p.other), self.buf(5), p.pc)),
        )[slot]()
        return remote(src, dst, self.ssem.at[slot], self.rsem.at[slot], dev)

    def add(self, group, which, *index):
        for z in range(4):
            at = self.own_lead + (group, z)
            other = self.bufs[which][self.leads[which] + index + (z,)]
            self.whole[at] = (self.whole[at].astype(F32) + other.astype(F32)).astype(BF16)

    def take(self, n, send=False):
        p = self.p
        if n == 0:
            self.copy(0).wait_recv()
            for group, slot in ((p.gd, 1), (p.ga, 2)):
                self.add(group, 0, group)
                if send:
                    self.copy(slot).start()
            for group in (self.gb, self.gyx):
                self.add(group, 0, group)
        elif n == 1:
            self.copy(1).wait_recv()
            self.add(self.gb, 1, 1)
            if send:
                self.copy(3).start()
            self.copy(2).wait_recv()
            self.add(self.gyx, 1, 0)
        elif n == 2:
            self.copy(3).wait_recv()
            self.add(self.gyx, 2)
            if send:
                self.send(3)
        elif n == 3:
            total = self.whole[self.own_lead + (self.gyx, p.z)].astype(F32)
            for d in range(3):
                self.copy(4 + d).wait_recv()
                total = total + self.bufs[3][self.leads[3] + (d,)].astype(F32)
            half = total.shape[0] // 2
            self.bufs[4][self.leads[4] + (0,)] = total[:half]
            self.bufs[4][self.leads[4] + (1,)] = total[half:]
            if send:
                self.send(4)

    def send(self, n):
        for slot in ((0,), (1, 2), (3,), (4, 5, 6), (7,))[n]:
            self.copy(slot).start()

    def close(self, *slots):
        for s in slots:
            self.copy(s).wait_send()

    def stage(self, n, first=0):
        if n == 0:
            self.send(0)
        elif n < 5:
            self.take(n - 1, True)
        else:
            p = self.p
            self.copy(7).wait_recv()
            mine, theirs = self.bufs[4][self.leads[4] + (p.core,)], self.bufs[5][self.leads[5] + (...,)]
            left = jnp.where(p.core == 0, mine, theirs)
            right = jnp.where(p.core == 0, theirs, mine)
            self.close(*range(first, 8))
            return left, right


class Totals:
    def __init__(self, p, v, bufs, ssem, rsem):
        self.p, self.v, self.bufs, self.ssem, self.rsem = p, v, bufs, ssem, rsem

    def copy(self, slot):
        p = self.p
        dev = ([p.pc, p.pa, p.pb] + p.pz)[slot]
        return remote(self.v.at[min(slot, 3)], self.bufs.at[slot], self.ssem.at[slot], self.rsem.at[slot], dev)

    def stage(self, n):
        if n < 3:
            self.copy(n).start()
        if n == 3:
            for s in (3, 4, 5):
                self.copy(s).start()

    def step(self, n):
        if n < 3:
            self.copy(n).wait_recv()
            self.v[n + 1] = self.v[n] + self.bufs[n]
            return None
        total = self.v[3]
        for s in (3, 4, 5):
            self.copy(s).wait_recv()
            total = total + self.bufs[s]
        for s in range(6):
            self.copy(s).wait_send()
        return total


BACKWARD_ORDER = (
    (M0 + 2, M1 + 2),
    (M2 + 1,),
    (),
    (),
    (OUT + 0, M0 + 3),
    (BY + 0,),
    (OUT + 1, M1 + 3),
    (M2 + 2, BY + 1),
    (GATE + 0, OUT + 2),
    (M2 + 3, GATE + 1),
    (BY + 2,),
    (BX + 0, OUT + 3),
    (BX + 1, GATE + 2, BY + 3),
    (TOT + 0, BX + 2, M0 + 4, M1 + 4),
    (
        TOT + 1, GATE + 3, M0 + 5, M1 + 5, M2 + 4, BX + 3, TOT + 2, OUT + 4, BY + 4, TOT + 3, M2 + 5, OUT + 5,
        BY + 5, GATE + 4, GATE + 5, BX + 4, TOT + 4, BX + 5,
    ),
)


def backward_kernel(count, reach, *refs):
    (tokens, lengths, par, gain, gg2, i_wbx, i_wby, i_wgate, i_wout, i_by, i_fac, i_gx, i_ga, i_sc, i_st, i_bx, i_coded,
     i_mixed, i_u1, i_dmid, i_db, i_part01, i_part2,
     grad_tokens, o_proj, o_out, o_gate, o_in, o_down, o_cw, o_cb, o_gb, o_dec, o_g1, o_g2,
     wbx, wby, wgate, wout, adj, fac, st, pp, gslot, coded, mixed, u1, db, dby, dgx, since,
     own01, own2, gout, gpy, gpx, ggate,
     m_ra, m_rb, m_rz, m_tot, m_rc, p_r0, p_ra, p_rb, p_rz, p_tot, p_rc, t_r0, t_ra, t_rb, t_rz, t_tot, t_rc,
     edge, sums, gsum, vsum, vbuf, hin, mine, inbox,
     rs, rr, vs, vr, cs, cr, es, er, isem, gsem, lsem) = refs
    p = Place()
    me = p.me
    rows, width = tokens.shape

    inbox[...] = jnp.zeros_like(inbox)
    edge[...] = jnp.zeros_like(edge)
    def fetch(g, slot):
        return [
            pltpu.make_async_copy(src.at[g], gslot.at[slot, i, 0:rows], gsem.at[slot, i])
            for i, src in enumerate((i_gx, i_ga, i_sc))
        ]

    def fetch_bx(g, slot):
        return pltpu.make_async_copy(i_bx.at[g], gslot.at[slot, 0], gsem.at[slot, 3])

    parts = [
        pltpu.make_async_copy(i_part01, own01, lsem.at[0]),
        pltpu.make_async_copy(i_part2, own2, lsem.at[1]),
    ]
    parts[0].start()
    (load_db, load_wout, load_by, load_st, load_fac, load_mixed, load_u1, load_coded, load_wgate, load_wby, load_wbx) = loads = [
        pltpu.make_async_copy(src, dst, isem.at[i])
        for i, (src, dst) in enumerate((
            (i_db, db), (i_wout, wout), (i_by, adj.at[:, 0:rows]), (i_st, st), (i_fac, fac.at[:, 0:rows]), (i_mixed, mixed),
            (i_u1, u1), (i_coded, coded), (i_wgate, wgate), (i_wby, wby), (i_wbx, wbx)))
    ]
    for c in loads[:5] + parts[1:] + loads[5:7] + [c for g in range(SLOTS - 1) for c in fetch(g, g)] + loads[7:]:
        c.start()
    entry_barrier(p, count, reach)

    mbufs = (None, m_ra, m_rb, m_rz, m_tot, m_rc)
    red_m = [
        Reduce(p, None, own, lead, mbufs, (None, (), (k,), (k,), (k,), (k,)), rs.at[k], rr.at[k], groups)
        for k, own, lead, groups in ((0, own01, (0,), (0, 1)), (1, own01, (1,), (0, 1)), (2, own2, (), None))
    ]
    pbufs = (p_r0, p_ra, p_rb, p_rz, p_tot, p_rc)
    red_out, red_py, red_px = [
        Reduce(p, g, g, (p.core,), pbufs, ((k,),) * 6, rs.at[3 + k], rr.at[3 + k]) for k, g in enumerate((gout, gpy, gpx))
    ]
    red_gate = Reduce(
        p, ggate, ggate, (p.core,), (t_r0, t_ra, t_rb, t_rz, t_tot, t_rc), ((),) * 6, rs.at[6], rr.at[6]
    )

    sums[...] = jnp.zeros_like(sums)
    gsum[...] = jnp.zeros_like(gsum)

    tot = Totals(p, vsum, vbuf, vs, vr)
    sums_of = {M0: red_m[0], M1: red_m[1], M2: red_m[2], OUT: red_out, BY: red_py, BX: red_px, GATE: red_gate}
    began = {M0: 2, M1: 2, M2: 1}
    points = iter(BACKWARD_ORDER)

    def write(name, left, right):
        if name in began:
            lo = 24 * ((name - M0) // 10)
            o_in[lo : lo + 24, 0:1152] = left
            o_in[lo : lo + 24, 1152:1536] = right[:, :384]
            o_down[lo : lo + 24, :] = right[:, 384:]
        elif name == OUT:
            o_out[:, :512], o_out[:, 512:] = left, right
        elif name == BY:
            o_proj[:, 1024:1536], o_proj[:, 1536:2048] = left, right
        elif name == BX:
            o_proj[:, 0:512], o_proj[:, 512:1024] = left, right
        else:
            o_gate[:, :256], o_gate[:, 256:] = left, right

    def write_totals(total):
        chan = pltpu.roll(total[0:8], lax.rem(1024 - 32 * me, 1024), 1)
        o_cw[...] = chan[0:4, 0:32]
        o_cb[...] = chan[4:5, 0:32]
        o_gb[...] = chan[5:7, 0:32]
        o_dec[...] = chan[7:8, 0:32]
        gains = pltpu.roll(total[8:16], lax.rem(1024 - 24 * me, 1024), 1)
        o_g1[...] = gains[0:1, 0:24]
        o_g2[...] = gains[1:2, 0:24]

    def at_point():
        for step in next(points):
            name, n = step // 10 * 10, step % 10
            if name == TOT:
                total = tot.step(n - 1) if n > 0 else None
                if n < 4:
                    tot.stage(n)
                else:
                    write_totals(total)
            elif n == began.get(name):
                sums_of[name].send(n)
            elif n < 5:
                sums_of[name].stage(n)
            else:
                first = began.get(name, 0)
                write(name, *sums_of[name].stage(5, (0, 1, 3)[first]))

    parts[0].wait()
    at_point()
    load_db.wait()
    load_wout.wait()

    def mix_dots(h, c):
        cols = pl.ds(pl.multiple_of(lax.rem(h, 2) * 256, 256), 256)
        v = nn(db[...], chips(wout[lax.div(h, 2), :, :, :, cols]))
        pp[2 * h, 0:rows, :], pp[2 * h + 1, 0:rows, :] = v[:, :128], v[:, 128:]
        return c

    lax.fori_loop(0, 4, mix_dots, 0)
    parts[1].wait()
    at_point()
    load_by.wait()
    load_st.wait()

    def branch_y(g, r0):
        at = pl.ds(r0, 64)
        dm = pp[g, at, :]
        act, slope = gelu_parts(adj[g, at, :])
        adj[g, at, :] = dm * act
        dby[g, at, :] = (dm * st[g, pl.ds(r0 + 8, 64), :] * slope).astype(BF16)

    blocks_loop(8, rows, 64, branch_y)
    at_point()
    load_fac.wait()
    fac[:, rows:, :] = jnp.ones((8, PAD, 128), F32)
    adj[:, rows:, :] = jnp.zeros((8, PAD, 128), F32)
    ends = scan_segments(fac, adj, pp, 0, 0, 0, True)
    _, leave = chain(ends, [jnp.zeros((1, 128), F32)] * 8, True)
    whole = products(ends)
    for g in range(8):
        mine[0, g : g + 1, :] = whole[g]
        mine[1, g : g + 1, :] = leave[g]
    carry_send(p, count, reach, -1, mine, inbox, cs, cr)
    since[...] = sequence_offset(lengths, me * rows, rows + 8)
    at_point()
    load_mixed.wait()

    def halves(target, left, page):
        for h in range(2):
            v = tn(left, jnp.concatenate([page[4 * h + i] for i in range(4)], axis=1))
            put_chips(target, h, v.astype(BF16))

    halves(gout, db[...], mixed)
    at_point()
    load_u1.wait()
    halves(gpy, u1[...], dby)
    at_point()
    carry_wait(p, count, reach, -1, mine, inbox, cs, cr)
    inside, _ = chain(ends, carry_fold(p, count, reach, -1, inbox), True)
    for g in range(8):
        hin[g] = inside[g]
    step = rows // SEG

    def adjoint(g, c):
        inside_g = hin[g]
        for s in range(SEG):
            lo = s * step
            adj[g, lo : lo + step, :] += pp[g, lo : lo + step, :] * segment_rows(inside_g, s, step)
        return c

    lax.fori_loop(0, 8, adjoint, 0)
    at_point()
    load_coded.wait()
    dga = mixed

    def gate_back(g, slot, last):
        @pl.when(jnp.logical_not(last))
        def _():
            for c_ in fetch(g + SLOTS - 1, (slot + SLOTS - 1) % SLOTS):
                c_.start()

        for c_ in fetch(g, slot):
            c_.wait()
        row = par[g]
        sp8 = -8.0 * softplus(row[7:8])

        def block(i, acc):
            r0 = pl.multiple_of(i * 64, 64)
            at = pl.ds(r0, 64)
            a, f = adj[g, at, :], fac[g, at, :]
            gate_x, gate_a, scale = gslot[slot, 0, at, :], gslot[slot, 1, at, :], gslot[slot, 2, at, :]
            code = coded[g, at, :].astype(F32)
            before = st[g, pl.ds(r0, 72), :][7:71]
            d_log = a * f * (before - gate_x * code * f / scale)
            d_a = d_log * gate_a
            d_ga = d_a * sp8 * (1.0 - gate_a)
            d_part = a * scale * gate_x
            d_gx = d_part * code * (1.0 - gate_x)
            dgx[g, at, :] = d_gx.astype(BF16)
            dga[g, at, :] = d_ga.astype(BF16)
            adj[g, at, :] = d_part
            return acc[0] + fold8(d_gx), acc[1] + fold8(d_ga), acc[2] + fold8(d_a)

        zero = jnp.zeros((8, 128), F32)
        acc = lax.fori_loop(0, rows // 64, block, (zero, zero, zero))
        slope = jax.nn.sigmoid(row[7:8])
        sums[g, 5:6, :] = jnp.sum(acc[0], axis=0, keepdims=True)
        sums[g, 6:7, :] = jnp.sum(acc[1], axis=0, keepdims=True)
        sums[g, 7:8, :] = jnp.sum(acc[2], axis=0, keepdims=True) * (-8.0 * slope)

    slots_loop(gate_back)
    for g in range(SLOTS - 1):
        fetch_bx(g, g).start()
    load_dmid = pltpu.make_async_copy(i_dmid, st.at[0:6, 0:rows], isem.at[11])
    load_dmid.start()
    dbx = dgx
    at_point()
    load_wgate.wait()

    def gate_dots(h, c):
        dx, da, code = lanes(dgx, 2 * h, 0, rows), lanes(dga, 2 * h, 0, rows), lanes(coded, 2 * h, 0, rows)
        v = nt(dx, wgate[0, :, h].reshape(256, 256)) + nt(da, wgate[1, :, h].reshape(256, 256))
        adj[2 * h, 0:rows, :] += v[:, :128]
        adj[2 * h + 1, 0:rows, :] += v[:, 128:]
        ggate[0, :, h] = tn(code, dx).astype(BF16).reshape(4, 64, 256)
        ggate[1, :, h] = tn(code, da).astype(BF16).reshape(4, 64, 256)
        return c

    lax.fori_loop(0, 4, gate_dots, 0)
    edge[0] = adj[:, 0:8, :]
    to_prev = remote(edge.at[0], edge.at[1], es.at[0], er.at[0], me - 1)

    @pl.when(me > 0)
    def _():
        to_prev.start()

    at_point()
    load_wby.wait()
    put(pp, nt(jnp.concatenate([dby[g] for g in range(8)], axis=1), whole_w(wby)), 0, 0)
    at_point()

    @pl.when(me > 0)
    def _():
        to_prev.wait_send()

    @pl.when(me + 1 < count)
    def _():
        to_prev.wait_recv()

    adj[:, rows : rows + 8, :] = edge[1]

    def conv_back(g, slot, last):
        @pl.when(jnp.logical_not(last))
        def _():
            fetch_bx(g + SLOTS - 1, (slot + SLOTS - 1) % SLOTS).start()

        fetch_bx(g, slot).wait()
        row = par[g]

        def block(i, acc):
            r0 = pl.multiple_of(i * 64, 64)
            d = adj[g, pl.ds(r0, 72), :]
            off = since[pl.ds(r0, 72), :]
            b = gslot[slot, 0, pl.ds(r0 + 8, 72), :]
            own, off0 = d[0:64], off[0:64]
            total = row[0:1] * own
            out = [acc[0] + fold8(own * b[8:72])]
            for k in range(1, 4):
                total = total + row[k : k + 1] * jnp.where(off[k : 64 + k] >= k, d[k : 64 + k], 0.0)
                out.append(acc[k] + fold8(own * jnp.where(off0 >= k, b[8 - k : 72 - k], 0.0)))
            out.append(acc[4] + fold8(own))
            dbx[g, pl.ds(r0, 64), :] = total.astype(BF16)
            return tuple(out)

        acc = lax.fori_loop(0, rows // 64, block, tuple(jnp.zeros((8, 128), F32) for _ in range(5)))
        for k in range(5):
            sums[g, k : k + 1, :] = jnp.sum(acc[k], axis=0, keepdims=True)

    slots_loop(conv_back)
    at_point()
    halves(gpx, u1[...], dbx)
    at_point()
    load_wbx.wait()
    du = nt(jnp.concatenate([dbx[g] for g in range(8)], axis=1), whole_w(wbx))
    for g in range(6):
        pp[g, 0:rows, :] += du[:, g * 128 : (g + 1) * 128]
    at_point()
    load_dmid.wait()

    def finish(r0):
        at = pl.ds(r0, 32)
        x = tokens[at, :].astype(F32)
        d = wide(pp, 6, r0, 32)
        inv = lax.rsqrt(jnp.mean(x * x, axis=1, keepdims=True) + EPSILON)
        gsum[...] += fold8(d * x * inv)
        scaled = d * gain[0:1, :]
        back = jnp.mean(scaled * x, axis=1, keepdims=True)
        grad_tokens[at, :] = (wide(st, 6, r0, 32) + inv * scaled - x * (inv * inv * inv * back)).astype(BF16)

    rows_loop(rows, 32, finish)
    vsum[0] = jnp.zeros((16, 1024), F32)
    for g in range(8):
        vsum[0, 0:8, g * 128 : (g + 1) * 128] = sums[g]
    vsum[0, 8:9, 0:width] = jnp.sum(gsum[...], axis=0, keepdims=True)
    vsum[0, 9:10, 0:width] = jnp.sum(gg2[...], axis=0, keepdims=True)
    at_point()
    at_point()


def backward_call(count, reach, args):
    tokens = args[0]
    rows, width = tokens.shape
    S = jax.ShapeDtypeStruct
    V = pltpu.VMEM
    dma = pltpu.SemaphoreType.DMA
    page = (8, rows, 128)
    outs = [
        S((rows, width), BF16), S((24, 2048), F32), S((24, 1024), F32), S((32, 512), F32), S((72, 1536), F32),
        S((72, 768), F32), S((4, 32), F32), S((1, 32), F32), S((2, 32), F32), S((1, 32), F32), S((1, 24), F32),
        S((1, 24), F32),
    ]

    def bufs(n, r, c):
        lead = (n,) if n else ()
        return [V(lead + (4, 4, r, c), BF16), V(lead + (2, 4, r, c), BF16), V(lead + (4, r, c), BF16),
                V(lead + (3, r, c), BF16), V(lead + (2, r // 2, c), F32), V(lead + (r // 2, c), F32)]

    scratch = [
        V((2, 4, 4, 48, 512), BF16), V((2, 4, 4, 48, 512), BF16), V((2, 4, 4, 64, 256), BF16), V((2, 4, 4, 48, 512), BF16),
        V((8, rows + PAD, 128), F32),
        V((8, rows + PAD, 128), F32),
        V((8, rows + 8, 128), F32),
        V((8, rows + PAD, 128), F32),
        V((SLOTS, 3, rows + 16, 128), F32),
        V(page, BF16), V(page, BF16), V((rows, width), BF16), V((rows, width), BF16),
        V(page, BF16), V(page, BF16),
        V((rows + 8, 128), jnp.int32),
        V((2, 2, 4, 48, 1152), BF16), V((4, 4, 48, 1152), BF16),
        V((2, 4, 4, 48, 512), BF16), V((2, 4, 4, 48, 512), BF16), V((2, 4, 4, 48, 512), BF16),
        V((2, 4, 4, 64, 256), BF16),
        V((2, 4, 48, 1152), BF16), *bufs(3, 48, 1152)[2:], *bufs(3, 48, 512), *bufs(0, 64, 256),
        V((2, 8, 8, 128), F32),
        V((8, 8, 128), F32), V((8, width), F32), V((4, 16, 1024), F32), V((6, 16, 1024), F32),
        V((8, 8, 128), F32), V((2, 8, 128), F32), V((reach, 2, 8, 128), F32),
        dma((7, 8)), dma((7, 8)), dma((6,)), dma((6,)), dma((reach,)), dma((reach,)), dma((1,)), dma((1,)),
        dma((12,)), dma((SLOTS, 4)), dma((2,)),
    ]
    return pl.pallas_call(
        functools.partial(backward_kernel, count, reach),
        out_shape=outs,
        in_specs=[VM, SM, VM, VM, VM] + [ANY] * 18,
        out_specs=[VM] * len(outs),
        scratch_shapes=scratch,
        name="backward",
        cost_estimate=pl.CostEstimate(flops=12 * 10**9, bytes_accessed=60 * 10**6, transcendentals=10**7),
        compiler_params=pltpu.CompilerParams(
            collective_id=1, has_side_effects=True, vmem_limit_bytes=63 * MIB
        ),
    )(*args)


def results_kernel(n, *refs):
    for i in range(n):
        refs[n + i][...] = refs[i][...]


def results_call(arrays):
    n = len(arrays)
    return pl.pallas_call(
        functools.partial(results_kernel, n),
        out_shape=[jax.ShapeDtypeStruct(a.shape, a.dtype) for a in arrays],
        in_specs=[VM] * n,
        out_specs=[VM] * n,
        name="results",
        cost_estimate=pl.CostEstimate(flops=0, bytes_accessed=2 * sum(a.size * a.dtype.itemsize for a in arrays), transcendentals=0),
    )(*arrays)


def from_behind(x, axis, by):
    size = lax.axis_size(axis)
    pairs = [(i, i + by) for i in range(size) if 0 <= i + by < size]
    return lax.ppermute(x, axis, pairs)


def prefix(part, axis, combine, identity, reverse):
    count = lax.axis_size(axis)
    place = lax.axis_index(axis)
    ahead = count - 1 - place if reverse else place
    gathered = jax.tree.map(lambda a: lax.all_gather(a, axis), part)
    state = jax.tree.map(lambda a, e: jnp.zeros_like(a) + jnp.asarray(e, a.dtype), part, identity)

    def one(lap, state):
        source = count - 1 - lap if reverse else lap
        return combine(
            state, jax.tree.map(lambda a: lax.dynamic_index_in_dim(a, source, 0, False), gathered)
        )

    return lax.fori_loop(0, ahead, one, state)


def rms_scale(values, gain_row):
    inverse = lax.rsqrt(jnp.mean(values * values, axis=-1, keepdims=True) + EPSILON)
    return values * inverse * gain_row


def combine_steps(earlier, later):
    return (earlier[0] * later[0], later[0] * earlier[1] + later[1])


def smooth_gelu(inputs):
    return jax.nn.gelu(inputs, approximate=True)


def glu_piece(gate_pre, up_value):
    return smooth_gelu(gate_pre) * up_value


def gate_math(gate_pre, bias_rows, decay_vec, coded_rows, fresh_row):
    tok_rows, rnn_width = coded_rows.shape
    block_size = gate_pre.shape[2] // 2
    gate_x = jax.nn.sigmoid(gate_pre[:, :, :block_size].reshape(tok_rows, rnn_width) + bias_rows[0])
    gate_a = jax.nn.sigmoid(gate_pre[:, :, block_size:].reshape(tok_rows, rnn_width) + bias_rows[1])
    log_a = -8.0 * gate_a * jax.nn.softplus(decay_vec)
    factor = jnp.where(fresh_row, 0.0, jnp.exp(log_a))
    scale_term = jnp.where(fresh_row, 1.0, jnp.sqrt(-jnp.expm1(2.0 * log_a)))
    return (factor, scale_term * gate_x * coded_rows)


def per_device(
    tokens,
    cotangent,
    lengths,
    gain_norm1,
    gain_norm2,
    proj_in,
    out_proj,
    gate_blocks,
    conv_weight,
    conv_bias,
    gate_bias,
    decay_param,
    mlp_in,
    mlp_down,
):
    tok_rows, model_width = tokens.shape
    conv_taps = conv_weight.shape[0]
    reach_back = conv_taps - 1
    first_row = lax.axis_index("dp") * tok_rows
    places = first_row + jnp.arange(-reach_back, tok_rows, dtype=jnp.int32)
    bounds = jnp.cumsum(lengths)
    labels = jnp.sum((places[:, None] >= bounds[None, :]).astype(jnp.int32), axis=1)
    labels = jnp.where(places < 0, -1, labels)
    own_label = labels[reach_back:]
    fresh_row = (own_label != labels[reach_back - 1 : reach_back - 1 + tok_rows])[:, None]
    tap_masks = [
        (labels[reach_back - offset : reach_back - offset + tok_rows] == own_label)[:, None].astype(
            jnp.float32
        )
        for offset in range(conv_taps)
    ]
    gathered = (
        lax.all_gather(proj_in, "dp", axis=0, tiled=True),
        lax.all_gather(out_proj, "dp", axis=0, tiled=True),
        lax.all_gather(gate_blocks, "dp", axis=0, tiled=True),
        lax.all_gather(gain_norm1, "dp", axis=0, tiled=True),
        lax.all_gather(gain_norm2, "dp", axis=0, tiled=True),
        lax.all_gather(conv_weight, "dp", axis=1, tiled=True),
        lax.all_gather(conv_bias, "dp", axis=0, tiled=True),
        lax.all_gather(gate_bias, "dp", axis=1, tiled=True),
        lax.all_gather(decay_param, "dp", axis=0, tiled=True),
    )
    w_proj, w_out, w_gates = (gathered[0], gathered[1], gathered[2])
    gain_one = gathered[3].astype(jnp.float32)
    gain_two = gathered[4].astype(jnp.float32)
    w_conv = gathered[5].astype(jnp.float32)
    b_conv = gathered[6].astype(jnp.float32)
    b_gates = gathered[7].astype(jnp.float32)
    w_decay = gathered[8].astype(jnp.float32)
    rnn_width = w_conv.shape[1]
    w_mlp, w_down = (
        lax.all_gather(mlp_in, "dp", axis=0, tiled=True),
        lax.all_gather(mlp_down, "dp", axis=0, tiled=True),
    )
    residual = tokens.astype(jnp.float32)
    normed_one, norm_one_back = jax.vjp(rms_scale, residual, gain_one)
    u_one = normed_one.astype(jnp.bfloat16)
    projected = jnp.dot(u_one, w_proj, preferred_element_type=jnp.float32)
    branch_x = projected[:, :rnn_width].astype(jnp.bfloat16)
    branch_y = projected[:, rnn_width:]
    rim_rows = from_behind(branch_x[tok_rows - reach_back :], "dp", 1)
    padded = jnp.concatenate([rim_rows, branch_x], axis=0)
    conv_sum = jnp.zeros((tok_rows, rnn_width), jnp.float32) + b_conv
    for offset in range(conv_taps):
        conv_sum = (
            conv_sum
            + w_conv[offset]
            * padded[reach_back - offset : reach_back - offset + tok_rows].astype(jnp.float32)
            * tap_masks[offset]
        )
    coded_rows = conv_sum.astype(jnp.bfloat16)
    block_size = w_gates.shape[1] // 2
    head_count = rnn_width // block_size
    blocks_w = w_gates.reshape(head_count, block_size, 2 * block_size)
    coded_heads = coded_rows.reshape(tok_rows, head_count, block_size)
    gate_pre = jnp.einsum("thi,hij->thj", coded_heads, blocks_w, preferred_element_type=jnp.float32)
    gate_fn = functools.partial(gate_math, fresh_row=fresh_row)
    (factor, drive_term), gate_back = jax.vjp(
        gate_fn, gate_pre, b_gates, w_decay, coded_rows.astype(jnp.float32)
    )
    prefix_a, local_h = lax.associative_scan(combine_steps, (factor, drive_term), axis=0)
    unit_pair = (jnp.ones((rnn_width,), jnp.float32), jnp.zeros((rnn_width,), jnp.float32))
    carry_unused, carry_h = prefix(
        (prefix_a[-1], local_h[-1]), "dp", combine_steps, unit_pair, False
    )
    state_rows = local_h + prefix_a * carry_h[None, :]
    y_branch_act, y_back = jax.vjp(smooth_gelu, branch_y)
    mixed_rows = (state_rows * y_branch_act).astype(jnp.bfloat16)
    middle = residual + jnp.einsum(
        "tr,dr->td", mixed_rows, w_out, preferred_element_type=jnp.float32
    )
    normed_two, norm_two_back = jax.vjp(rms_scale, middle, gain_two)
    u_two = normed_two.astype(jnp.bfloat16)
    gate_val = jnp.einsum(
        "td,fd->tf", u_two, w_mlp[:, :model_width], preferred_element_type=jnp.float32
    )
    up_val = jnp.einsum(
        "td,fd->tf", u_two, w_mlp[:, model_width:], preferred_element_type=jnp.float32
    )
    glu_value, glu_back = jax.vjp(glu_piece, gate_val, up_val)
    hidden = glu_value.astype(jnp.bfloat16)
    output = (middle + jnp.dot(hidden, w_down, preferred_element_type=jnp.float32)).astype(
        jnp.bfloat16
    )
    w_proj, w_out, w_gates = (
        lax.all_gather(proj_in, "dp", axis=0, tiled=True),
        lax.all_gather(out_proj, "dp", axis=0, tiled=True),
        lax.all_gather(gate_blocks, "dp", axis=0, tiled=True),
    )
    w_mlp, w_down = (
        lax.all_gather(mlp_in, "dp", axis=0, tiled=True),
        lax.all_gather(mlp_down, "dp", axis=0, tiled=True),
    )
    blocks_w = w_gates.reshape(head_count, block_size, 2 * block_size)
    d_hidden = jnp.einsum("td,fd->tf", cotangent, w_down, preferred_element_type=jnp.float32)
    d_gate_f, d_up_f = glu_back(d_hidden)
    d_gate = d_gate_f.astype(jnp.bfloat16)
    d_up = d_up_f.astype(jnp.bfloat16)
    feed_sum = None
    d_u_two = jnp.einsum(
        "tf,fd->td", d_gate, w_mlp[:, :model_width], preferred_element_type=jnp.float32
    )
    d_u_two = d_u_two + jnp.einsum(
        "tf,fd->td", d_up, w_mlp[:, model_width:], preferred_element_type=jnp.float32
    )
    d_norm_mid, d_gain_two = norm_two_back(d_u_two)
    d_middle = cotangent.astype(jnp.float32) + d_norm_mid
    d_branch = d_middle.astype(jnp.bfloat16)
    d_mixed = jnp.dot(d_branch, w_out, preferred_element_type=jnp.float32)
    d_state = d_mixed * y_branch_act
    d_branch_y = y_back(d_mixed * state_rows)[0].astype(jnp.bfloat16)
    ahead_factor = jnp.concatenate([factor[1:], jnp.ones((1, rnn_width), jnp.float32)], axis=0)
    back_prod, local_g = lax.associative_scan(
        combine_steps, (ahead_factor, d_state), reverse=True, axis=0
    )
    carry_skip, carry_q = prefix(
        (factor[0] * back_prod[0], factor[0] * local_g[0]), "dp", combine_steps, unit_pair, True
    )
    adjoint = local_g + back_prod * carry_q[None, :]
    before = jnp.concatenate([carry_h[None, :], state_rows[:-1]], axis=0)
    d_pre_f, d_shift, d_decay, d_coded_part = gate_back((adjoint * before, adjoint))
    d_pre = d_pre_f.astype(jnp.bfloat16)
    d_coded = d_coded_part + jnp.einsum(
        "thj,hij->thi", d_pre, blocks_w, preferred_element_type=jnp.float32
    ).reshape(tok_rows, rnn_width)
    gate_grad = jnp.einsum(
        "thi,thj->hij", coded_heads, d_pre, preferred_element_type=jnp.float32
    ).reshape(rnn_width, 2 * block_size)
    spread = jnp.zeros((tok_rows + reach_back, rnn_width), jnp.float32)
    tap_grads = []
    for offset in range(conv_taps):
        spread = spread + jnp.pad(
            w_conv[offset] * tap_masks[offset] * d_coded, ((reach_back - offset, offset), (0, 0))
        )
        tap_grads.append(
            jnp.sum(
                d_coded
                * tap_masks[offset]
                * padded[reach_back - offset : reach_back - offset + tok_rows].astype(jnp.float32),
                axis=0,
            )
        )
    d_conv_w = jnp.stack(tap_grads, axis=0)
    d_conv_b = jnp.sum(d_coded, axis=0)
    back_rim = from_behind(spread[:reach_back], "dp", -1)
    d_branch_x = (
        spread[reach_back:] + jnp.pad(back_rim, ((tok_rows - reach_back, 0), (0, 0)))
    ).astype(jnp.bfloat16)
    d_projected = jnp.concatenate([d_branch_x, d_branch_y], axis=1)
    d_u_one = jnp.einsum("tk,dk->td", d_projected, w_proj, preferred_element_type=jnp.float32)
    d_norm_in, d_gain_one = norm_one_back(d_u_one)
    grad_tokens = (d_middle + d_norm_in).astype(jnp.bfloat16)
    part_gate = jnp.einsum("tf,td->fd", d_gate, u_two, preferred_element_type=jnp.float32)
    part_up = jnp.einsum("tf,td->fd", d_up, u_two, preferred_element_type=jnp.float32)
    part_down = jnp.einsum("tf,td->fd", hidden, cotangent, preferred_element_type=jnp.float32)
    feed_sum = lax.psum_scatter(
        jnp.concatenate([part_gate, part_up, part_down], axis=1),
        "dp",
        scatter_dimension=0,
        tiled=True,
    )
    part_proj = jnp.einsum("td,tk->dk", u_one, d_projected, preferred_element_type=jnp.float32)
    part_out = jnp.einsum("td,tr->dr", d_branch, mixed_rows, preferred_element_type=jnp.float32)
    rec_sum = lax.psum_scatter(
        jnp.concatenate([part_proj, part_out], axis=1), "dp", scatter_dimension=0, tiled=True
    )
    channel_sums = (
        lax.psum_scatter(d_gain_one, "dp", scatter_dimension=0, tiled=True),
        lax.psum_scatter(d_gain_two, "dp", scatter_dimension=0, tiled=True),
        lax.psum_scatter(d_conv_w, "dp", scatter_dimension=1, tiled=True),
        lax.psum_scatter(d_conv_b, "dp", scatter_dimension=0, tiled=True),
        lax.psum_scatter(d_shift, "dp", scatter_dimension=1, tiled=True),
        lax.psum_scatter(d_decay, "dp", scatter_dimension=0, tiled=True),
        lax.psum_scatter(gate_grad, "dp", scatter_dimension=0, tiled=True),
    )
    return (
        output,
        grad_tokens,
        channel_sums[0],
        channel_sums[1],
        rec_sum[:, : 2 * rnn_width],
        rec_sum[:, 2 * rnn_width :],
        channel_sums[6],
        channel_sums[2],
        channel_sums[3],
        channel_sums[4],
        channel_sums[5],
        feed_sum[:, : 2 * model_width],
        feed_sum[:, 2 * model_width :],
    )


def kernels_step(
    tokens, cotangent, lengths, gain_norm1, gain_norm2, proj_in, out_proj, gate_blocks, conv_weight, conv_bias, gate_bias,
    decay_param, mlp_in, mlp_down,
):
    count = lax.axis_size("dp")
    rows = tokens.shape[0]
    longest = rows * count // 12
    reach = -(-(longest - 1) // rows)
    (output, par, gain, gg2, wbx, wby, wgate, wout, by, fac, gx, ga, sc, st, bx, coded, mixed, u1, dmid, db, part01,
     part2) = forward_call(
        count, reach,
        (tokens, cotangent, lengths, conv_weight, conv_bias[None], gate_bias, decay_param[None], gain_norm1[None],
         gain_norm2[None], proj_in, out_proj, gate_blocks, mlp_in, mlp_down),
    )
    grads = backward_call(
        count, reach,
        (tokens, lengths, par, gain, gg2, wbx, wby, wgate, wout, by, fac, gx, ga, sc, st, bx, coded, mixed, u1, dmid, db,
         part01, part2),
    )
    (output, grad_tokens, g_proj, g_out, g_gate, g_in, g_down, g_cw, g_cb, g_gb, g_dec, g_n1, g_n2) = results_call(
        [output, *grads]
    )
    return (
        output, grad_tokens, g_n1[0], g_n2[0], g_proj, g_out, g_gate, g_cw, g_cb[0], g_gb, g_dec[0], g_in, g_down,
    )


def fits(mesh):
    return mesh.shape["dp"] == 32


def solution(mesh):
    placed = (
        P("dp", None),
        P("dp", None),
        P(),
        P("dp"),
        P("dp"),
        P("dp", None),
        P("dp", None),
        P("dp", None),
        P(None, "dp"),
        P("dp"),
        P(None, "dp"),
        P("dp"),
        P("dp", None),
        P("dp", None),
    )
    return jax.shard_map(
        kernels_step if fits(mesh) else per_device,
        mesh=mesh,
        in_specs=placed,
        out_specs=(
            P("dp", None),
            P("dp", None),
            P("dp"),
            P("dp"),
            P("dp", None),
            P("dp", None),
            P("dp", None),
            P(None, "dp"),
            P("dp"),
            P(None, "dp"),
            P("dp"),
            P("dp", None),
            P("dp", None),
        ),
        check_vma=False,
    )
```
